32 devices in a mesh: seq: 16 (over z, y, core), chan: 2 (over x).
Axes of the slice: x: 2, y: 2, z: 4, core: 2. Of those that a mesh axis runs over, the one named last changes fastest.
Arguments:
- block_in: bfloat16 [10240, 1152], P(('seq', 'chan')), may hold values from -6 to 6
- routes: int32 [10240, 1], P(('seq', 'chan')), may hold values from 0 to 7; in each aligned block of 320 rows (0 to 319, 320 to 639, ...) at most 51 rows name the same one
- doc_lengths: int32 [4], replicated, may hold values from 64 to 10048, as said below
- norm_gain: float32 [1152], replicated, may hold values from 0.5 to 1.5
- in_weight: bfloat16 [2, 1152, 2304], P(None, None, 'chan'), may hold values from -0.1875 to 0.1875
- conv_weight: float32 [4, 2304], P(None, 'chan'), may hold values from -3 to 3
- conv_bias: float32 [2304], P('chan'), may hold values from -1.5 to 1.5
- xproj_weight: bfloat16 [2304, 104], P('chan'), may hold values from -0.125 to 0.125
- dt_weight: float32 [72, 2304], P(None, 'chan'), may hold values from -0.75 to 0.75
- dt_bias: float32 [2304], P('chan'), may hold values from -5 to 0.5
- a_log: float32 [2304, 16], P('chan'), may hold values from -5.8 to -2.3
- skip_gain: float32 [2304], P('chan'), may hold values from 0.5 to 1.5
- out_weight: bfloat16 [2304, 1152], P('chan'), may hold values from -0.125 to 0.125
- moe_gain: float32 [1152], replicated, may hold values from 0.5 to 1.5
- router_weight: float32 [1152, 8], replicated, may hold values from -0.125 to 0.125
- up_weight: bfloat16 [8, 1152, 3072], P('chan', 'seq'), may hold values from -0.1875 to 0.1875
- down_weight: bfloat16 [8, 1152, 3072], P('chan', 'seq'), may hold values from -0.109375 to 0.109375
- out_grad: bfloat16 [10240, 1152], P(('seq', 'chan')), may hold values from -6 to 6
Outputs:
- block_out: bfloat16 [10240, 1152], P(('seq', 'chan'))
- in_grad: float32 [10240, 1152], P(('seq', 'chan'))
- norm_gain_grad: float32 [1152], replicated
- in_weight_grad: float32 [2, 1152, 2304], P(None, None, 'chan')
- conv_weight_grad: float32 [4, 2304], P(None, 'chan')
- conv_bias_grad: float32 [2304], P('chan')
- xproj_grad: float32 [2304, 104], P('chan')
- dt_weight_grad: float32 [72, 2304], P(None, 'chan')
- dt_bias_grad: float32 [2304], P('chan')
- a_log_grad: float32 [2304, 16], P('chan')
- skip_grad: float32 [2304], P('chan')
- out_weight_grad: float32 [2304, 1152], P('chan')
- moe_gain_grad: float32 [1152], replicated
- router_grad: float32 [1152, 8], replicated
- up_grad: float32 [8, 1152, 3072], P('chan', 'seq')
- down_grad: float32 [8, 1152, 3072], P('chan', 'seq')
The draws below stay inside these ranges and needn't reach their ends.
Inputs may be any that keep to these rules, and one draw needn't show every extreme that they name: `doc_lengths`: document lengths in time order; each is a multiple of 64, they add up to 10240, and one of them is longer than 9600. `routes`: among the 320 tokens of one device (aligned blocks) no expert is chosen more than 51 times, and in every draw some expert is chosen exactly 51 times in some block.
All inputs are finite; a program needn't handle non-finite values.
Results may differ from the reference program's by a relative error of at most 0.017.
Values may be sent and summed in bfloat16 or wider, within the bound.
A program may use at most 768 MiB of HBM per device.

```python
import math
from functools import partial
import jax
import jax.numpy as jnp
import numpy as np
from jax import lax

D = 1152
INNER = 2304
STATE = 16
CONV = 4
DT_RANK = 72
FF = 3072
EXPERTS = 8
TOK_SEQ = 640
NDOC = 4
ALIGN = 64
SINK = 8
XP = 104
TOK_DEV = 320
TOKENS = 10240
CAP = 51


def draw_doc_lengths(key, part):
    pick_key, size_key = jax.random.split(jax.random.fold_in(key, 17))
    longest = jax.random.randint(pick_key, (), 0, NDOC)
    shorts = ALIGN * jax.random.randint(size_key, (NDOC,), 1, TOK_SEQ // (4 * ALIGN) + 1)
    places = jnp.arange(NDOC)
    others = jnp.sum(jnp.where(places == longest, 0, shorts))
    return jnp.where(places == longest, TOKENS - others, shorts).astype(jnp.int32)


def shard_levels(stream_key, shape, cuts, least, high):
    level = 1.0
    for dim, shards_of in cuts:
        steps = jax.random.uniform(jax.random.fold_in(jax.random.fold_in(stream_key, 6), dim), (shards_of,), jnp.float32, least / len(cuts), high / len(cuts))
        level = level * jnp.repeat(jnp.exp(steps), shape[dim] // shards_of).reshape((-1,) + (1,) * (len(shape) - 1 - dim))
    return level


def shared_out(own_key, own, number, rows, count, top, limit, skew):
    sequence = jax.random.permutation(own_key, count)
    crowded, usual = load_shares(count, rows * top, limit, skew, True), load_shares(count, rows * top, limit, skew, False)
    places = jnp.arange(count)

    def named(sizes, offset_by):
        used = int((sizes > 0).sum())
        fixed = max(1, used // 4)
        passed = fixed + (places - fixed + offset_by * (used - fixed)) % max(1, count - fixed)
        return jnp.zeros((count,), jnp.int32).at[sequence[jnp.where(places < fixed, places, passed)]].set(jnp.asarray(sizes, jnp.int32))

    sizes = jnp.where(number % 4 == 0, named(crowded, number // 4), named(usual, number - number // 4 - 1))
    mixed = jax.random.permutation(jax.random.fold_in(own, 3), count)
    donor, sink = mixed[0:count // 2 * 2:2], mixed[1:count // 2 * 2:2]
    slack = jnp.minimum(sizes[donor] - 1, limit - sizes[sink]) // 2
    slack = jnp.where((donor == sequence[0]) | (sink == sequence[0]) | (sizes[sink] == 0), 0, jnp.maximum(slack, 0))
    passed = jax.random.randint(jax.random.fold_in(own, 4), (count // 2,), 0, 1 << 20) % (slack + 1)
    sizes = sizes.at[donor].add(-passed).at[sink].add(passed)
    members = jnp.searchsorted(jnp.cumsum(sizes), jnp.arange(rows * top), side="right").astype(jnp.int32)
    table = members.reshape(top, rows).T
    table = table[jax.random.permutation(jax.random.fold_in(own, 1), rows)]
    offset_by = jax.random.randint(jax.random.fold_in(own, 2), (rows, 1), 0, top)
    return jnp.take_along_axis(table, (jnp.arange(top)[None, :] + offset_by) % top, axis=1)


def load_shares(count, total, limit, skew, full):
    loads = [(1 << 20) // math.isqrt(standing ** skew) + 1 for standing in range(1, count + 1)]
    largest = limit if full else min(limit, max(-(-total // count), total * loads[0] // sum(loads)))
    least = 1 if total - largest >= count - 1 else 0
    given, spare = [largest] + [least] * (count - 1), total - largest - least * (count - 1)
    while spare > 0:
        movable = [i for i in range(1, count) if given[i] < largest] or [i for i in range(1, count) if given[i] < limit]
        mass, left = sum([loads[i] for i in movable]), spare
        for i in movable:
            more = min(limit - given[i], max(1, left * loads[i] // mass), spare)
            given[i] = given[i] + more
            spare = spare - more
    return np.array(given)


def normal_values(key, shape, scale, most, cuts=(), kind=jnp.bfloat16):
    values = scale * jax.random.normal(key, shape, jnp.float32)
    if cuts:
        values = values * shard_levels(key, shape, cuts, -0.22, 0.18)
    return jnp.clip(values, -most, most).astype(kind)


def setup_inputs(seed: int = 0) -> dict:
    keys = jax.random.split(jax.random.key(seed), 19)
    block_in = normal_values(keys[0], (TOKENS, D), 1.0, 6.0, ((0, 32),))
    routes_keys = jax.random.split(jax.random.fold_in(keys[1], 1), TOKENS // TOK_DEV)
    routes_turns = jax.random.permutation(jax.random.fold_in(keys[1], 3), TOKENS // TOK_DEV)
    routes = jax.vmap(lambda own, number: shared_out(jax.random.fold_in(keys[1], 2), own, number, TOK_DEV, EXPERTS, 1, CAP, 1))(routes_keys, routes_turns).reshape((TOKENS, 1))
    doc_lengths = draw_doc_lengths(jax.random.fold_in(keys[18], 71), 0)
    norm_gain = jnp.clip(1.0 + 0.1 * jax.random.normal(keys[3], (D,), jnp.float32), 0.5, 1.5)
    in_weight = normal_values(keys[4], (2, D, INNER), D ** -0.5, 0.1875, ((2, 2),))
    conv_weight = normal_values(keys[5], (CONV, INNER), CONV ** -0.5, 3.0, ((1, 2),), jnp.float32)
    conv_bias = normal_values(keys[6], (INNER,), 0.3, 1.5, ((0, 2),), jnp.float32)
    xproj_weight = normal_values(keys[7], (INNER, XP), INNER ** -0.5, 0.125, ((0, 2),))
    dt_weight = normal_values(keys[8], (DT_RANK, INNER), DT_RANK ** -0.5, 0.75, ((1, 2),), jnp.float32)
    dt_bias = jnp.clip(-5.0 + 5.5 * jax.random.uniform(keys[9], (INNER,), jnp.float32) ** shard_levels(keys[9], (INNER,), ((0, 2),), -0.2, 0.2), -5.0, 0.5)
    a_log = jnp.clip(-5.8 + 3.5000002 * jax.random.uniform(keys[10], (INNER, STATE), jnp.float32) ** shard_levels(keys[10], (INNER, STATE), ((0, 2),), -0.2, 0.2), -5.8, -2.3)
    skip_gain = jnp.clip(0.5 + 1.0 * jax.random.uniform(keys[11], (INNER,), jnp.float32) ** shard_levels(keys[11], (INNER,), ((0, 2),), -0.2, 0.2), 0.5, 1.5)
    out_weight = normal_values(keys[12], (INNER, D), INNER ** -0.5, 0.125, ((0, 2),))
    moe_gain = jnp.clip(1.0 + 0.1 * jax.random.normal(keys[13], (D,), jnp.float32), 0.5, 1.5)
    router_weight = normal_values(keys[14], (D, EXPERTS), (2 * D) ** -0.5, 0.125, (), jnp.float32)
    up_weight = normal_values(keys[15], (EXPERTS, D, FF), D ** -0.5, 0.1875, ((0, 2), (1, 16)))
    down_weight = normal_values(keys[16], (EXPERTS, D, FF), FF ** -0.5, 0.109375, ((0, 2), (1, 16)))
    out_grad = normal_values(keys[17], (TOKENS, D), 1.0, 6.0, ((0, 32),))
    return dict(block_in=block_in, routes=routes, doc_lengths=doc_lengths, norm_gain=norm_gain, in_weight=in_weight, conv_weight=conv_weight, conv_bias=conv_bias, xproj_weight=xproj_weight, dt_weight=dt_weight, dt_bias=dt_bias, a_log=a_log, skip_gain=skip_gain, out_weight=out_weight, moe_gain=moe_gain, router_weight=router_weight, up_weight=up_weight, down_weight=down_weight, out_grad=out_grad)


EPS = 1e-05
HIGH = lax.Precision.HIGHEST

@jax.custom_vjp
def low(v):
    return lax.optimization_barrier(v.astype(jnp.bfloat16)).astype(jnp.float32)

@jax.custom_vjp
def low_back(v):
    return v

def low_keep(v):
    return (low(v), None)

def low_pass(kept, grad):
    return (grad,)

def back_keep(v):
    return (v, None)

def back_low(kept, grad):
    return (low(grad),)
low.defvjp(low_keep, low_pass)
low_back.defvjp(back_keep, back_low)

def rms_norm(values, gain):
    return values * lax.rsqrt(lax.optimization_barrier(jnp.mean(values * values, -1, keepdims=True)) + EPS) * gain

def token_step(rates, state, pieces):
    step_size, mixed, b_in, c_out, keep = pieces
    decay = jnp.exp(-step_size[:, None] * rates) * keep
    state = decay * state + (step_size * mixed)[:, None] * b_in[None, :]
    return (state, lax.optimization_barrier(jnp.sum(state * c_out[None, :], 1)))

def sub_block(rates, state, pieces):
    return lax.scan(partial(token_step, rates), state, pieces)

def mixer_block(params, carry, blocks):
    norm_gain, in_weight, conv_weight, conv_bias, xproj_weight, dt_weight, dt_bias, a_log, skip_gain, out_weight, starts = params
    state, tail = carry
    rows_in, position = blocks
    rows = rows_in.shape[0]
    normed = low(rms_norm(rows_in, norm_gain))
    projected = low_back(jnp.einsum('td,kde->kte', normed, in_weight, precision=HIGH))
    inner = low(projected[0])
    padded = jnp.concatenate([tail, inner], 0)
    doc_first = lax.optimization_barrier(jnp.max(jnp.where(starts[None, :] <= position[:, None], starts[None, :], 0), axis=1)).astype(jnp.int32)
    conv_pre = conv_bias[None, :] + jnp.zeros((rows, inner.shape[1]), jnp.float32)
    for offset in range(CONV):
        delay = CONV - 1 - offset
        usable = (position - delay >= doc_first).astype(jnp.float32)
        conv_pre = conv_pre + conv_weight[offset][None, :] * padded[offset:offset + rows] * usable[:, None]
    mixed = low(jax.nn.silu(conv_pre))
    projection = low_back(jnp.dot(mixed, xproj_weight, precision=HIGH))
    low_rank = projection[:, :DT_RANK]
    b_in = projection[:, DT_RANK:DT_RANK + STATE]
    c_out = projection[:, DT_RANK + STATE:]
    step_size = jax.nn.softplus(jnp.dot(low_rank, dt_weight, precision=HIGH) + dt_bias)
    keep = 1.0 - (doc_first == position).astype(jnp.float32)
    rates = jnp.exp(a_log)
    width = math.gcd(rows, 128)
    count = rows // width
    scan_fn = jax.checkpoint(sub_block)

    def outer(state_now, pieces):
        return scan_fn(rates, state_now, pieces)
    state, outputs = lax.scan(outer, state, (step_size.reshape(count, width, -1), mixed.reshape(count, width, -1), b_in.reshape(count, width, -1), c_out.reshape(count, width, -1), keep.reshape(count, width)))
    scan_out = outputs.reshape(rows, -1) + skip_gain * mixed
    gated = low(scan_out * jax.nn.silu(projected[1]))
    mixer_out = low_back(jnp.dot(gated, out_weight, precision=HIGH))
    return ((state, padded[rows:]), rows_in + mixer_out)

def expert_apply(pieces):
    rows_in, first_weight, second_weight = pieces
    pre = low_back(jnp.dot(rows_in, first_weight, precision=HIGH))
    act = low(jax.nn.gelu(pre, approximate=True))
    return low(low_back(jnp.dot(act, second_weight.T, precision=HIGH)))

def layer(route_col, starts, block_in, norm_gain, in_weight, conv_weight, conv_bias, xproj_weight, dt_weight, dt_bias, a_log, skip_gain, out_weight, moe_gain, router_weight, up_weight, down_weight):
    rows_total = block_in.shape[0]
    params = (norm_gain, in_weight, conv_weight, conv_bias, xproj_weight, dt_weight, dt_bias, a_log, skip_gain, out_weight, starts)
    rows = math.gcd(rows_total, 4096)
    position = jnp.arange(rows_total, dtype=jnp.int32)
    channels = in_weight.shape[2]
    initial = (jnp.zeros((channels, STATE), jnp.float32), jnp.zeros((CONV - 1, channels), jnp.float32))
    block_fn = jax.checkpoint(mixer_block)

    def outer(carry, pieces):
        return block_fn(params, carry, pieces)
    final_carry, hidden = lax.scan(outer, initial, (block_in.reshape(-1, rows, D), position.reshape(-1, rows)))
    hidden_one = hidden.reshape(rows_total, D)
    moe_in = rms_norm(hidden_one, moe_gain)
    probs = jnp.exp(jnp.dot(moe_in, router_weight, precision=HIGH))
    for sweep in range(SINK):
        probs = probs / lax.optimization_barrier(jnp.sum(probs, 0, keepdims=True))
        probs = probs / lax.optimization_barrier(jnp.sum(probs, 1, keepdims=True))
    chosen = (route_col[:, None] == jnp.arange(EXPERTS, dtype=jnp.int32)[None, :]).astype(jnp.int32)
    gate = EXPERTS * lax.optimization_barrier(jnp.sum(probs * chosen.astype(jnp.float32), 1))
    sent = low_back(low(moe_in))
    groups = rows_total // TOK_DEV
    counts = jnp.cumsum(chosen.reshape(groups, TOK_DEV, EXPERTS), 1).astype(jnp.int32).reshape(rows_total, EXPERTS)
    rank = (lax.optimization_barrier(jnp.sum(counts * chosen, 1)) - 1).astype(jnp.int32)
    slot = (position // TOK_DEV * CAP + rank).astype(jnp.int32)
    buffer = jnp.zeros((EXPERTS, groups * CAP, D), jnp.float32).at[route_col, slot].set(sent)
    results = lax.map(jax.checkpoint(expert_apply), (buffer, up_weight, down_weight))
    expert_tok = results[route_col, slot]
    return hidden_one + gate[:, None] * expert_tok

def reference(block_in, routes, doc_lengths, norm_gain, in_weight, conv_weight, conv_bias, xproj_weight, dt_weight, dt_bias, a_log, skip_gain, out_weight, moe_gain, router_weight, up_weight, down_weight, out_grad):
    lengths = doc_lengths.astype(jnp.int32)
    ends = jnp.cumsum(lengths).astype(jnp.int32)
    starts = (ends - lengths).astype(jnp.int32)
    route_col = routes[:, 0].astype(jnp.int32)
    output, pullback = jax.vjp(partial(layer, route_col, starts), block_in.astype(jnp.float32), norm_gain, in_weight.astype(jnp.float32), conv_weight, conv_bias, xproj_weight.astype(jnp.float32), dt_weight, dt_bias, a_log, skip_gain, out_weight.astype(jnp.float32), moe_gain, router_weight, up_weight.astype(jnp.float32), down_weight.astype(jnp.float32))
    grads = pullback(out_grad.astype(jnp.float32))
    return (output.astype(jnp.bfloat16), grads[0], grads[1], grads[2], grads[3], grads[4], grads[5], grads[6], grads[7], grads[8], grads[9], grads[10], grads[11], grads[12], grads[13], grads[14])
```

```python
from functools import partial

import jax
import jax.numpy as jnp
from jax import lax
from jax.experimental import pallas as pl
from jax.experimental.pallas import tpu as pltpu
from jax.sharding import PartitionSpec as P

STATE = 16
CONV = 4
DT_RANK = 72
EXPERTS = 8
SINK = 8
CHUNKS = 8
LANES = 128
VMEM_LIMIT = 56 * 1024 * 1024

EPS = 1e-05
HIGH = lax.Precision.HIGHEST
LOG2E = 1.4426950408889634
LN2 = 0.6931471805599453
BREAK = 1e30


def passed_along(value, axis, steps):
    count = lax.axis_size(axis)
    leading, last = (max(0, -steps), min(count, count - steps))
    return lax.ppermute(value, axis, [(source, source + steps) for source in range(leading, last)])


def swapped(value, axis, bit):
    count = lax.axis_size(axis)
    return lax.ppermute(value, axis, [(source, source ^ bit) for source in range(count)])


def chan_rows(values):
    if lax.axis_size("chan") != 2:
        return lax.all_gather(values, "chan", axis=0, tiled=True)
    first = lax.axis_index("chan") == 0
    other = swapped(values, "chan", 1)
    return jnp.concatenate([jnp.where(first, values, other), jnp.where(first, other, values)], 0)


def chan_sums(term_fn, operand):
    count, place = lax.axis_size("chan"), lax.axis_index("chan")
    rows = operand.shape[0] // count
    if count != 2:
        return lax.psum_scatter(term_fn(operand), "chan", scatter_dimension=0, tiled=True)
    theirs = term_fn(lax.dynamic_slice_in_dim(operand, (1 - place) * rows, rows, 0))
    arrived = swapped(theirs.astype(jnp.bfloat16), "chan", 1)
    return term_fn(lax.dynamic_slice_in_dim(operand, place * rows, rows, 0)) + arrived.astype(
        jnp.float32
    )


def proj_total(values):
    if lax.axis_size("chan") != 2:
        return lax.psum(values, "chan")
    return values + swapped(values, "chan", 1)


def expert_groups():
    own = EXPERTS // lax.axis_size("chan")
    return own, lax.axis_size("seq") // own


def across_experts(values):
    own, share = expert_groups()
    if own == 1:
        return values
    groups = [[k * share + q for k in range(own)] for q in range(share)]
    return lax.all_to_all(
        values, "seq", split_axis=0, concat_axis=0, tiled=True, axis_index_groups=groups
    )


def to_experts(packed):
    own, share = expert_groups()
    count = lax.axis_size("chan")
    slots, width = packed.shape[1:]
    arrived = lax.all_to_all(packed, "chan", split_axis=0, concat_axis=0, tiled=True)
    arrived = jnp.swapaxes(arrived.reshape(count, own, slots, width), 0, 1)
    return across_experts(arrived).reshape(own * count * slots, width)


def to_tokens(rows):
    own, share = expert_groups()
    count = lax.axis_size("chan")
    width = rows.shape[1]
    slots = rows.shape[0] // (own * count)
    back = across_experts(rows.reshape(own, count, slots, width))
    back = jnp.swapaxes(back, 0, 1).reshape(count * own, slots, width)
    return lax.all_to_all(back, "chan", split_axis=0, concat_axis=0, tiled=True)


def whole_expert(weight):
    own, share = expert_groups()
    mine = across_experts(weight)
    groups = [[k * share + q for q in range(share)] for k in range(own)]
    full = lax.all_gather(mine, "seq", axis=1, axis_index_groups=groups)
    return full.reshape(own * share * weight.shape[1], weight.shape[2])


def expert_grad_total(grad):
    own, share = expert_groups()
    place = lax.rem(lax.axis_index("seq"), share)
    hidden = grad.shape[1]
    features = grad.shape[0] // (own * share)
    held = grad.reshape(own, share, features, hidden)
    bit = 1
    while bit < share:
        pairs = held.reshape(own, held.shape[1] // 2, 2, features, hidden)
        side = lax.rem(place // bit, 2)
        sent = lax.dynamic_index_in_dim(pairs, 1 - side, 2, False)
        kept = lax.dynamic_index_in_dim(pairs, side, 2, False)
        came = swapped(sent, "seq", bit)
        held = (kept.astype(jnp.float32) + came.astype(jnp.float32)).astype(grad.dtype)
        bit *= 2
    return across_experts(held.reshape(own, features, hidden)).astype(jnp.float32)


def to_steps(values):
    rows = values.shape[0]
    parts = values.reshape((CHUNKS, rows // CHUNKS) + values.shape[1:])
    return jnp.swapaxes(parts, 0, 1).reshape(values.shape)


def from_steps(values):
    rows = values.shape[0]
    parts = values.reshape((rows // CHUNKS, CHUNKS) + values.shape[1:])
    return jnp.swapaxes(parts, 0, 1).reshape(values.shape)


def norm_apply(values, gain):
    return values * lax.rsqrt(jnp.mean(values * values, -1, keepdims=True) + EPS) * gain


def silu_grad(values):
    sigma = jax.nn.sigmoid(values)
    return sigma * (1.0 + values * (1.0 - sigma))


def gelu_grad(values, upstream):
    return jax.vjp(partial(jax.nn.gelu, approximate=True), values)[1](upstream)[0]


def spread(target, source):
    for n in range(STATE):
        target[n] = jnp.broadcast_to(source[:, n : n + 1], target.shape[1:])


def full(row):
    return jnp.broadcast_to(row, (CHUNKS, LANES))


def shifted(values, by, down):
    sub = lax.broadcasted_iota(jnp.int32, (CHUNKS, LANES), 0)
    if down:
        return jnp.where(sub >= by, pltpu.roll(values, by, 0), 0.0)
    return jnp.where(sub < CHUNKS - by, pltpu.roll(values, CHUNKS - by, 0), 0.0)


def chunk_windows(sums, down):
    windows = []
    for by in (1, 2, 4):
        windows.append(sums)
        sums = sums + shifted(sums, by, down)
    return windows, sums


def chunk_prefix(ends, windows, rate, down):
    for by, window in zip((1, 2, 4), windows):
        ends = ends + jnp.exp2(rate * window) * shifted(ends, by, down)
    return ends


def ends_kernel(halves, reverse, step_ref, drive_ref, break_ref, map_ref, rate_ref, part_ref, sum_ref, tot_ref, wide):
    rows = step_ref.shape[0]
    steps = rows // (halves * CHUNKS)

    @pl.when(pl.program_id(0) == 0)
    def _():
        spread(wide, map_ref)

    rates = [full(rate_ref[n : n + 1, :]) for n in range(STATE)]
    zero = jnp.zeros((CHUNKS, LANES), jnp.float32)

    def half(turn, carry):
        h = halves - 1 - turn if reverse else turn
        before_sum, before = carry[0], carry[1:]

        def body(k, state):
            s = steps - 1 - k if reverse else k
            at = pl.ds(pl.multiple_of((h * steps + s) * CHUNKS, CHUNKS), CHUNKS)
            step = step_ref[at, :]
            decay_step = step + break_ref[at, :]
            drive = drive_ref[at, :]
            if not reverse:
                drive = drive * step
            new = [state[0] + decay_step]
            for n in range(STATE):
                decay = jnp.exp2(decay_step * rates[n])
                if reverse:
                    new.append(decay * (state[n + 1] + drive * wide[n, at, :]))
                else:
                    new.append(decay * state[n + 1] + drive * wide[n, at, :])
            return tuple(new)

        out = lax.fori_loop(0, steps, body, (zero,) * (STATE + 1), unroll=2)
        windows, sums = chunk_windows(out[0], not reverse)
        prior = shifted(sums, 1, not reverse)
        last = slice(0, 1) if reverse else slice(CHUNKS - 1, CHUNKS)
        sum_ref[h] = prior + before_sum
        new = [before_sum + full(sums[last])]
        for n in range(STATE):
            joined = chunk_prefix(out[n + 1], windows, rates[n], not reverse)
            part_ref[h, n] = shifted(joined, 1, not reverse) + jnp.exp2(rates[n] * prior) * before[n]
            new.append(full(joined[last]) + jnp.exp2(rates[n] * full(sums[last])) * before[n])
        return tuple(new)

    total = lax.fori_loop(0, halves, half, (zero,) * (STATE + 1))
    for n in range(STATE):
        tot_ref[n : n + 1, :] = total[n + 1][0:1]
    tot_ref[STATE:, :] = total[0]


def joined_over_devices(place_ref, all_ref, rate_ref, reverse):
    count = all_ref.shape[0]
    place = place_ref[0]
    rates = rate_ref[...]

    def turn(k, state):
        source = count - 1 - k if reverse else k
        part = all_ref[source]
        reached = source > place if reverse else source < place
        new = jnp.exp2(rates * part[STATE : STATE + 1]) * state + part[:STATE]
        return jnp.where(reached, new, state)

    return lax.fori_loop(0, count, turn, jnp.zeros((STATE, LANES), jnp.float32))


def outputs_kernel(
    halves, place_ref, step_ref, mixed_ref, break_ref, b_ref, c_ref, rate_ref, part_ref, sum_ref, all_ref,
    skip_ref, gate_ref, scan_ref, gated_ref, entry_ref, b_wide, c_wide, device,
):
    rows = step_ref.shape[0]
    steps = rows // (halves * CHUNKS)

    @pl.when(pl.program_id(0) == 0)
    def _():
        spread(b_wide, b_ref)
        spread(c_wide, c_ref)

    rates = [full(rate_ref[n : n + 1, :]) for n in range(STATE)]
    device[...] = joined_over_devices(place_ref, all_ref, rate_ref, False)

    def half(h, carry):
        state = []
        for n in range(STATE):
            state.append(
                part_ref[h, n] + jnp.exp2(rates[n] * sum_ref[h]) * full(device[n : n + 1, :])
            )
            entry_ref[h, n] = state[n]

        def body(s, state):
            at = pl.ds(pl.multiple_of((h * steps + s) * CHUNKS, CHUNKS), CHUNKS)
            step = step_ref[at, :]
            decay_step = step + break_ref[at, :]
            drive = mixed_ref[at, :] * step
            total = None
            new = []
            for n in range(STATE):
                value = jnp.exp2(decay_step * rates[n]) * state[n] + drive * b_wide[n, at, :]
                term = value * c_wide[n, at, :]
                total = term if total is None else total + term
                new.append(value)
            scan_ref[at, :] = total
            return tuple(new)

        lax.fori_loop(0, steps, body, tuple(state), unroll=2)
        return carry

    lax.fori_loop(0, halves, half, 0)
    gate = gate_ref[...]
    out = scan_ref[...] + skip_ref[...] * mixed_ref[...]
    scan_ref[...] = out
    gated_ref[...] = (out * (gate * jax.nn.sigmoid(gate))).astype(gated_ref.dtype)


def grads_kernel(
    halves, place_ref, step_ref, mixed_ref, break_ref, grad_ref, b_ref, c_ref, rate_ref, entry_ref, part_ref,
    sum_ref, all_ref, step_out, mixed_out, b_out, c_out, rate_out, b_wide, c_wide, b_sum, c_sum, decays,
    states, device,
):
    rows = step_ref.shape[0]
    steps = rows // (halves * CHUNKS)
    group = pl.program_id(0)
    block = STATE // 2

    @pl.when(group == 0)
    def _():
        spread(b_wide, b_ref)
        spread(c_wide, c_ref)
        b_sum[...] = jnp.zeros_like(b_sum)
        c_sum[...] = jnp.zeros_like(c_sum)

    device[...] = joined_over_devices(place_ref, all_ref, rate_ref, True)
    zero = jnp.zeros((CHUNKS, LANES), jnp.float32)

    for first in (0, block):
        rates = [full(rate_ref[first + n : first + n + 1, :]) for n in range(block)]

        def half(h, rate_sums):
            entry = []
            for n in range(block):
                entry.append(entry_ref[h, first + n])
                states[0, n] = entry[n]

            def ahead(s, state):
                at = pl.ds(pl.multiple_of((h * steps + s) * CHUNKS, CHUNKS), CHUNKS)
                step = step_ref[at, :]
                decay_step = step + break_ref[at, :]
                drive = mixed_ref[at, :] * step
                new = []
                for n in range(block):
                    decay = jnp.exp2(decay_step * rates[n])
                    value = decay * state[n] + drive * b_wide[first + n, at, :]
                    decays[s, n] = decay
                    states[s + 1, n] = value
                    new.append(value)
                return tuple(new)

            lax.fori_loop(0, steps, ahead, tuple(entry), unroll=2)

            exits = [
                part_ref[h, first + n]
                + jnp.exp2(rates[n] * sum_ref[h]) * full(device[first + n : first + n + 1, :])
                for n in range(block)
            ]

            def back(k, carry):
                s = steps - 1 - k
                at = pl.ds(pl.multiple_of((h * steps + s) * CHUNKS, CHUNKS), CHUNKS)
                step = step_ref[at, :]
                mixed = mixed_ref[at, :]
                grad = grad_ref[at, :]
                drive = mixed * step
                by_rate, by_map = zero, zero
                flows, sums = [], []
                for n in range(block):
                    b_now, c_now = b_wide[first + n, at, :], c_wide[first + n, at, :]
                    here = carry[n] + c_now * grad
                    flow = decays[s, n] * here
                    log_grad = flow * states[s, n]
                    by_rate = by_rate + rates[n] * log_grad
                    by_map = by_map + b_now * here
                    b_sum[first + n, at, :] += drive * here
                    c_sum[first + n, at, :] += grad * states[s + 1, n]
                    flows.append(flow)
                    sums.append(carry[block + n] + step * log_grad)
                by_rate = by_rate * LN2 + mixed * by_map
                by_map = step * by_map
                if first == 0:
                    step_out[at, :] = by_rate
                    mixed_out[at, :] = by_map
                else:
                    step_out[at, :] += by_rate
                    mixed_out[at, :] += by_map
                return tuple(flows + sums)

            out = lax.fori_loop(0, steps, back, tuple(exits) + rate_sums)
            return out[block:]

        rate_sums = lax.fori_loop(0, halves, half, (zero,) * block)
        for n in range(block):
            rate_out[first + n : first + n + 1, :] = jnp.sum(rate_sums[n], 0, keepdims=True)

    @pl.when(group == pl.num_programs(0) - 1)
    def _():
        for n in range(STATE):
            b_out[:, n : n + 1] = jnp.sum(b_sum[n], -1, keepdims=True)
            c_out[:, n : n + 1] = jnp.sum(c_sum[n], -1, keepdims=True)


class Scan:
    def __init__(self, rows, channels, halves, seq):
        self.rows, self.channels, self.halves, self.seq = rows, channels, halves, seq
        self.groups = channels // LANES
        row_spec = pl.BlockSpec((rows, LANES), lambda g: (0, g))
        fixed = lambda *shape: pl.BlockSpec(shape, lambda g: (0,) * len(shape))
        self.row_spec = row_spec
        self.break_spec = fixed(rows, LANES)
        self.map_spec = fixed(rows, STATE)
        self.rate_spec = pl.BlockSpec((STATE, LANES), lambda g: (0, g))
        self.part_spec = pl.BlockSpec((halves, STATE, CHUNKS, LANES), lambda g: (0, 0, 0, g))
        self.sum_spec = pl.BlockSpec((halves, CHUNKS, LANES), lambda g: (0, 0, g))
        self.tot_spec = pl.BlockSpec((STATE + CHUNKS, LANES), lambda g: (0, g))
        self.all_spec = pl.BlockSpec((seq, STATE + CHUNKS, LANES), lambda g: (0, 0, g))
        self.skip_spec = pl.BlockSpec((1, LANES), lambda g: (0, g))
        self.place_spec = pl.BlockSpec(memory_space=pltpu.SMEM)
        self.row_f32 = jax.ShapeDtypeStruct((rows, channels), jnp.float32)
        self.part_f32 = jax.ShapeDtypeStruct((halves, STATE, CHUNKS, channels), jnp.float32)
        self.sum_f32 = jax.ShapeDtypeStruct((halves, CHUNKS, channels), jnp.float32)
        self.tot_f32 = jax.ShapeDtypeStruct((STATE + CHUNKS, channels), jnp.float32)
        self.wide = pltpu.VMEM((STATE, rows, LANES), jnp.float32)
        self.device = pltpu.VMEM((STATE, LANES), jnp.float32)

    def params(self):
        return pltpu.CompilerParams(
            dimension_semantics=("arbitrary",), vmem_limit_bytes=VMEM_LIMIT
        )

    def cost(self, per_element):
        count = self.rows * self.channels * STATE
        return pl.CostEstimate(
            flops=per_element * count, bytes_accessed=12 * self.rows * self.channels, transcendentals=count
        )

    def ends(self, reverse, step, drive, breaks, maps, rates):
        return pl.pallas_call(
            partial(ends_kernel, self.halves, reverse),
            grid=(self.groups,),
            in_specs=[self.row_spec, self.row_spec, self.break_spec, self.map_spec, self.rate_spec],
            out_specs=[self.part_spec, self.sum_spec, self.tot_spec],
            out_shape=[self.part_f32, self.sum_f32, self.tot_f32],
            scratch_shapes=[self.wide],
            compiler_params=self.params(),
            cost_estimate=self.cost(5),
            name="scan_ends_back" if reverse else "scan_ends",
        )(step, drive, breaks, maps, rates)

    def outputs(self, place, step, mixed, breaks, b_in, c_out, rates, part, sums, every, skip, gate):
        return pl.pallas_call(
            partial(outputs_kernel, self.halves),
            grid=(self.groups,),
            in_specs=[
                self.place_spec, self.row_spec, self.row_spec, self.break_spec, self.map_spec, self.map_spec,
                self.rate_spec, self.part_spec, self.sum_spec, self.all_spec, self.skip_spec, self.row_spec,
            ],
            out_specs=[self.row_spec, self.row_spec, self.part_spec],
            out_shape=[
                self.row_f32,
                jax.ShapeDtypeStruct((self.rows, self.channels), jnp.bfloat16),
                self.part_f32,
            ],
            scratch_shapes=[self.wide, self.wide, self.device],
            compiler_params=self.params(),
            cost_estimate=self.cost(7),
            name="scan_outputs",
        )(place, step, mixed, breaks, b_in, c_out, rates, part, sums, every, skip, gate)

    def grads(self, place, step, mixed, breaks, grad, b_in, c_out, rates, entry, part, sums, every):
        steps = self.rows // (self.halves * CHUNKS)
        block = STATE // 2
        return pl.pallas_call(
            partial(grads_kernel, self.halves),
            grid=(self.groups,),
            in_specs=[
                self.place_spec, self.row_spec, self.row_spec, self.break_spec, self.row_spec, self.map_spec,
                self.map_spec, self.rate_spec, self.part_spec, self.part_spec, self.sum_spec, self.all_spec,
            ],
            out_specs=[self.row_spec, self.row_spec, self.map_spec, self.map_spec, self.rate_spec],
            out_shape=[
                self.row_f32,
                self.row_f32,
                jax.ShapeDtypeStruct((self.rows, STATE), jnp.float32),
                jax.ShapeDtypeStruct((self.rows, STATE), jnp.float32),
                jax.ShapeDtypeStruct((STATE, self.channels), jnp.float32),
            ],
            scratch_shapes=[
                self.wide, self.wide, self.wide, self.wide,
                pltpu.VMEM((steps, block, CHUNKS, LANES), jnp.float32),
                pltpu.VMEM((steps + 1, block, CHUNKS, LANES), jnp.float32),
                self.device,
            ],
            compiler_params=self.params(),
            cost_estimate=self.cost(20),
            name="scan_grads",
        )(place, step, mixed, breaks, grad, b_in, c_out, rates, entry, part, sums, every)


def over_tokens(values):
    return jnp.sum(jnp.sum(values, 0), -1, keepdims=True)


def sinkhorn_kernel(place_ref, logit_ref, route_ref, gate_ref, scaled_ref, row_ref, column_ref):
    probs = jnp.exp(logit_ref[...])
    for sweep in range(SINK):
        column = over_tokens(probs)
        scaled = probs / column[None]
        row = jnp.sum(scaled, 1, keepdims=True)
        scaled_ref[sweep] = scaled
        row_ref[sweep] = row
        column_ref[sweep] = jnp.broadcast_to(column, column_ref.shape[1:])
        probs = scaled / row
    place = place_ref[0]
    own = scaled_ref[SINK - 1, place] / row_ref[SINK - 1, place]
    ids = lax.broadcasted_iota(jnp.int32, own.shape, 0)
    gate_ref[...] = EXPERTS * jnp.sum(jnp.where(ids == route_ref[...], own, 0.0), 0, keepdims=True)


def sinkhorn_back_kernel(place_ref, logit_ref, scaled_ref, row_ref, column_ref, route_ref, grad_ref, out_ref, held):
    shape = logit_ref.shape
    ids = lax.broadcasted_iota(jnp.int32, shape, 1)
    grad = jnp.where(ids == route_ref[...], EXPERTS * grad_ref[...], 0.0)
    for sweep in reversed(range(SINK)):
        scaled, row = scaled_ref[sweep], row_ref[sweep]
        inner = jnp.sum(grad * (scaled / row), 1, keepdims=True)
        grad = (grad - inner) / row
        along = over_tokens(grad * scaled)
        grad = (grad - along[None]) / column_ref[sweep][:, 0:1][None]
    held[...] = grad
    place = place_ref[0]
    out_ref[...] = held[place] * jnp.exp(logit_ref[place])


def in_vmem(count):
    return [pl.BlockSpec(memory_space=pltpu.SMEM)] + [pl.BlockSpec(memory_space=pltpu.VMEM)] * count


def sinkhorn(place, logits, routes):
    devices, experts, tokens = logits.shape
    f32 = lambda *shape: jax.ShapeDtypeStruct(shape, jnp.float32)
    return pl.pallas_call(
        sinkhorn_kernel,
        in_specs=in_vmem(2),
        out_specs=in_vmem(4)[1:],
        out_shape=[
            f32(1, tokens),
            f32(SINK, devices, experts, tokens),
            f32(SINK, devices, 1, tokens),
            f32(SINK, experts, LANES),
        ],
        compiler_params=pltpu.CompilerParams(vmem_limit_bytes=VMEM_LIMIT),
        name="sinkhorn",
    )(place, logits, routes)


def sinkhorn_back(place, logits, scaled, rows, columns, routes, grad):
    devices, experts, tokens = logits.shape
    return pl.pallas_call(
        sinkhorn_back_kernel,
        in_specs=in_vmem(6),
        out_specs=in_vmem(1)[1],
        out_shape=jax.ShapeDtypeStruct((experts, tokens), jnp.float32),
        scratch_shapes=[pltpu.VMEM(logits.shape, jnp.float32)],
        compiler_params=pltpu.CompilerParams(vmem_limit_bytes=VMEM_LIMIT),
        name="sinkhorn_back",
    )(place, logits, scaled, rows, columns, routes, grad)


def on_device(
    block_in,
    routes,
    doc_lengths,
    norm_gain,
    in_weight,
    conv_weight,
    conv_bias,
    xproj_weight,
    dt_weight,
    dt_bias,
    a_log,
    skip_gain,
    out_weight,
    moe_gain,
    router_weight,
    up_weight,
    down_weight,
    out_grad,
):
    tok_dev, model_width = block_in.shape
    chan_count, seq_count = lax.axis_size("chan"), lax.axis_size("seq")
    chan_place, seq_place = lax.axis_index("chan"), lax.axis_index("seq")
    seq_ref = seq_place.astype(jnp.int32).reshape(1)
    dev_ref = (seq_place * chan_count + chan_place).astype(jnp.int32).reshape(1)
    steps = tok_dev // CHUNKS
    tok_seq = tok_dev * chan_count
    channels = in_weight.shape[2]
    padded_channels = -(-channels // LANES) * LANES
    f32, bf16 = jnp.float32, jnp.bfloat16

    route_col = routes[:, 0]
    expert_ids = lax.broadcasted_iota(jnp.int32, (1, EXPERTS), 1)
    chosen = (route_col[:, None] == expert_ids).astype(bf16)
    row_ids = lax.broadcasted_iota(jnp.int32, (tok_dev, tok_dev), 0)
    col_ids = lax.broadcasted_iota(jnp.int32, (tok_dev, tok_dev), 1)
    counts = jnp.dot((col_ids <= row_ids).astype(bf16), chosen, preferred_element_type=f32)
    rank = (jnp.sum(counts * chosen.astype(f32), 1) - 1.0).astype(jnp.int32)
    capacity = tok_dev * 5 // (4 * EXPERTS) + 1
    capacity = -(-capacity // 8) * 8
    slot = to_steps(route_col * capacity + rank)
    route_steps = to_steps(route_col)
    slot_ids = lax.broadcasted_iota(jnp.int32, (1, EXPERTS * capacity), 1)
    placer = (slot[:, None] == slot_ids).astype(bf16)

    def pack(values):
        rows = jnp.einsum("ts,td->sd", placer, values, preferred_element_type=f32).astype(bf16)
        return rows.reshape(EXPERTS, capacity, model_width)

    def unpack(values):
        return jnp.einsum(
            "ts,sd->td",
            placer,
            values.reshape(EXPERTS * capacity, model_width),
            preferred_element_type=f32,
        )

    block_steps = to_steps(block_in)
    grad_steps = to_steps(out_grad)
    residual = block_steps.astype(f32)
    normed, norm_back = jax.vjp(norm_apply, residual, norm_gain)
    gathered = chan_rows(normed.astype(bf16))
    full_up = whole_expert(up_weight)
    full_down = whole_expert(down_weight)
    grad_arrived = to_experts(pack(grad_steps))
    every_route = lax.all_gather(route_steps.reshape(1, tok_dev), ("seq", "chan"))

    inner_b = jnp.dot(gathered, in_weight[0], preferred_element_type=f32).astype(bf16)
    gate_z = jnp.dot(gathered, in_weight[1], preferred_element_type=f32)

    shape4 = (chan_count, steps, CHUNKS)
    ids = [lax.broadcasted_iota(jnp.int32, shape4, axis) for axis in range(3)]
    position = seq_place * tok_seq + ids[0] * tok_dev + ids[2] * steps + ids[1]
    starts = jnp.cumsum(doc_lengths) - doc_lengths
    doc_first = jnp.max(
        jnp.where(starts <= position[..., None], starts, 0), axis=-1
    )
    reach = CONV - 1
    inner = inner_b.astype(f32).reshape(shape4 + (channels,))
    tails = jnp.swapaxes(inner[:, steps - reach :], 0, 1).reshape(reach, chan_count * CHUNKS, channels)
    previous = passed_along(tails[:, -1], "seq", 1)
    heads = jnp.concatenate([previous[:, None], tails[:, :-1]], 1)
    heads = jnp.swapaxes(heads.reshape(reach, chan_count, CHUNKS, channels), 0, 1)
    padded = jnp.concatenate([heads, inner], 1)
    masks = [
        (position - (reach - offset) >= doc_first).astype(f32)[..., None] for offset in range(CONV)
    ]
    conv_pre = conv_bias
    for offset in range(CONV):
        conv_pre = conv_pre + conv_weight[offset] * padded[:, offset : offset + steps] * masks[offset]
    conv_pre = conv_pre.reshape(tok_seq, channels)
    mixed_b = jax.nn.silu(conv_pre).astype(bf16)
    mixed = mixed_b.astype(f32)
    proj_all = proj_total(jnp.dot(mixed_b, xproj_weight, preferred_element_type=f32))
    low_rank = proj_all[:, :DT_RANK]
    b_in = proj_all[:, DT_RANK : DT_RANK + STATE]
    c_out = proj_all[:, DT_RANK + STATE :]
    step_pre = jnp.dot(low_rank, dt_weight, precision=HIGH) + dt_bias
    step_size = jax.nn.softplus(step_pre)

    def widened(values, axis=-1):
        more = padded_channels - channels
        if not more:
            return values
        pads = [(0, 0)] * values.ndim
        pads[axis] = (0, more)
        return jnp.pad(values, pads)

    scan = Scan(tok_seq, padded_channels, chan_count, seq_count)
    decay_rates = jnp.exp(a_log)
    rates = widened((-LOG2E * decay_rates).T)
    breaks = jnp.any(position[..., None] == starts, axis=-1).astype(f32) * BREAK
    breaks = jnp.broadcast_to(breaks.reshape(tok_seq, 1), (tok_seq, LANES))
    step_w, mixed_w = widened(step_size), widened(mixed)
    part, sums, total = scan.ends(False, step_w, mixed_w, breaks, b_in, rates)
    every = lax.all_gather(total, "seq")
    scan_out, gated_b, entry = scan.outputs(
        seq_ref, step_w, mixed_w, breaks, b_in, c_out, rates, part, sums, every,
        widened(skip_gain[None]), widened(gate_z),
    )
    scan_out, gated_b = scan_out[:, :channels], gated_b[:, :channels]

    mixer_rows = chan_sums(
        lambda rows: jnp.dot(rows, out_weight, preferred_element_type=f32), gated_b
    )
    hidden_one = residual + mixer_rows
    moe_in, moe_back = jax.vjp(norm_apply, hidden_one, moe_gain)
    logits = jnp.einsum("td,de->et", moe_in, router_weight, precision=HIGH)
    every_logit = lax.all_gather(logits, ("seq", "chan"))
    gate_row, scaled, row_totals, columns = sinkhorn(
        dev_ref, every_logit, route_steps.reshape(1, tok_dev)
    )
    gate = gate_row.reshape(tok_dev)

    arrived = to_experts(pack(moe_in.astype(bf16)))
    pre = jnp.dot(arrived, full_up, preferred_element_type=f32)
    act_b = jax.nn.gelu(pre, approximate=True).astype(bf16)
    expert_out = jnp.einsum("sf,df->sd", act_b, full_down, preferred_element_type=f32).astype(bf16)
    grad_act = jnp.dot(grad_arrived, full_down, preferred_element_type=f32)
    plain_grad_pre = gelu_grad(pre, grad_act)
    grad_rows_in = jnp.einsum(
        "sf,df->sd", plain_grad_pre.astype(bf16), full_up, preferred_element_type=f32
    ).astype(bf16)
    expert_tok = unpack(to_tokens(expert_out))
    plain_grad_part = unpack(to_tokens(grad_rows_in))

    gate_slots = jnp.einsum("ts,t->s", placer.astype(f32), gate, precision=HIGH)
    gate_slots = jnp.broadcast_to(gate_slots.reshape(EXPERTS, capacity, 1), (EXPERTS, capacity, LANES))
    gate_arrived = to_experts(gate_slots)[:, 0:1]
    grad_gated_rows = (grad_arrived.astype(f32) * gate_arrived).astype(bf16)
    grad_pre_b = (plain_grad_pre * gate_arrived).astype(bf16)
    down_part = jnp.einsum("sd,sf->df", grad_gated_rows, act_b, preferred_element_type=f32)
    up_part = jnp.einsum("sd,sf->df", arrived, grad_pre_b, preferred_element_type=f32)
    down_grad = expert_grad_total(down_part.astype(bf16))
    up_grad = expert_grad_total(up_part.astype(bf16))

    block_out = from_steps((hidden_one + gate[:, None] * expert_tok).astype(bf16))
    grad_two = grad_steps.astype(f32)
    grad_gate = jnp.sum(expert_tok * grad_two, 1)
    every_grad = lax.all_gather(grad_gate.reshape(1, tok_dev), ("seq", "chan"))
    grad_logits = sinkhorn_back(
        dev_ref, every_logit, scaled, row_totals, columns, every_route, every_grad
    )
    router_grad = jnp.einsum("td,et->de", moe_in, grad_logits, precision=HIGH)
    grad_moe_in = gate[:, None] * plain_grad_part + jnp.einsum(
        "et,de->td", grad_logits, router_weight, precision=HIGH
    )
    grad_hidden, moe_gain_grad = moe_back(grad_moe_in)
    grad_hidden = grad_hidden + grad_two

    grad_mix = chan_rows(grad_hidden.astype(bf16))
    grad_gated = jnp.einsum("td,ed->te", grad_mix, out_weight, preferred_element_type=f32)
    out_weight_grad = jnp.einsum("te,td->ed", gated_b, grad_mix, preferred_element_type=f32)
    grad_scan = grad_gated * jax.nn.silu(gate_z)
    grad_gate_z = (grad_gated * scan_out * silu_grad(gate_z)).astype(bf16)
    skip_grad = jnp.sum(grad_scan * mixed, 0)
    gate_weight_grad = jnp.einsum("td,te->de", gathered, grad_gate_z, preferred_element_type=f32)
    early = lax.psum(
        (out_weight_grad.astype(bf16), gate_weight_grad.astype(bf16), skip_grad.astype(bf16)), "seq"
    )
    grad_scan_w = widened(grad_scan)
    back_part, back_sums, back_total = scan.ends(True, step_w, grad_scan_w, breaks, c_out, rates)
    back_every = lax.all_gather(back_total, "seq")
    step_grad, mixed_grad, b_grad, c_grad, rate_grad = scan.grads(
        seq_ref, step_w, mixed_w, breaks, grad_scan_w, b_in, c_out, rates, entry, back_part, back_sums,
        back_every,
    )
    step_grad, mixed_grad = step_grad[:, :channels], mixed_grad[:, :channels]
    mixed_grad = mixed_grad + skip_gain * grad_scan
    a_log_grad = -decay_rates * rate_grad[:, :channels].T
    step_pre_grad = step_grad * jax.nn.sigmoid(step_pre)
    dt_bias_grad = jnp.sum(step_pre_grad, 0)
    dt_weight_grad = jnp.einsum("tr,te->re", low_rank, step_pre_grad, precision=HIGH)
    rank_grad = jnp.einsum("te,re->tr", step_pre_grad, dt_weight, precision=HIGH)
    proj_grad_b = proj_total(jnp.concatenate([rank_grad, b_grad, c_grad], 1)).astype(bf16)
    mixed_grad = mixed_grad + jnp.einsum(
        "tp,ep->te", proj_grad_b, xproj_weight, preferred_element_type=f32
    )
    xproj_grad = jnp.einsum("te,tp->ep", mixed_b, proj_grad_b, preferred_element_type=f32)
    conv_grad = (mixed_grad * silu_grad(conv_pre)).reshape(shape4 + (channels,))
    conv_bias_grad = jnp.sum(conv_grad, (0, 1, 2))
    conv_weight_grad = jnp.stack(
        [
            jnp.sum(conv_grad * masks[offset] * padded[:, offset : offset + steps], (0, 1, 2))
            for offset in range(CONV)
        ]
    )
    padded_grad = 0.0
    for offset in range(CONV):
        padded_grad = padded_grad + jnp.pad(
            conv_weight[offset] * conv_grad * masks[offset],
            ((0, 0), (offset, reach - offset), (0, 0), (0, 0)),
        )
    head_grad = jnp.swapaxes(padded_grad[:, :reach], 0, 1).reshape(
        reach, chan_count * CHUNKS, channels
    )
    from_next = passed_along(head_grad[:, 0], "seq", -1)
    tail_grad = jnp.concatenate([head_grad[:, 1:], from_next[:, None]], 1)
    tail_grad = jnp.swapaxes(tail_grad.reshape(reach, chan_count, CHUNKS, channels), 0, 1)
    inner_grad = padded_grad[:, reach:] + jnp.pad(
        tail_grad, ((0, 0), (steps - reach, 0), (0, 0), (0, 0))
    )
    inner_grad_b = inner_grad.reshape(tok_seq, channels).astype(bf16)
    inner_weight_grad = jnp.einsum("td,te->de", gathered, inner_grad_b, preferred_element_type=f32)
    both_grad = jnp.concatenate([inner_grad_b, grad_gate_z], 1)
    normed_grad = chan_sums(
        lambda rows: jnp.dot(rows[:, :channels], in_weight[0].T, preferred_element_type=f32)
        + jnp.dot(rows[:, channels:], in_weight[1].T, preferred_element_type=f32),
        both_grad,
    )
    residual_grad, norm_gain_grad = norm_back(normed_grad)
    in_grad = from_steps(residual_grad + grad_hidden)

    late = (
        inner_weight_grad, xproj_grad, dt_weight_grad, a_log_grad,
        conv_weight_grad, conv_bias_grad, dt_bias_grad,
    )
    late, early = lax.optimization_barrier((tuple(part.astype(bf16) for part in late), early))
    late = lax.psum(late, "seq")
    (
        inner_weight_grad, xproj_grad, dt_weight_grad, a_log_grad,
        conv_weight_grad, conv_bias_grad, dt_bias_grad,
    ) = (part.astype(f32) for part in late)
    out_weight_grad, gate_weight_grad, skip_grad = (part.astype(f32) for part in early)
    in_weight_grad = jnp.stack([inner_weight_grad, gate_weight_grad])
    norm_gain_grad, moe_gain_grad, router_grad = lax.psum(
        (norm_gain_grad, moe_gain_grad, router_grad), ("seq", "chan")
    )
    return (
        block_out,
        in_grad,
        norm_gain_grad,
        in_weight_grad,
        conv_weight_grad,
        conv_bias_grad,
        xproj_grad,
        dt_weight_grad,
        dt_bias_grad,
        a_log_grad,
        skip_grad,
        out_weight_grad,
        moe_gain_grad,
        router_grad,
        up_grad,
        down_grad,
    )


def solution(mesh):
    in_specs = (
        P(("seq", "chan"), None),
        P(("seq", "chan"), None),
        P(),
        P(),
        P(None, None, "chan"),
        P(None, "chan"),
        P("chan"),
        P("chan", None),
        P(None, "chan"),
        P("chan"),
        P("chan", None),
        P("chan"),
        P("chan", None),
        P(),
        P(),
        P("chan", "seq", None),
        P("chan", "seq", None),
        P(("seq", "chan"), None),
    )
    out_specs = (
        P(("seq", "chan"), None),
        P(("seq", "chan"), None),
        P(),
        P(None, None, "chan"),
        P(None, "chan"),
        P("chan"),
        P("chan", None),
        P(None, "chan"),
        P("chan"),
        P("chan", None),
        P("chan"),
        P("chan", None),
        P(),
        P(),
        P("chan", "seq", None),
        P("chan", "seq", None),
    )
    return jax.shard_map(
        on_device, mesh=mesh, in_specs=in_specs, out_specs=out_specs, check_vma=False
    )
```

```python
from functools import partial

import jax
import jax.numpy as jnp
from jax import lax
from jax.experimental import pallas as pl
from jax.experimental.pallas import tpu as pltpu
from jax.sharding import PartitionSpec as P

STATE = 16
CONV = 4
DT_RANK = 72
EXPERTS = 8
SINK = 8
CHUNKS = 8
LANES = 128
VMEM_LIMIT = 56 * 1024 * 1024

EPS = 1e-05
HIGH = lax.Precision.HIGHEST
LOG2E = 1.4426950408889634
LN2 = 0.6931471805599453
BREAK = 1e30
MESH = pl.DeviceIdType.MESH


def passed_along(value, axis, steps):
    count = lax.axis_size(axis)
    leading, last = (max(0, -steps), min(count, count - steps))
    return lax.ppermute(value, axis, [(source, source + steps) for source in range(leading, last)])


def swapped(value, axis, bit):
    count = lax.axis_size(axis)
    return lax.ppermute(value, axis, [(source, source ^ bit) for source in range(count)])


def chan_rows(values):
    if lax.axis_size("chan") != 2:
        return lax.all_gather(values, "chan", axis=0, tiled=True)
    first = lax.axis_index("chan") == 0
    other = swapped(values, "chan", 1)
    return jnp.concatenate([jnp.where(first, values, other), jnp.where(first, other, values)], 0)


def chan_sums(term_fn, operand):
    count, place = lax.axis_size("chan"), lax.axis_index("chan")
    rows = operand.shape[0] // count
    if count != 2:
        return lax.psum_scatter(term_fn(operand), "chan", scatter_dimension=0, tiled=True)
    theirs = term_fn(lax.dynamic_slice_in_dim(operand, (1 - place) * rows, rows, 0))
    arrived = swapped(theirs.astype(jnp.bfloat16), "chan", 1)
    return term_fn(lax.dynamic_slice_in_dim(operand, place * rows, rows, 0)) + arrived.astype(
        jnp.float32
    )


def proj_total(values):
    if lax.axis_size("chan") != 2:
        return lax.psum(values, "chan")
    return values + swapped(values, "chan", 1)


def expert_groups():
    own = EXPERTS // lax.axis_size("chan")
    return own, lax.axis_size("seq") // own


def across_experts(values, axis, wait=None):
    own, share = expert_groups()
    place = lax.div(lax.axis_index("seq"), share)
    out = values
    for d in range(1, own):
        peer = lax.bitwise_xor(place, d)
        came = swapped(lax.dynamic_slice_in_dim(values, peer, 1, axis), "seq", d * share)
        if wait is not None:
            came = after(came, wait)
        out = lax.dynamic_update_slice_in_dim(out, came, peer, axis)
    return out


def to_owners(grad):
    own, share = expert_groups()
    if own == 1:
        return grad
    groups = [[k * share + q for k in range(own)] for q in range(share)]
    return lax.all_to_all(
        grad, "seq", split_axis=0, concat_axis=0, tiled=True, axis_index_groups=groups
    )


def expert_rows_early(packed):
    own, share = expert_groups()
    count = lax.axis_size("chan")
    slots, width = packed.shape[1:]
    if count == 2:
        place = lax.axis_index("chan")
        halves = packed.reshape(2, own, slots, width)
        kept = lax.dynamic_index_in_dim(halves, place, 0, False)
        came = swapped(lax.dynamic_index_in_dim(halves, 1 - place, 0, False), "chan", 1)
        first = place == 0
        arrived = jnp.stack([jnp.where(first, kept, came), jnp.where(first, came, kept)])
    else:
        arrived = lax.all_to_all(packed, "chan", split_axis=0, concat_axis=0, tiled=True)
        arrived = arrived.reshape(count, own, slots, width)
    return across_experts(arrived, 1).reshape(count * own, slots, width)


def expert_rows(ident, *arrays):
    return exchange(ident, arrays)


def whole_expert(weight, start, wait):
    own, share = expert_groups()
    features, hidden = weight.shape[1:]
    if start is not None:
        weight = after(weight, start)
    mine = across_experts(weight, 0, wait)
    groups = [[k * share + q for q in range(share)] for k in range(own)]
    full = lax.all_gather(mine, "seq", axis=1, axis_index_groups=groups)
    return full.reshape(own * share * features, hidden)


def halved(grad, stage):
    own, share = expert_groups()
    bit = 1 << stage
    pairs = grad.reshape(own, grad.shape[1] // 2, 2, *grad.shape[2:])
    side = lax.rem(lax.div(lax.axis_index("seq"), bit), 2)
    sent = lax.dynamic_index_in_dim(pairs, 1 - side, 2, False)
    kept = lax.dynamic_index_in_dim(pairs, side, 2, False)
    came = swapped(sent, "seq", bit)
    return (kept.astype(jnp.float32) + came.astype(jnp.float32)).astype(grad.dtype)


def after(value, *others):
    return lax.optimization_barrier((value,) + others)[0]


def opposite(place, bit):
    return place + bit - 2 * bit * lax.rem(lax.div(place, bit), 2)


def greet(targets):
    barrier = pltpu.get_barrier_semaphore()
    for target in targets:
        pl.semaphore_signal(barrier, inc=1, device_id=target, device_id_type=MESH)
    pl.semaphore_wait(barrier, len(targets))


def exchange_kernel(own, share, chans, count, *refs):
    sources, results = refs[:count], refs[count : 2 * count]
    send_sem, recv_sem, own_sem = refs[2 * count :]
    seq, chan = lax.axis_index("seq"), lax.axis_index("chan")
    column = lax.rem(seq, share)
    me = chan * own + lax.div(seq, share)
    total = own * chans
    peers = [lax.rem(me + d, total) for d in range(1, total)]
    targets = [(lax.rem(peer, own) * share + column, lax.div(peer, own)) for peer in peers]
    greet(targets)
    copies = []
    for k in range(count):
        for d in range(total - 1):
            copies.append(
                pltpu.make_async_remote_copy(
                    src_ref=sources[k].at[peers[d]],
                    dst_ref=results[k].at[me],
                    send_sem=send_sem.at[k, d],
                    recv_sem=recv_sem.at[k, d],
                    device_id=targets[d],
                    device_id_type=MESH,
                )
            )
        copies.append(pltpu.make_async_copy(sources[k].at[me], results[k].at[me], own_sem.at[k]))
    for copy in copies:
        copy.start()
    for copy in copies:
        copy.wait()


def exchange(ident, arrays):
    own, share = expert_groups()
    chans, count = lax.axis_size("chan"), len(arrays)
    anywhere = pl.BlockSpec(memory_space=pl.ANY)
    others = own * chans - 1
    return pl.pallas_call(
        partial(exchange_kernel, own, share, chans, count),
        in_specs=[anywhere] * count,
        out_specs=[anywhere] * count,
        out_shape=[jax.ShapeDtypeStruct(part.shape, part.dtype) for part in arrays],
        scratch_shapes=[
            pltpu.SemaphoreType.DMA((count, others)),
            pltpu.SemaphoreType.DMA((count, others)),
            pltpu.SemaphoreType.DMA((count,)),
        ],
        compiler_params=pltpu.CompilerParams(collective_id=ident, has_side_effects=True),
        name="expert_rows",
    )(*arrays)


def gather_kernel(devices, chans, own_ref, every_ref, send_sem, recv_sem):
    me = lax.axis_index("seq") * chans + lax.axis_index("chan")
    barrier = pltpu.get_barrier_semaphore()

    def target(d):
        peer = lax.rem(me + d, devices)
        return (lax.div(peer, chans), lax.rem(peer, chans))

    def copy(d):
        return pltpu.make_async_remote_copy(
            src_ref=own_ref,
            dst_ref=every_ref.at[me],
            send_sem=send_sem.at[d - 1],
            recv_sem=recv_sem.at[d - 1],
            device_id=target(d),
            device_id_type=MESH,
        )

    def signal(d, carry):
        pl.semaphore_signal(barrier, inc=1, device_id=target(d), device_id_type=MESH)
        return carry

    def start(d, carry):
        copy(d).start()
        return carry

    def finish(d, carry):
        copy(d).wait()
        return carry

    lax.fori_loop(1, devices, signal, 0)
    every_ref[me] = own_ref[...]
    pl.semaphore_wait(barrier, devices - 1)
    lax.fori_loop(1, devices, start, 0)
    lax.fori_loop(1, devices, finish, 0)


def gathered_everywhere(values):
    chans = lax.axis_size("chan")
    devices = lax.axis_size("seq") * chans
    return pl.pallas_call(
        partial(gather_kernel, devices, chans),
        in_specs=[pl.BlockSpec(memory_space=pltpu.VMEM)],
        out_specs=pl.BlockSpec(memory_space=pltpu.VMEM),
        out_shape=jax.ShapeDtypeStruct((devices,) + values.shape, values.dtype),
        scratch_shapes=[
            pltpu.SemaphoreType.DMA((devices - 1,)),
            pltpu.SemaphoreType.DMA((devices - 1,)),
        ],
        compiler_params=pltpu.CompilerParams(
            collective_id=3, has_side_effects=True, vmem_limit_bytes=VMEM_LIMIT
        ),
        name="gather_small",
    )(values)


def carry_kernel(
    count, reverse, total_ref, rate_ref, entry_ref, ends_out, ends_in, sums_out, sums_in, ends_sems, sums_sems
):
    me = lax.axis_index("seq")
    bits = [1 << k for k in range(count.bit_length() - 1)]
    greet([{"seq": opposite(me, bit)} for bit in bits])
    rates = rate_ref[...]
    ends, sums = total_ref[:STATE], total_ref[STATE : STATE + 1]
    before, before_sum = jnp.zeros_like(ends), jnp.zeros_like(sums)
    for k, bit in enumerate(bits):
        ends_out[k] = ends.astype(ends_out.dtype)
        sums_out[k] = sums
        copies = [
            pltpu.make_async_remote_copy(
                src_ref=out.at[k],
                dst_ref=into.at[k],
                send_sem=sems.at[0, k],
                recv_sem=sems.at[1, k],
                device_id={"seq": opposite(me, bit)},
                device_id_type=MESH,
            )
            for out, into, sems in ((ends_out, ends_in, ends_sems), (sums_out, sums_in, sums_sems))
        ]
        for copy in copies:
            copy.start()
        for copy in copies:
            copy.wait()
        their_ends, their_sums = ends_in[k].astype(jnp.float32), sums_in[k]
        theirs_first = lax.rem(lax.div(me, bit), 2) == (0 if reverse else 1)
        before = jnp.where(theirs_first, jnp.exp2(rates * before_sum) * their_ends + before, before)
        before_sum = jnp.where(theirs_first, before_sum + their_sums, before_sum)
        ends = jnp.where(
            theirs_first,
            jnp.exp2(rates * sums) * their_ends + ends,
            jnp.exp2(rates * their_sums) * ends + their_ends,
        )
        sums = sums + their_sums
    entry_ref[...] = before


def carried(total, rates, reverse):
    count = lax.axis_size("seq")
    rounds = count.bit_length() - 1
    channels = rates.shape[1]
    vmem = pl.BlockSpec(memory_space=pltpu.VMEM)
    return pl.pallas_call(
        partial(carry_kernel, count, reverse),
        in_specs=[vmem, vmem],
        out_specs=vmem,
        out_shape=jax.ShapeDtypeStruct(rates.shape, jnp.float32),
        scratch_shapes=[
            pltpu.VMEM((rounds, STATE, channels), jnp.bfloat16),
            pltpu.VMEM((rounds, STATE, channels), jnp.bfloat16),
            pltpu.VMEM((rounds, 1, channels), jnp.float32),
            pltpu.VMEM((rounds, 1, channels), jnp.float32),
            pltpu.SemaphoreType.DMA((2, rounds)),
            pltpu.SemaphoreType.DMA((2, rounds)),
        ],
        compiler_params=pltpu.CompilerParams(
            collective_id=5 if reverse else 4, has_side_effects=True, vmem_limit_bytes=VMEM_LIMIT
        ),
        name="carry_back" if reverse else "carry",
    )(total, rates)


def sum_kernel(count, places, sizes, *refs):
    parts, sum_ref = refs[: len(places)], refs[len(places)]
    held, incoming, send_sem, recv_sem = refs[len(places) + 1 :]
    me = lax.axis_index("seq")
    bits = [1 << k for k in range(count.bit_length() - 1)]
    peers = [{"seq": opposite(me, bit)} for bit in bits]
    chunks, rows = held.shape[0], held.shape[1]
    rounds = len(bits)
    barrier = pltpu.get_barrier_semaphore()
    for peer in peers:
        pl.semaphore_signal(barrier, inc=1, device_id=peer, device_id_type=MESH)
    for c in range(chunks):
        for part, place, size in zip(parts, places, sizes):
            low, high = max(place, c * rows), min(place + size, (c + 1) * rows)
            if low < high:
                held[c, low - c * rows : high - c * rows] = part[low - place : high - place].astype(held.dtype)
        used = max(place + size for place, size in zip(places, sizes))
        if used < (c + 1) * rows:
            low = max(used - c * rows, 0)
            held[c, low:] = jnp.zeros((rows - low, held.shape[2]), held.dtype)
    pl.semaphore_wait(barrier, rounds)

    sides = [lax.rem(lax.div(me, bit), 2) for bit in bits]
    lows, lengths = [0], [rows]
    for side in sides:
        lengths.append(lengths[-1] // 2)
        lows.append(lows[-1] + side * lengths[-1])

    def span(low, length):
        return pl.ds(pl.multiple_of(low, 16), length)

    def copy(c, step):
        if step < rounds:
            k = step
            other = lows[k] + (1 - sides[k]) * lengths[k + 1]
            source = held.at[c, span(other, lengths[k + 1])]
            target = incoming.at[c, pl.ds(rows - lengths[k], lengths[k + 1])]
        else:
            k = 2 * rounds - 1 - step
            here = span(lows[k + 1], lengths[k + 1])
            source, target = sum_ref.at[c, here], sum_ref.at[c, here]
        return pltpu.make_async_remote_copy(
            src_ref=source,
            dst_ref=target,
            send_sem=send_sem.at[c, step],
            recv_sem=recv_sem.at[c, step],
            device_id=peers[k],
            device_id_type=MESH,
        )

    copy(0, 0).start()
    for turn in range(2 * rounds + chunks - 1):
        if turn + 1 < chunks:
            copy(turn + 1, 0).start()
        for c in range(max(0, turn - 2 * rounds + 1), min(chunks, turn + 1)):
            step = turn - c
            copy(c, step).wait()
            if step < rounds:
                kept = span(lows[step + 1], lengths[step + 1])
                came = incoming[c, pl.ds(rows - lengths[step], lengths[step + 1])]
                total = held[c, kept].astype(jnp.float32) + came.astype(jnp.float32)
                if step < rounds - 1:
                    held[c, kept] = total.astype(held.dtype)
                else:
                    sum_ref[c, kept] = total.astype(sum_ref.dtype)
            if step < 2 * rounds - 1:
                copy(c, step + 1).start()


def summed(parts):
    count = lax.axis_size("seq")
    rounds = count.bit_length() - 1
    width = parts[0].shape[1]
    sizes = [part.shape[0] for part in parts]
    places, used = [], 0
    for size in sizes:
        places.append(used)
        used += -(-size // 16) * 16
    chunk = 16 * count * max(1, 48 // count)
    chunks = -(-used // chunk)
    vmem = pl.BlockSpec(memory_space=pltpu.VMEM)
    padded = [jnp.pad(part, ((0, -part.shape[0] % 16), (0, 0))) for part in parts]
    total = pl.pallas_call(
        partial(sum_kernel, count, places, [part.shape[0] for part in padded]),
        in_specs=[vmem] * len(parts),
        out_specs=vmem,
        out_shape=jax.ShapeDtypeStruct((chunks, chunk, width), jnp.bfloat16),
        scratch_shapes=[
            pltpu.VMEM((chunks, chunk, width), jnp.bfloat16),
            pltpu.VMEM((chunks, chunk, width), jnp.bfloat16),
            pltpu.SemaphoreType.DMA((chunks, 2 * rounds)),
            pltpu.SemaphoreType.DMA((chunks, 2 * rounds)),
        ],
        compiler_params=pltpu.CompilerParams(
            collective_id=6, has_side_effects=True, vmem_limit_bytes=VMEM_LIMIT
        ),
        name="sum_late",
    )(*padded).reshape(chunks * chunk, width)
    return [total[place : place + size].astype(jnp.float32) for place, size in zip(places, sizes)]


def to_steps(values):
    rows = values.shape[0]
    parts = values.reshape((CHUNKS, rows // CHUNKS) + values.shape[1:])
    return jnp.swapaxes(parts, 0, 1).reshape(values.shape)


def from_steps(values):
    rows = values.shape[0]
    parts = values.reshape((rows // CHUNKS, CHUNKS) + values.shape[1:])
    return jnp.swapaxes(parts, 0, 1).reshape(values.shape)


def stacked(*parts):
    rows = sum(part.shape[0] for part in parts)
    whole = jnp.concatenate([part.astype(jnp.bfloat16) for part in parts], 0)
    return jnp.pad(whole, ((0, -rows % 16), (0, 0)))


def unstacked(whole, parts):
    out, first = [], 0
    for part in parts:
        out.append(whole[first : first + part.shape[0]].astype(jnp.float32))
        first += part.shape[0]
    return out


def norm_apply(values, gain):
    return values * lax.rsqrt(jnp.mean(values * values, -1, keepdims=True) + EPS) * gain


def silu_grad(values):
    sigma = jax.nn.sigmoid(values)
    return sigma * (1.0 + values * (1.0 - sigma))


def gelu_grad(values, upstream):
    return jax.vjp(partial(jax.nn.gelu, approximate=True), values)[1](upstream)[0]


def spread(target, source):
    for n in range(STATE):
        target[n] = jnp.broadcast_to(source[:, n : n + 1], target.shape[1:])


def full(row):
    return jnp.broadcast_to(row, (CHUNKS, LANES))


def shifted(values, by, down):
    sub = lax.broadcasted_iota(jnp.int32, (CHUNKS, LANES), 0)
    if down:
        return jnp.where(sub >= by, pltpu.roll(values, by, 0), 0.0)
    return jnp.where(sub < CHUNKS - by, pltpu.roll(values, CHUNKS - by, 0), 0.0)


def chunk_windows(sums, down):
    windows = []
    for by in (1, 2, 4):
        windows.append(sums)
        sums = sums + shifted(sums, by, down)
    return windows, sums


def chunk_prefix(ends, windows, rate, down):
    for by, window in zip((1, 2, 4), windows):
        ends = ends + jnp.exp2(rate * window) * shifted(ends, by, down)
    return ends


def ends_kernel(halves, reverse, step_ref, drive_ref, break_ref, map_ref, rate_ref, part_ref, sum_ref, tot_ref, wide):
    rows = step_ref.shape[0]
    steps = rows // (halves * CHUNKS)

    @pl.when(pl.program_id(0) == 0)
    def _():
        spread(wide, map_ref)

    rates = [full(rate_ref[n : n + 1, :]) for n in range(STATE)]
    zero = jnp.zeros((CHUNKS, LANES), jnp.float32)

    def half(turn, carry):
        h = halves - 1 - turn if reverse else turn
        before_sum, before = carry[0], carry[1:]

        def body(k, state):
            s = steps - 1 - k if reverse else k
            at = pl.ds(pl.multiple_of((h * steps + s) * CHUNKS, CHUNKS), CHUNKS)
            step = step_ref[at, :]
            decay_step = step + break_ref[at, :]
            drive = drive_ref[at, :]
            if not reverse:
                drive = drive * step
            new = [state[0] + decay_step]
            for n in range(STATE):
                decay = jnp.exp2(decay_step * rates[n])
                if reverse:
                    new.append(decay * (state[n + 1] + drive * wide[n, at, :]))
                else:
                    new.append(decay * state[n + 1] + drive * wide[n, at, :])
            return tuple(new)

        out = lax.fori_loop(0, steps, body, (zero,) * (STATE + 1), unroll=2)
        windows, sums = chunk_windows(out[0], not reverse)
        prior = shifted(sums, 1, not reverse)
        last = slice(0, 1) if reverse else slice(CHUNKS - 1, CHUNKS)
        sum_ref[h] = prior + before_sum
        new = [before_sum + full(sums[last])]
        for n in range(STATE):
            joined = chunk_prefix(out[n + 1], windows, rates[n], not reverse)
            part_ref[h, n] = shifted(joined, 1, not reverse) + jnp.exp2(rates[n] * prior) * before[n]
            new.append(full(joined[last]) + jnp.exp2(rates[n] * full(sums[last])) * before[n])
        return tuple(new)

    total = lax.fori_loop(0, halves, half, (zero,) * (STATE + 1))
    for n in range(STATE):
        tot_ref[n : n + 1, :] = total[n + 1][0:1]
    tot_ref[STATE:, :] = total[0]


def outputs_kernel(
    halves, step_ref, mixed_ref, break_ref, b_ref, c_ref, rate_ref, part_ref, sum_ref, device,
    skip_ref, gate_ref, scan_ref, gated_ref, entry_ref, b_wide, c_wide,
):
    rows = step_ref.shape[0]
    steps = rows // (halves * CHUNKS)

    @pl.when(pl.program_id(0) == 0)
    def _():
        spread(b_wide, b_ref)
        spread(c_wide, c_ref)

    rates = [full(rate_ref[n : n + 1, :]) for n in range(STATE)]

    def half(h, carry):
        state = []
        for n in range(STATE):
            state.append(
                part_ref[h, n] + jnp.exp2(rates[n] * sum_ref[h]) * full(device[n : n + 1, :])
            )
            entry_ref[h, n] = state[n]

        def body(s, state):
            at = pl.ds(pl.multiple_of((h * steps + s) * CHUNKS, CHUNKS), CHUNKS)
            step = step_ref[at, :]
            decay_step = step + break_ref[at, :]
            drive = mixed_ref[at, :] * step
            total = None
            new = []
            for n in range(STATE):
                value = jnp.exp2(decay_step * rates[n]) * state[n] + drive * b_wide[n, at, :]
                term = value * c_wide[n, at, :]
                total = term if total is None else total + term
                new.append(value)
            scan_ref[at, :] = total
            return tuple(new)

        lax.fori_loop(0, steps, body, tuple(state), unroll=2)
        return carry

    lax.fori_loop(0, halves, half, 0)
    gate = gate_ref[...]
    out = scan_ref[...] + skip_ref[...] * mixed_ref[...]
    scan_ref[...] = out
    gated_ref[...] = (out * (gate * jax.nn.sigmoid(gate))).astype(gated_ref.dtype)


def grads_kernel(
    halves, step_ref, mixed_ref, break_ref, grad_ref, b_ref, c_ref, rate_ref, entry_ref, part_ref, sum_ref,
    device, step_out, mixed_out, b_out, c_out, rate_out, b_wide, c_wide, b_sum, c_sum, decays, states,
):
    rows = step_ref.shape[0]
    steps = rows // (halves * CHUNKS)
    group = pl.program_id(0)
    block = STATE // 2

    @pl.when(group == 0)
    def _():
        spread(b_wide, b_ref)
        spread(c_wide, c_ref)
        b_sum[...] = jnp.zeros_like(b_sum)
        c_sum[...] = jnp.zeros_like(c_sum)

    zero = jnp.zeros((CHUNKS, LANES), jnp.float32)

    for first in (0, block):
        rates = [full(rate_ref[first + n : first + n + 1, :]) for n in range(block)]

        def half(h, rate_sums):
            entry = []
            for n in range(block):
                entry.append(entry_ref[h, first + n])
                states[0, n] = entry[n]

            def ahead(s, state):
                at = pl.ds(pl.multiple_of((h * steps + s) * CHUNKS, CHUNKS), CHUNKS)
                step = step_ref[at, :]
                decay_step = step + break_ref[at, :]
                drive = mixed_ref[at, :] * step
                new = []
                for n in range(block):
                    decay = jnp.exp2(decay_step * rates[n])
                    value = decay * state[n] + drive * b_wide[first + n, at, :]
                    decays[s, n] = decay
                    states[s + 1, n] = value
                    new.append(value)
                return tuple(new)

            lax.fori_loop(0, steps, ahead, tuple(entry), unroll=2)

            exits = [
                part_ref[h, first + n]
                + jnp.exp2(rates[n] * sum_ref[h]) * full(device[first + n : first + n + 1, :])
                for n in range(block)
            ]

            def back(k, carry):
                s = steps - 1 - k
                at = pl.ds(pl.multiple_of((h * steps + s) * CHUNKS, CHUNKS), CHUNKS)
                step = step_ref[at, :]
                mixed = mixed_ref[at, :]
                grad = grad_ref[at, :]
                drive = mixed * step
                by_rate, by_map = zero, zero
                flows, sums = [], []
                for n in range(block):
                    b_now, c_now = b_wide[first + n, at, :], c_wide[first + n, at, :]
                    here = carry[n] + c_now * grad
                    flow = decays[s, n] * here
                    log_grad = flow * states[s, n]
                    by_rate = by_rate + rates[n] * log_grad
                    by_map = by_map + b_now * here
                    b_sum[first + n, at, :] += drive * here
                    c_sum[first + n, at, :] += grad * states[s + 1, n]
                    flows.append(flow)
                    sums.append(carry[block + n] + step * log_grad)
                by_rate = by_rate * LN2 + mixed * by_map
                by_map = step * by_map
                if first == 0:
                    step_out[at, :] = by_rate
                    mixed_out[at, :] = by_map
                else:
                    step_out[at, :] += by_rate
                    mixed_out[at, :] += by_map
                return tuple(flows + sums)

            out = lax.fori_loop(0, steps, back, tuple(exits) + rate_sums)
            return out[block:]

        rate_sums = lax.fori_loop(0, halves, half, (zero,) * block)
        for n in range(block):
            rate_out[first + n : first + n + 1, :] = jnp.sum(rate_sums[n], 0, keepdims=True)

    @pl.when(group == pl.num_programs(0) - 1)
    def _():
        for n in range(STATE):
            b_out[:, n : n + 1] = jnp.sum(b_sum[n], -1, keepdims=True)
            c_out[:, n : n + 1] = jnp.sum(c_sum[n], -1, keepdims=True)


class Scan:
    def __init__(self, rows, channels, halves):
        self.rows, self.channels, self.halves = rows, channels, halves
        self.groups = channels // LANES
        row_spec = pl.BlockSpec((rows, LANES), lambda g: (0, g))
        fixed = lambda *shape: pl.BlockSpec(shape, lambda g: (0,) * len(shape))
        self.row_spec = row_spec
        self.break_spec = fixed(rows, LANES)
        self.map_spec = fixed(rows, STATE)
        self.rate_spec = pl.BlockSpec((STATE, LANES), lambda g: (0, g))
        self.part_spec = pl.BlockSpec((halves, STATE, CHUNKS, LANES), lambda g: (0, 0, 0, g))
        self.sum_spec = pl.BlockSpec((halves, CHUNKS, LANES), lambda g: (0, 0, g))
        self.tot_spec = pl.BlockSpec((STATE + CHUNKS, LANES), lambda g: (0, g))
        self.skip_spec = pl.BlockSpec((1, LANES), lambda g: (0, g))
        self.row_f32 = jax.ShapeDtypeStruct((rows, channels), jnp.float32)
        self.part_f32 = jax.ShapeDtypeStruct((halves, STATE, CHUNKS, channels), jnp.float32)
        self.sum_f32 = jax.ShapeDtypeStruct((halves, CHUNKS, channels), jnp.float32)
        self.tot_f32 = jax.ShapeDtypeStruct((STATE + CHUNKS, channels), jnp.float32)
        self.wide = pltpu.VMEM((STATE, rows, LANES), jnp.float32)

    def params(self):
        return pltpu.CompilerParams(
            dimension_semantics=("arbitrary",), vmem_limit_bytes=VMEM_LIMIT
        )

    def cost(self, per_element):
        count = self.rows * self.channels * STATE
        return pl.CostEstimate(
            flops=per_element * count, bytes_accessed=12 * self.rows * self.channels, transcendentals=count
        )

    def ends(self, reverse, step, drive, breaks, maps, rates):
        return pl.pallas_call(
            partial(ends_kernel, self.halves, reverse),
            grid=(self.groups,),
            in_specs=[self.row_spec, self.row_spec, self.break_spec, self.map_spec, self.rate_spec],
            out_specs=[self.part_spec, self.sum_spec, self.tot_spec],
            out_shape=[self.part_f32, self.sum_f32, self.tot_f32],
            scratch_shapes=[self.wide],
            compiler_params=self.params(),
            cost_estimate=self.cost(5),
            name="scan_ends_back" if reverse else "scan_ends",
        )(step, drive, breaks, maps, rates)

    def outputs(self, step, mixed, breaks, b_in, c_out, rates, part, sums, device, skip, gate):
        return pl.pallas_call(
            partial(outputs_kernel, self.halves),
            grid=(self.groups,),
            in_specs=[
                self.row_spec, self.row_spec, self.break_spec, self.map_spec, self.map_spec, self.rate_spec,
                self.part_spec, self.sum_spec, self.rate_spec, self.skip_spec, self.row_spec,
            ],
            out_specs=[self.row_spec, self.row_spec, self.part_spec],
            out_shape=[
                self.row_f32,
                jax.ShapeDtypeStruct((self.rows, self.channels), jnp.bfloat16),
                self.part_f32,
            ],
            scratch_shapes=[self.wide, self.wide],
            compiler_params=self.params(),
            cost_estimate=self.cost(7),
            name="scan_outputs",
        )(step, mixed, breaks, b_in, c_out, rates, part, sums, device, skip, gate)

    def grads(self, step, mixed, breaks, grad, b_in, c_out, rates, entry, part, sums, device):
        steps = self.rows // (self.halves * CHUNKS)
        block = STATE // 2
        return pl.pallas_call(
            partial(grads_kernel, self.halves),
            grid=(self.groups,),
            in_specs=[
                self.row_spec, self.row_spec, self.break_spec, self.row_spec, self.map_spec, self.map_spec,
                self.rate_spec, self.part_spec, self.part_spec, self.sum_spec, self.rate_spec,
            ],
            out_specs=[self.row_spec, self.row_spec, self.map_spec, self.map_spec, self.rate_spec],
            out_shape=[
                self.row_f32,
                self.row_f32,
                jax.ShapeDtypeStruct((self.rows, STATE), jnp.float32),
                jax.ShapeDtypeStruct((self.rows, STATE), jnp.float32),
                jax.ShapeDtypeStruct((STATE, self.channels), jnp.float32),
            ],
            scratch_shapes=[
                self.wide, self.wide, self.wide, self.wide,
                pltpu.VMEM((steps, block, CHUNKS, LANES), jnp.float32),
                pltpu.VMEM((steps + 1, block, CHUNKS, LANES), jnp.float32),
            ],
            compiler_params=self.params(),
            cost_estimate=self.cost(20),
            name="scan_grads",
        )(step, mixed, breaks, grad, b_in, c_out, rates, entry, part, sums, device)


def over_tokens(values):
    return jnp.sum(jnp.sum(values, 0), -1, keepdims=True)


def sinkhorn_kernel(place_ref, logit_ref, route_ref, gate_ref, scaled_ref, row_ref, column_ref):
    probs = jnp.exp(logit_ref[...])
    for sweep in range(SINK):
        column = over_tokens(probs)
        scaled = probs / column[None]
        row = jnp.sum(scaled, 1, keepdims=True)
        scaled_ref[sweep] = scaled
        row_ref[sweep] = row
        column_ref[sweep] = jnp.broadcast_to(column, column_ref.shape[1:])
        probs = scaled / row
    place = place_ref[0]
    own = scaled_ref[SINK - 1, place] / row_ref[SINK - 1, place]
    ids = lax.broadcasted_iota(jnp.int32, own.shape, 0)
    gate_ref[...] = EXPERTS * jnp.sum(jnp.where(ids == route_ref[...], own, 0.0), 0, keepdims=True)


def sinkhorn_back_kernel(place_ref, logit_ref, scaled_ref, row_ref, column_ref, grad_ref, out_ref, held):
    grad = grad_ref[...]
    for sweep in reversed(range(SINK)):
        scaled, row = scaled_ref[sweep], row_ref[sweep]
        inner = jnp.sum(grad * (scaled / row), 1, keepdims=True)
        grad = (grad - inner) / row
        along = over_tokens(grad * scaled)
        grad = (grad - along[None]) / column_ref[sweep][:, 0:1][None]
    held[...] = grad
    place = place_ref[0]
    out_ref[...] = held[place] * jnp.exp(logit_ref[place])


def in_vmem(count):
    return [pl.BlockSpec(memory_space=pltpu.SMEM)] + [pl.BlockSpec(memory_space=pltpu.VMEM)] * count


def sinkhorn(place, logits, routes):
    devices, experts, tokens = logits.shape
    f32 = lambda *shape: jax.ShapeDtypeStruct(shape, jnp.float32)
    return pl.pallas_call(
        sinkhorn_kernel,
        in_specs=in_vmem(2),
        out_specs=in_vmem(4)[1:],
        out_shape=[
            f32(1, tokens),
            f32(SINK, devices, experts, tokens),
            f32(SINK, devices, 1, tokens),
            f32(SINK, experts, LANES),
        ],
        compiler_params=pltpu.CompilerParams(vmem_limit_bytes=VMEM_LIMIT),
        name="sinkhorn",
    )(place, logits, routes)


def sinkhorn_back(place, logits, scaled, rows, columns, grad):
    devices, experts, tokens = logits.shape
    return pl.pallas_call(
        sinkhorn_back_kernel,
        in_specs=in_vmem(5),
        out_specs=in_vmem(1)[1],
        out_shape=jax.ShapeDtypeStruct((experts, tokens), jnp.float32),
        scratch_shapes=[pltpu.VMEM(logits.shape, jnp.float32)],
        compiler_params=pltpu.CompilerParams(vmem_limit_bytes=VMEM_LIMIT),
        name="sinkhorn_back",
    )(place, logits, scaled, rows, columns, grad)


def on_device(
    block_in,
    routes,
    doc_lengths,
    norm_gain,
    in_weight,
    conv_weight,
    conv_bias,
    xproj_weight,
    dt_weight,
    dt_bias,
    a_log,
    skip_gain,
    out_weight,
    moe_gain,
    router_weight,
    up_weight,
    down_weight,
    out_grad,
):
    tok_dev, model_width = block_in.shape
    chan_count = lax.axis_size("chan")
    chan_place, seq_place = lax.axis_index("chan"), lax.axis_index("seq")
    dev_ref = (seq_place * chan_count + chan_place).astype(jnp.int32).reshape(1)
    steps = tok_dev // CHUNKS
    tok_seq = tok_dev * chan_count
    channels = in_weight.shape[2]
    padded_channels = -(-channels // LANES) * LANES
    f32, bf16 = jnp.float32, jnp.bfloat16

    route_col = routes[:, 0]
    expert_ids = lax.broadcasted_iota(jnp.int32, (1, EXPERTS), 1)
    chosen = (route_col[:, None] == expert_ids).astype(bf16)
    row_ids = lax.broadcasted_iota(jnp.int32, (tok_dev, tok_dev), 0)
    col_ids = lax.broadcasted_iota(jnp.int32, (tok_dev, tok_dev), 1)
    counts = jnp.dot((col_ids <= row_ids).astype(bf16), chosen, preferred_element_type=f32)
    rank = (jnp.sum(counts * chosen.astype(f32), 1) - 1.0).astype(jnp.int32)
    capacity = tok_dev * 5 // (4 * EXPERTS) + 1
    capacity = -(-capacity // 16) * 16
    slot = to_steps(route_col * capacity + rank)
    route_steps = to_steps(route_col)
    slot_ids = lax.broadcasted_iota(jnp.int32, (1, EXPERTS * capacity), 1)
    placer = (slot[:, None] == slot_ids).astype(bf16)

    def pack(values):
        rows = jnp.einsum("ts,td->sd", placer, values, preferred_element_type=f32).astype(bf16)
        return rows.reshape(EXPERTS, capacity, model_width)

    def unpack(values):
        return jnp.einsum(
            "ts,sd->td",
            placer,
            values.reshape(EXPERTS * capacity, model_width),
            preferred_element_type=f32,
        )

    block_steps = to_steps(block_in)
    grad_steps = to_steps(out_grad)
    residual = block_steps.astype(f32)
    normed, norm_back = jax.vjp(norm_apply, residual, norm_gain)
    gathered = chan_rows(normed.astype(bf16))

    inner_b = jnp.dot(gathered, in_weight[0], preferred_element_type=f32).astype(bf16)
    gate_z = jnp.dot(gathered, in_weight[1], preferred_element_type=f32)

    shape4 = (chan_count, steps, CHUNKS)
    ids = [lax.broadcasted_iota(jnp.int32, shape4, axis) for axis in range(3)]
    position = seq_place * tok_seq + ids[0] * tok_dev + ids[2] * steps + ids[1]
    starts = jnp.cumsum(doc_lengths) - doc_lengths
    doc_first = jnp.max(
        jnp.where(starts <= position[..., None], starts, 0), axis=-1
    )
    reach = CONV - 1
    inner = inner_b.astype(f32).reshape(shape4 + (channels,))
    tails = jnp.swapaxes(inner[:, steps - reach :], 0, 1).reshape(reach, chan_count * CHUNKS, channels)
    previous = passed_along(tails[:, -1], "seq", 1)
    heads = jnp.concatenate([previous[:, None], tails[:, :-1]], 1)
    heads = jnp.swapaxes(heads.reshape(reach, chan_count, CHUNKS, channels), 0, 1)
    padded = jnp.concatenate([heads, inner], 1)
    masks = [
        (position - (reach - offset) >= doc_first).astype(f32)[..., None] for offset in range(CONV)
    ]
    conv_pre = conv_bias
    for offset in range(CONV):
        conv_pre = conv_pre + conv_weight[offset] * padded[:, offset : offset + steps] * masks[offset]
    conv_pre = conv_pre.reshape(tok_seq, channels)
    mixed_b = jax.nn.silu(conv_pre).astype(bf16)
    mixed = mixed_b.astype(f32)
    proj_all = proj_total(jnp.dot(mixed_b, xproj_weight, preferred_element_type=f32))
    low_rank = proj_all[:, :DT_RANK]
    b_in = proj_all[:, DT_RANK : DT_RANK + STATE]
    c_out = proj_all[:, DT_RANK + STATE :]
    step_pre = jnp.dot(low_rank, dt_weight, precision=HIGH) + dt_bias
    step_size = jax.nn.softplus(step_pre)

    def widened(values, axis=-1):
        more = padded_channels - channels
        if not more:
            return values
        pads = [(0, 0)] * values.ndim
        pads[axis] = (0, more)
        return jnp.pad(values, pads)

    scan = Scan(tok_seq, padded_channels, chan_count)
    decay_rates = jnp.exp(a_log)
    rates = widened((-LOG2E * decay_rates).T)
    breaks = jnp.any(position[..., None] == starts, axis=-1).astype(f32) * BREAK
    breaks = jnp.broadcast_to(breaks.reshape(tok_seq, 1), (tok_seq, LANES))
    step_w, mixed_w = widened(step_size), widened(mixed)
    part, sums, total = scan.ends(False, step_w, mixed_w, breaks, b_in, rates)
    device_entry = carried(total, rates, False)
    full_up = whole_expert(up_weight, None, device_entry)
    grad_arrived = expert_rows_early(after(pack(grad_steps), device_entry)).reshape(-1, model_width)
    scan_out, gated_b, entry = scan.outputs(
        step_w, mixed_w, breaks, b_in, c_out, rates, part, sums, device_entry,
        widened(skip_gain[None]), widened(gate_z),
    )
    scan_out, gated_b = scan_out[:, :channels], gated_b[:, :channels]
    full_down = whole_expert(down_weight, device_entry, gated_b)

    mixer_rows = chan_sums(
        lambda rows: jnp.dot(rows, out_weight, preferred_element_type=f32), gated_b
    )
    hidden_one = residual + mixer_rows
    moe_in, moe_back = jax.vjp(norm_apply, hidden_one, moe_gain)
    logits = jnp.einsum("td,de->et", moe_in, router_weight, precision=HIGH)
    every_logit = gathered_everywhere(logits)
    gate_row, scaled, row_totals, columns = sinkhorn(
        dev_ref, every_logit, route_steps.reshape(1, tok_dev)
    )
    gate = gate_row.reshape(tok_dev)

    gate_slots = jnp.einsum("ts,t->s", placer.astype(f32), gate, precision=HIGH)
    gate_slots = jnp.pad(gate_slots.reshape(EXPERTS, 1, capacity), ((0, 0), (0, 7), (0, LANES - capacity)))
    arrived, gate_arrived = expert_rows(1, pack(moe_in.astype(bf16)), gate_slots)
    arrived = arrived.reshape(-1, model_width)
    gate_arrived = gate_arrived[:, 0, :capacity].reshape(-1, 1)
    pre = jnp.dot(arrived, full_up, preferred_element_type=f32)
    act_b = jax.nn.gelu(pre, approximate=True).astype(bf16)
    expert_out = jnp.einsum("sf,df->sd", act_b, full_down, preferred_element_type=f32).astype(bf16)
    grad_act = jnp.dot(grad_arrived, full_down, preferred_element_type=f32)
    plain_grad_pre = gelu_grad(pre, grad_act)
    grad_rows_in = jnp.einsum(
        "sf,df->sd", plain_grad_pre.astype(bf16), full_up, preferred_element_type=f32
    ).astype(bf16)
    blocks = (EXPERTS, capacity, model_width)

    grad_gated_rows = (grad_arrived.astype(f32) * gate_arrived).astype(bf16)
    grad_pre_b = (plain_grad_pre * gate_arrived).astype(bf16)
    down_part = jnp.einsum("sd,sf->df", grad_gated_rows, act_b, preferred_element_type=f32)
    up_part = jnp.einsum("sd,sf->df", arrived, grad_pre_b, preferred_element_type=f32)
    own, share = expert_groups()
    expert_grads = [
        halved(part.astype(bf16).reshape(own, share, -1, part.shape[1]), 0) for part in (up_part, down_part)
    ]
    expert_back, grad_back = expert_rows(
        2, after(expert_out, *expert_grads).reshape(blocks), grad_rows_in.reshape(blocks)
    )
    for stage in range(1, share.bit_length() - 1):
        expert_grads = [halved(part, stage) for part in expert_grads]
    expert_tok = unpack(after(expert_back, *expert_grads))
    plain_grad_part = unpack(grad_back)
    up_part, down_part = expert_grads
    up_grad = to_owners(after(up_part.reshape(own, *up_part.shape[2:]), expert_back))

    block_out = from_steps((hidden_one + gate[:, None] * expert_tok).astype(bf16))
    grad_two = grad_steps.astype(f32)
    grad_gate = jnp.sum(expert_tok * grad_two, 1)
    grad_probs = jnp.where(
        route_steps[None] == lax.broadcasted_iota(jnp.int32, (EXPERTS, 1), 0),
        EXPERTS * grad_gate[None],
        0.0,
    )
    grad_logits = sinkhorn_back(
        dev_ref, every_logit, scaled, row_totals, columns, gathered_everywhere(grad_probs)
    )
    router_grad = jnp.einsum("td,et->ed", moe_in, grad_logits, precision=HIGH)
    grad_moe_in = gate[:, None] * plain_grad_part + jnp.einsum(
        "et,de->td", grad_logits, router_weight, precision=HIGH
    )
    grad_hidden, moe_gain_grad = moe_back(grad_moe_in)
    grad_hidden = grad_hidden + grad_two

    grad_mix = chan_rows(grad_hidden.astype(bf16))
    grad_gated = jnp.einsum("td,ed->te", grad_mix, out_weight, preferred_element_type=f32)
    out_weight_grad = jnp.einsum("te,td->ed", gated_b, grad_mix, preferred_element_type=f32)
    grad_scan = grad_gated * jax.nn.silu(gate_z)
    grad_gate_z = (grad_gated * scan_out * silu_grad(gate_z)).astype(bf16)
    skip_grad = jnp.sum(grad_scan * mixed, 0)
    gate_weight_grad = jnp.einsum("td,te->de", gathered, grad_gate_z, preferred_element_type=f32)
    gains = jnp.concatenate([moe_gain_grad[None], router_grad], 0)
    gains = lax.psum(gains, "chan") if chan_count != 2 else gains + swapped(gains, "chan", 1)
    grad_scan_w = widened(grad_scan)
    back_part, back_sums, back_total = scan.ends(True, step_w, grad_scan_w, breaks, c_out, rates)
    back_entry = carried(after(back_total, up_grad), rates, True)
    down_grad = to_owners(after(down_part.reshape(own, *down_part.shape[2:]), back_entry))
    step_grad, mixed_grad, b_grad, c_grad, rate_grad = scan.grads(
        step_w, mixed_w, breaks, grad_scan_w, b_in, c_out, rates, entry, back_part, back_sums,
        back_entry,
    )
    step_grad = after(step_grad, down_grad)
    step_grad, mixed_grad = step_grad[:, :channels], mixed_grad[:, :channels]
    mixed_grad = mixed_grad + skip_gain * grad_scan
    a_log_rows = -decay_rates.T * rate_grad[:, :channels]
    step_pre_grad = step_grad * jax.nn.sigmoid(step_pre)
    dt_bias_grad = jnp.sum(step_pre_grad, 0)
    dt_weight_grad = jnp.einsum("tr,te->re", low_rank, step_pre_grad, precision=HIGH)
    rank_grad = jnp.einsum("te,re->tr", step_pre_grad, dt_weight, precision=HIGH)
    proj_grad_b = proj_total(jnp.concatenate([rank_grad, b_grad, c_grad], 1)).astype(bf16)
    mixed_grad = mixed_grad + jnp.einsum(
        "tp,ep->te", proj_grad_b, xproj_weight, preferred_element_type=f32
    )
    xproj_rows = jnp.einsum("te,tp->pe", mixed_b, proj_grad_b, preferred_element_type=f32)
    conv_grad = (mixed_grad * silu_grad(conv_pre)).reshape(shape4 + (channels,))
    conv_bias_grad = jnp.sum(conv_grad, (0, 1, 2))
    conv_weight_grad = jnp.stack(
        [
            jnp.sum(conv_grad * masks[offset] * padded[:, offset : offset + steps], (0, 1, 2))
            for offset in range(CONV)
        ]
    )
    padded_grad = 0.0
    for offset in range(CONV):
        padded_grad = padded_grad + jnp.pad(
            conv_weight[offset] * conv_grad * masks[offset],
            ((0, 0), (offset, reach - offset), (0, 0), (0, 0)),
        )
    head_grad = jnp.swapaxes(padded_grad[:, :reach], 0, 1).reshape(
        reach, chan_count * CHUNKS, channels
    )
    from_next = passed_along(head_grad[:, 0], "seq", -1)
    tail_grad = jnp.concatenate([head_grad[:, 1:], from_next[:, None]], 1)
    tail_grad = jnp.swapaxes(tail_grad.reshape(reach, chan_count, CHUNKS, channels), 0, 1)
    inner_grad = padded_grad[:, reach:] + jnp.pad(
        tail_grad, ((0, 0), (steps - reach, 0), (0, 0), (0, 0))
    )
    inner_grad_b = inner_grad.reshape(tok_seq, channels).astype(bf16)
    inner_weight_grad = jnp.einsum("td,te->de", gathered, inner_grad_b, preferred_element_type=f32)
    both_grad = jnp.concatenate([inner_grad_b, grad_gate_z], 1)
    normed_grad = chan_sums(
        lambda rows: jnp.dot(rows[:, :channels], in_weight[0].T, preferred_element_type=f32)
        + jnp.dot(rows[:, channels:], in_weight[1].T, preferred_element_type=f32),
        both_grad,
    )
    residual_grad, norm_gain_grad = norm_back(normed_grad)
    in_grad = from_steps(residual_grad + grad_hidden)

    norm_rows = norm_gain_grad[None]
    norm_rows = lax.psum(norm_rows, "chan") if chan_count != 2 else norm_rows + swapped(norm_rows, "chan", 1)
    pieces = (
        xproj_rows, dt_weight_grad, a_log_rows, conv_weight_grad, conv_bias_grad[None], dt_bias_grad[None],
        skip_grad[None], norm_rows.reshape(-1, channels), gains.reshape(-1, channels),
    )
    bounds = [sum(part.shape[0] for part in pieces[: k + 1]) for k in range(len(pieces) - 1)]
    inner_weight_grad, gate_weight_grad, out_weight_grad, small = summed(
        [
            inner_weight_grad.astype(bf16), gate_weight_grad.astype(bf16),
            out_weight_grad.astype(bf16).reshape(-1, channels), jnp.concatenate(pieces, 0),
        ]
    )
    (
        xproj_rows, dt_weight_grad, a_log_rows, conv_weight_grad, conv_bias_grad, dt_bias_grad, skip_grad,
        norm_rows, gains,
    ) = jnp.split(small, bounds, 0)
    out_weight_grad = out_weight_grad.reshape(channels, model_width)
    norm_gain_grad, gains = norm_rows.reshape(-1), gains.reshape(-1, model_width)
    xproj_grad, a_log_grad = xproj_rows.T, a_log_rows.T
    conv_bias_grad, dt_bias_grad, skip_grad = conv_bias_grad[0], dt_bias_grad[0], skip_grad[0]
    moe_gain_grad, router_grad = gains[0], gains[1:].T
    in_weight_grad = jnp.stack([inner_weight_grad, gate_weight_grad])
    return (
        block_out,
        in_grad,
        norm_gain_grad,
        in_weight_grad,
        conv_weight_grad,
        conv_bias_grad,
        xproj_grad,
        dt_weight_grad,
        dt_bias_grad,
        a_log_grad,
        skip_grad,
        out_weight_grad,
        moe_gain_grad,
        router_grad,
        up_grad.astype(f32),
        down_grad.astype(f32),
    )


def solution(mesh):
    in_specs = (
        P(("seq", "chan"), None),
        P(("seq", "chan"), None),
        P(),
        P(),
        P(None, None, "chan"),
        P(None, "chan"),
        P("chan"),
        P("chan", None),
        P(None, "chan"),
        P("chan"),
        P("chan", None),
        P("chan"),
        P("chan", None),
        P(),
        P(),
        P("chan", "seq", None),
        P("chan", "seq", None),
        P(("seq", "chan"), None),
    )
    out_specs = (
        P(("seq", "chan"), None),
        P(("seq", "chan"), None),
        P(),
        P(None, None, "chan"),
        P(None, "chan"),
        P("chan"),
        P("chan", None),
        P(None, "chan"),
        P("chan"),
        P("chan", None),
        P("chan"),
        P("chan", None),
        P(),
        P(),
        P("chan", "seq", None),
        P("chan", "seq", None),
    )
    return jax.shard_map(
        on_device, mesh=mesh, in_specs=in_specs, out_specs=out_specs, check_vma=False
    )
```

```python
from functools import partial

import jax
import jax.numpy as jnp
from jax import lax
from jax.experimental import pallas as pl
from jax.experimental.pallas import tpu as pltpu
from jax.sharding import PartitionSpec as P

STATE = 16
CONV = 4
DT_RANK = 72
EXPERTS = 8
SINK = 8
CHUNKS = 8
LANES = 128
VMEM_LIMIT = 56 * 1024 * 1024

EPS = 1e-05
HIGH = lax.Precision.HIGHEST
LOG2E = 1.4426950408889634
LN2 = 0.6931471805599453
BREAK = 1e30
MESH = pl.DeviceIdType.MESH
GELU_SCALE = 0.7978845608028654
GELU_CUBE = 0.044715


def passed_along(value, axis, steps):
    count = lax.axis_size(axis)
    leading, last = (max(0, -steps), min(count, count - steps))
    return lax.ppermute(value, axis, [(source, source + steps) for source in range(leading, last)])


def swapped(value, axis, bit):
    count = lax.axis_size(axis)
    return lax.ppermute(value, axis, [(source, source ^ bit) for source in range(count)])


def chan_rows(values):
    if lax.axis_size("chan") != 2:
        return lax.all_gather(values, "chan", axis=0, tiled=True)
    first = lax.axis_index("chan") == 0
    other = swapped(values, "chan", 1)
    return jnp.concatenate([jnp.where(first, values, other), jnp.where(first, other, values)], 0)


def chan_sums(term_fn, operand):
    count, place = lax.axis_size("chan"), lax.axis_index("chan")
    rows = operand.shape[0] // count
    if count != 2:
        return lax.psum_scatter(term_fn(operand), "chan", scatter_dimension=0, tiled=True)
    theirs = term_fn(lax.dynamic_slice_in_dim(operand, (1 - place) * rows, rows, 0))
    arrived = swapped(theirs.astype(jnp.bfloat16), "chan", 1)
    return term_fn(lax.dynamic_slice_in_dim(operand, place * rows, rows, 0)) + arrived.astype(
        jnp.float32
    )


def proj_total(values):
    if lax.axis_size("chan") != 2:
        return lax.psum(values, "chan")
    return values + swapped(values, "chan", 1)


def expert_groups():
    own = EXPERTS // lax.axis_size("chan")
    return own, lax.axis_size("seq") // own


def across_experts(values, axis, wait=None):
    own, share = expert_groups()
    place = lax.div(lax.axis_index("seq"), share)
    out = values
    for d in range(1, own):
        peer = lax.bitwise_xor(place, d)
        came = swapped(lax.dynamic_slice_in_dim(values, peer, 1, axis), "seq", d * share)
        if wait is not None:
            came = after(came, wait)
        out = lax.dynamic_update_slice_in_dim(out, came, peer, axis)
    return out


def to_owners(grad):
    own, share = expert_groups()
    if own == 1:
        return grad
    groups = [[k * share + q for k in range(own)] for q in range(share)]
    return lax.all_to_all(
        grad, "seq", split_axis=0, concat_axis=0, tiled=True, axis_index_groups=groups
    )


def expert_rows_early(packed):
    own, share = expert_groups()
    count = lax.axis_size("chan")
    slots, width = packed.shape[1:]
    if count == 2:
        place = lax.axis_index("chan")
        halves = packed.reshape(2, own, slots, width)
        kept = lax.dynamic_index_in_dim(halves, place, 0, False)
        came = swapped(lax.dynamic_index_in_dim(halves, 1 - place, 0, False), "chan", 1)
        first = place == 0
        arrived = jnp.stack([jnp.where(first, kept, came), jnp.where(first, came, kept)])
    else:
        arrived = lax.all_to_all(packed, "chan", split_axis=0, concat_axis=0, tiled=True)
        arrived = arrived.reshape(count, own, slots, width)
    return across_experts(arrived, 1).reshape(count * own, slots, width)


def expert_rows(ident, *arrays):
    return exchange(ident, arrays)


def whole_expert(weight, start, wait):
    own, share = expert_groups()
    features, hidden = weight.shape[1:]
    if start is not None:
        weight = after(weight, start)
    mine = across_experts(weight, 0, wait)
    groups = [[k * share + q for q in range(share)] for k in range(own)]
    return lax.all_gather(mine, "seq", axis_index_groups=groups)


def halved(grad, stage):
    own, share = expert_groups()
    bit = 1 << stage
    pairs = grad.reshape(own, grad.shape[1] // 2, 2, *grad.shape[2:])
    side = lax.rem(lax.div(lax.axis_index("seq"), bit), 2)
    sent = lax.dynamic_index_in_dim(pairs, 1 - side, 2, False)
    kept = lax.dynamic_index_in_dim(pairs, side, 2, False)
    came = swapped(sent, "seq", bit)
    return added(kept, came)


def added(kept, came):
    return (kept.astype(jnp.float32) + came.astype(jnp.float32)).astype(kept.dtype)


def after(value, *others):
    return lax.optimization_barrier((value,) + others)[0]


def opposite(place, bit):
    return place + bit - 2 * bit * lax.rem(lax.div(place, bit), 2)


def greet(targets):
    barrier = pltpu.get_barrier_semaphore()
    for target in targets:
        pl.semaphore_signal(barrier, inc=1, device_id=target, device_id_type=MESH)
    pl.semaphore_wait(barrier, len(targets))


def exchange_kernel(own, share, chans, count, *refs):
    sources, results = refs[:count], refs[count : 2 * count]
    send_sem, recv_sem, own_sem = refs[2 * count :]
    seq, chan = lax.axis_index("seq"), lax.axis_index("chan")
    column = lax.rem(seq, share)
    me = chan * own + lax.div(seq, share)
    total = own * chans
    peers = [lax.rem(me + d, total) for d in range(1, total)]
    targets = [(lax.rem(peer, own) * share + column, lax.div(peer, own)) for peer in peers]
    greet(targets)
    copies = []
    for k in range(count):
        for d in range(total - 1):
            copies.append(
                pltpu.make_async_remote_copy(
                    src_ref=sources[k].at[peers[d]],
                    dst_ref=results[k].at[me],
                    send_sem=send_sem.at[k, d],
                    recv_sem=recv_sem.at[k, d],
                    device_id=targets[d],
                    device_id_type=MESH,
                )
            )
        copies.append(pltpu.make_async_copy(sources[k].at[me], results[k].at[me], own_sem.at[k]))
    for copy in copies:
        copy.start()
    for copy in copies:
        copy.wait()


def exchange(ident, arrays):
    own, share = expert_groups()
    chans, count = lax.axis_size("chan"), len(arrays)
    anywhere = pl.BlockSpec(memory_space=pl.ANY)
    others = own * chans - 1
    return pl.pallas_call(
        partial(exchange_kernel, own, share, chans, count),
        in_specs=[anywhere] * count,
        out_specs=[anywhere] * count,
        out_shape=[jax.ShapeDtypeStruct(part.shape, part.dtype) for part in arrays],
        scratch_shapes=[
            pltpu.SemaphoreType.DMA((count, others)),
            pltpu.SemaphoreType.DMA((count, others)),
            pltpu.SemaphoreType.DMA((count,)),
        ],
        compiler_params=pltpu.CompilerParams(collective_id=ident, has_side_effects=True),
        name="expert_rows",
    )(*arrays)


def gather_kernel(devices, chans, own_ref, every_ref, send_sem, recv_sem):
    me = lax.axis_index("seq") * chans + lax.axis_index("chan")
    barrier = pltpu.get_barrier_semaphore()

    def target(d):
        peer = lax.rem(me + d, devices)
        return (lax.div(peer, chans), lax.rem(peer, chans))

    def copy(d):
        return pltpu.make_async_remote_copy(
            src_ref=own_ref,
            dst_ref=every_ref.at[me],
            send_sem=send_sem.at[d - 1],
            recv_sem=recv_sem.at[d - 1],
            device_id=target(d),
            device_id_type=MESH,
        )

    def signal(d, carry):
        pl.semaphore_signal(barrier, inc=1, device_id=target(d), device_id_type=MESH)
        return carry

    def start(d, carry):
        copy(d).start()
        return carry

    def finish(d, carry):
        copy(d).wait()
        return carry

    lax.fori_loop(1, devices, signal, 0)
    every_ref[me] = own_ref[...]
    pl.semaphore_wait(barrier, devices - 1)
    lax.fori_loop(1, devices, start, 0)
    lax.fori_loop(1, devices, finish, 0)


def gathered_everywhere(values):
    chans = lax.axis_size("chan")
    devices = lax.axis_size("seq") * chans
    return pl.pallas_call(
        partial(gather_kernel, devices, chans),
        in_specs=[pl.BlockSpec(memory_space=pltpu.VMEM)],
        out_specs=pl.BlockSpec(memory_space=pltpu.VMEM),
        out_shape=jax.ShapeDtypeStruct((devices,) + values.shape, values.dtype),
        scratch_shapes=[
            pltpu.SemaphoreType.DMA((devices - 1,)),
            pltpu.SemaphoreType.DMA((devices - 1,)),
        ],
        compiler_params=pltpu.CompilerParams(
            collective_id=3, has_side_effects=True, vmem_limit_bytes=VMEM_LIMIT
        ),
        name="gather_small",
    )(values)


def carry_kernel(
    count, reverse, total_ref, rate_ref, entry_ref, ends_out, ends_in, sums_out, sums_in, ends_sems, sums_sems
):
    me = lax.axis_index("seq")
    bits = [1 << k for k in range(count.bit_length() - 1)]
    greet([{"seq": opposite(me, bit)} for bit in bits])
    rates = rate_ref[...]
    ends, sums = total_ref[:STATE], total_ref[STATE : STATE + 1]
    before, before_sum = jnp.zeros_like(ends), jnp.zeros_like(sums)
    for k, bit in enumerate(bits):
        ends_out[k] = ends.astype(ends_out.dtype)
        sums_out[k] = sums
        copies = [
            pltpu.make_async_remote_copy(
                src_ref=out.at[k],
                dst_ref=into.at[k],
                send_sem=sems.at[0, k],
                recv_sem=sems.at[1, k],
                device_id={"seq": opposite(me, bit)},
                device_id_type=MESH,
            )
            for out, into, sems in ((ends_out, ends_in, ends_sems), (sums_out, sums_in, sums_sems))
        ]
        for copy in copies:
            copy.start()
        for copy in copies:
            copy.wait()
        their_ends, their_sums = ends_in[k].astype(jnp.float32), sums_in[k]
        theirs_first = lax.rem(lax.div(me, bit), 2) == (0 if reverse else 1)
        before = jnp.where(theirs_first, jnp.exp2(rates * before_sum) * their_ends + before, before)
        before_sum = jnp.where(theirs_first, before_sum + their_sums, before_sum)
        ends = jnp.where(
            theirs_first,
            jnp.exp2(rates * sums) * their_ends + ends,
            jnp.exp2(rates * their_sums) * ends + their_ends,
        )
        sums = sums + their_sums
    entry_ref[...] = before


def carried(total, rates, reverse):
    count = lax.axis_size("seq")
    rounds = count.bit_length() - 1
    channels = rates.shape[1]
    vmem = pl.BlockSpec(memory_space=pltpu.VMEM)
    return pl.pallas_call(
        partial(carry_kernel, count, reverse),
        in_specs=[vmem, vmem],
        out_specs=vmem,
        out_shape=jax.ShapeDtypeStruct(rates.shape, jnp.float32),
        scratch_shapes=[
            pltpu.VMEM((rounds, STATE, channels), jnp.bfloat16),
            pltpu.VMEM((rounds, STATE, channels), jnp.bfloat16),
            pltpu.VMEM((rounds, 1, channels), jnp.float32),
            pltpu.VMEM((rounds, 1, channels), jnp.float32),
            pltpu.SemaphoreType.DMA((2, rounds)),
            pltpu.SemaphoreType.DMA((2, rounds)),
        ],
        compiler_params=pltpu.CompilerParams(
            collective_id=5 if reverse else 4, has_side_effects=True, vmem_limit_bytes=VMEM_LIMIT
        ),
        name="carry_back" if reverse else "carry",
    )(total, rates)


class Halving:
    def __init__(self, count, held, incoming, result, send_sem, recv_sem):
        self.held, self.incoming, self.result = held, incoming, result
        self.send_sem, self.recv_sem = send_sem, recv_sem
        self.chunks, self.rows = held.shape[0], held.shape[1]
        me = lax.axis_index("seq")
        bits = [1 << k for k in range(count.bit_length() - 1)]
        self.rounds = len(bits)
        self.peers = [{"seq": opposite(me, bit)} for bit in bits]
        self.sides = [lax.rem(lax.div(me, bit), 2) for bit in bits]
        self.lows, self.lengths = [0], [self.rows]
        for side in self.sides:
            self.lengths.append(self.lengths[-1] // 2)
            self.lows.append(self.lows[-1] + side * self.lengths[-1])
        self.turns = 4 * self.rounds + self.chunks - 1

    def greet(self):
        barrier = pltpu.get_barrier_semaphore()
        for peer in self.peers:
            pl.semaphore_signal(barrier, inc=1, device_id=peer, device_id_type=MESH)

    def greeted(self):
        pl.semaphore_wait(pltpu.get_barrier_semaphore(), self.rounds)

    def span(self, k, other=False):
        low = self.lows[k]
        if other:
            low = self.lows[k - 1] + (1 - self.sides[k - 1]) * self.lengths[k]
        return pl.ds(pl.multiple_of(low, 16), self.lengths[k])

    def landing(self, step):
        return pl.ds(self.rows - self.lengths[step], self.lengths[step + 1])

    def copy(self, c, step):
        if step < self.rounds:
            k = step
            source = self.held.at[c, self.span(k + 1, True)]
            target = self.incoming.at[c, self.landing(step)]
        else:
            k = 2 * self.rounds - 1 - step
            source = target = self.result.at[c, self.span(k + 1)]
        return pltpu.make_async_remote_copy(
            src_ref=source,
            dst_ref=target,
            send_sem=self.send_sem.at[c, step],
            recv_sem=self.recv_sem.at[c, step],
            device_id=self.peers[k],
            device_id_type=MESH,
        )

    def start(self):
        self.copy(0, 0).start()

    def turn(self, turn):
        if turn + 1 < self.chunks:
            self.copy(turn + 1, 0).start()
        for c in range(self.chunks):
            step, odd = divmod(turn - c - 1, 2)
            if odd or not 0 <= step < 2 * self.rounds:
                continue
            self.copy(c, step).wait()
            if step < self.rounds:
                kept = self.span(step + 1)
                total = self.held[c, kept].astype(jnp.float32)
                total = total + self.incoming[c, self.landing(step)].astype(jnp.float32)
                target = self.held if step < self.rounds - 1 else self.result
                target[c, kept] = total.astype(target.dtype)
            if step < 2 * self.rounds - 1:
                self.copy(c, step + 1).start()


def sum_scratch(chunks, rows, width, count):
    steps = 2 * (count.bit_length() - 1)
    return [
        pltpu.VMEM((chunks, rows, width), jnp.bfloat16),
        pltpu.VMEM((chunks, rows, width), jnp.bfloat16),
        pltpu.SemaphoreType.DMA((chunks, steps)),
        pltpu.SemaphoreType.DMA((chunks, steps)),
    ]


def sum_kernel(count, places, sizes, *refs):
    parts, sum_ref = refs[: len(places)], refs[len(places)]
    held, incoming, send_sem, recv_sem = refs[len(places) + 1 :]
    halving = Halving(count, held, incoming, sum_ref, send_sem, recv_sem)
    rows = halving.rows
    halving.greet()
    used = max(place + size for place, size in zip(places, sizes))
    for c in range(halving.chunks):
        for part, place, size in zip(parts, places, sizes):
            low, high = max(place, c * rows), min(place + size, (c + 1) * rows)
            if low < high:
                held[c, low - c * rows : high - c * rows] = part[low - place : high - place].astype(held.dtype)
        if used < (c + 1) * rows:
            low = max(used - c * rows, 0)
            held[c, low:] = jnp.zeros((rows - low, held.shape[2]), held.dtype)
    halving.greeted()
    halving.start()
    for turn in range(halving.turns):
        halving.turn(turn)


def summed(parts):
    count = lax.axis_size("seq")
    width = parts[0].shape[1]
    sizes = [part.shape[0] for part in parts]
    places, used = [], 0
    for size in sizes:
        places.append(used)
        used += -(-size // 16) * 16
    chunk = 16 * count
    chunks = -(-used // chunk)
    vmem = pl.BlockSpec(memory_space=pltpu.VMEM)
    padded = [jnp.pad(part, ((0, -part.shape[0] % 16), (0, 0))) for part in parts]
    total = pl.pallas_call(
        partial(sum_kernel, count, places, [part.shape[0] for part in padded]),
        in_specs=[vmem] * len(parts),
        out_specs=vmem,
        out_shape=jax.ShapeDtypeStruct((chunks, chunk, width), jnp.bfloat16),
        scratch_shapes=sum_scratch(chunks, chunk, width, count),
        compiler_params=pltpu.CompilerParams(
            collective_id=6, has_side_effects=True, vmem_limit_bytes=VMEM_LIMIT
        ),
        name="sum_late",
    )(*padded).reshape(chunks * chunk, width)
    return [total[place : place + size].astype(jnp.float32) for place, size in zip(places, sizes)]


def to_steps(values):
    rows = values.shape[0]
    parts = values.reshape((CHUNKS, rows // CHUNKS) + values.shape[1:])
    return jnp.swapaxes(parts, 0, 1).reshape(values.shape)


def from_steps(values):
    rows = values.shape[0]
    parts = values.reshape((rows // CHUNKS, CHUNKS) + values.shape[1:])
    return jnp.swapaxes(parts, 0, 1).reshape(values.shape)


def stacked(*parts):
    rows = sum(part.shape[0] for part in parts)
    whole = jnp.concatenate([part.astype(jnp.bfloat16) for part in parts], 0)
    return jnp.pad(whole, ((0, -rows % 16), (0, 0)))


def unstacked(whole, parts):
    out, first = [], 0
    for part in parts:
        out.append(whole[first : first + part.shape[0]].astype(jnp.float32))
        first += part.shape[0]
    return out


def norm_apply(values, gain):
    return values * lax.rsqrt(jnp.mean(values * values, -1, keepdims=True) + EPS) * gain


def silu_grad(values):
    sigma = jax.nn.sigmoid(values)
    return sigma * (1.0 + values * (1.0 - sigma))


def spread(target, source):
    for n in range(STATE):
        target[n] = jnp.broadcast_to(source[:, n : n + 1], target.shape[1:])


def full(row):
    return jnp.broadcast_to(row, (CHUNKS, LANES))


def shifted(values, by, down):
    sub = lax.broadcasted_iota(jnp.int32, (CHUNKS, LANES), 0)
    if down:
        return jnp.where(sub >= by, pltpu.roll(values, by, 0), 0.0)
    return jnp.where(sub < CHUNKS - by, pltpu.roll(values, CHUNKS - by, 0), 0.0)


def chunk_windows(sums, down):
    windows = []
    for by in (1, 2, 4):
        windows.append(sums)
        sums = sums + shifted(sums, by, down)
    return windows, sums


def chunk_prefix(ends, windows, rate, down):
    for by, window in zip((1, 2, 4), windows):
        ends = ends + jnp.exp2(rate * window) * shifted(ends, by, down)
    return ends


def ends_kernel(halves, reverse, step_ref, drive_ref, break_ref, map_ref, rate_ref, part_ref, sum_ref, tot_ref, wide):
    rows = step_ref.shape[0]
    steps = rows // (halves * CHUNKS)

    @pl.when(pl.program_id(0) == 0)
    def _():
        spread(wide, map_ref)

    rates = [full(rate_ref[n : n + 1, :]) for n in range(STATE)]
    zero = jnp.zeros((CHUNKS, LANES), jnp.float32)

    def half(turn, carry):
        h = halves - 1 - turn if reverse else turn
        before_sum, before = carry[0], carry[1:]

        def body(k, state):
            s = steps - 1 - k if reverse else k
            at = pl.ds(pl.multiple_of((h * steps + s) * CHUNKS, CHUNKS), CHUNKS)
            step = step_ref[at, :]
            decay_step = step + break_ref[at, :]
            drive = drive_ref[at, :]
            if not reverse:
                drive = drive * step
            new = [state[0] + decay_step]
            for n in range(STATE):
                decay = jnp.exp2(decay_step * rates[n])
                if reverse:
                    new.append(decay * (state[n + 1] + drive * wide[n, at, :]))
                else:
                    new.append(decay * state[n + 1] + drive * wide[n, at, :])
            return tuple(new)

        out = lax.fori_loop(0, steps, body, (zero,) * (STATE + 1), unroll=10)
        windows, sums = chunk_windows(out[0], not reverse)
        prior = shifted(sums, 1, not reverse)
        last = slice(0, 1) if reverse else slice(CHUNKS - 1, CHUNKS)
        sum_ref[h] = prior + before_sum
        new = [before_sum + full(sums[last])]
        for n in range(STATE):
            joined = chunk_prefix(out[n + 1], windows, rates[n], not reverse)
            part_ref[h, n] = shifted(joined, 1, not reverse) + jnp.exp2(rates[n] * prior) * before[n]
            new.append(full(joined[last]) + jnp.exp2(rates[n] * full(sums[last])) * before[n])
        return tuple(new)

    total = lax.fori_loop(0, halves, half, (zero,) * (STATE + 1))
    for n in range(STATE):
        tot_ref[n : n + 1, :] = total[n + 1][0:1]
    tot_ref[STATE:, :] = total[0]


def outputs_kernel(
    halves, step_ref, mixed_ref, break_ref, b_ref, c_ref, rate_ref, part_ref, sum_ref, device,
    skip_ref, gate_ref, scan_ref, gated_ref, entry_ref, b_wide, c_wide,
):
    rows = step_ref.shape[0]
    steps = rows // (halves * CHUNKS)

    @pl.when(pl.program_id(0) == 0)
    def _():
        spread(b_wide, b_ref)
        spread(c_wide, c_ref)

    rates = [full(rate_ref[n : n + 1, :]) for n in range(STATE)]

    def half(h, carry):
        state = []
        for n in range(STATE):
            state.append(
                part_ref[h, n] + jnp.exp2(rates[n] * sum_ref[h]) * full(device[n : n + 1, :])
            )
            entry_ref[h, n] = state[n]

        def body(s, state):
            at = pl.ds(pl.multiple_of((h * steps + s) * CHUNKS, CHUNKS), CHUNKS)
            step = step_ref[at, :]
            decay_step = step + break_ref[at, :]
            drive = mixed_ref[at, :] * step
            total = None
            new = []
            for n in range(STATE):
                value = jnp.exp2(decay_step * rates[n]) * state[n] + drive * b_wide[n, at, :]
                term = value * c_wide[n, at, :]
                total = term if total is None else total + term
                new.append(value)
            scan_ref[at, :] = total
            return tuple(new)

        lax.fori_loop(0, steps, body, tuple(state), unroll=5)
        return carry

    lax.fori_loop(0, halves, half, 0)
    gate = gate_ref[...]
    out = scan_ref[...] + skip_ref[...] * mixed_ref[...]
    scan_ref[...] = out
    gated_ref[...] = (out * (gate * jax.nn.sigmoid(gate))).astype(gated_ref.dtype)


def early_fills(first, second, held, own_sem):
    rows, copies, place = held.shape[1], [], 0
    for part in (first, second):
        done = 0
        while done < part.shape[0]:
            c, low = (place + done) // rows, (place + done) % rows
            length = min(rows - low, part.shape[0] - done)
            copies.append(
                pltpu.make_async_copy(
                    part.at[pl.ds(done, length)], held.at[c, pl.ds(low, length)], own_sem.at[len(copies)]
                )
            )
            done += length
        place += part.shape[0]
    return copies


def grads_kernel(
    halves, count, groups, step_ref, mixed_ref, break_ref, grad_ref, b_ref, c_ref, rate_ref, entry_ref,
    part_ref, sum_ref, device, first_early, second_early, step_out, mixed_out, b_out, c_out, rate_out, early_out,
    b_wide, c_wide, b_sum, c_sum, decays, states, held, incoming, summed_early, send_sem, recv_sem, own_sem,
):
    rows = step_ref.shape[0]
    steps = rows // (halves * CHUNKS)
    group = pl.program_id(0)
    block = STATE // 2
    halving = Halving(count, held, incoming, summed_early, send_sem, recv_sem)
    slots = [[] for _ in range(2 * groups)]
    for turn in range(halving.turns):
        slots[turn * 2 * groups // halving.turns].append(turn)

    @pl.when(group == 0)
    def _():
        halving.greet()
        fills = early_fills(first_early, second_early, held, own_sem)
        for fill in fills:
            fill.start()
        for fill in fills:
            fill.wait()
        halving.greeted()
        halving.start()
        spread(b_wide, b_ref)
        spread(c_wide, c_ref)
        b_sum[...] = jnp.zeros_like(b_sum)
        c_sum[...] = jnp.zeros_like(c_sum)

    zero = jnp.zeros((CHUNKS, LANES), jnp.float32)

    for first in (0, block):
        rates = [full(rate_ref[first + n : first + n + 1, :]) for n in range(block)]

        def half(h, rate_sums):
            entry = []
            for n in range(block):
                entry.append(entry_ref[h, first + n])
                states[0, n] = entry[n]

            def ahead(s, state):
                at = pl.ds(pl.multiple_of((h * steps + s) * CHUNKS, CHUNKS), CHUNKS)
                step = step_ref[at, :]
                decay_step = step + break_ref[at, :]
                drive = mixed_ref[at, :] * step
                new = []
                for n in range(block):
                    decay = jnp.exp2(decay_step * rates[n])
                    value = decay * state[n] + drive * b_wide[first + n, at, :]
                    decays[s, n] = decay
                    states[s + 1, n] = value
                    new.append(value)
                return tuple(new)

            lax.fori_loop(0, steps, ahead, tuple(entry), unroll=10)

            exits = [
                part_ref[h, first + n]
                + jnp.exp2(rates[n] * sum_ref[h]) * full(device[first + n : first + n + 1, :])
                for n in range(block)
            ]

            def back(k, carry):
                s = steps - 1 - k
                at = pl.ds(pl.multiple_of((h * steps + s) * CHUNKS, CHUNKS), CHUNKS)
                step = step_ref[at, :]
                mixed = mixed_ref[at, :]
                grad = grad_ref[at, :]
                drive = mixed * step
                by_rate, by_map = zero, zero
                flows, sums = [], []
                for n in range(block):
                    b_now, c_now = b_wide[first + n, at, :], c_wide[first + n, at, :]
                    here = carry[n] + c_now * grad
                    flow = decays[s, n] * here
                    log_grad = flow * states[s, n]
                    by_rate = by_rate + rates[n] * log_grad
                    by_map = by_map + b_now * here
                    b_sum[first + n, at, :] += drive * here
                    c_sum[first + n, at, :] += grad * states[s + 1, n]
                    flows.append(flow)
                    sums.append(carry[block + n] + step * log_grad)
                by_rate = by_rate * LN2 + mixed * by_map
                by_map = step * by_map
                if first == 0:
                    step_out[at, :] = by_rate
                    mixed_out[at, :] = by_map
                else:
                    step_out[at, :] += by_rate
                    mixed_out[at, :] += by_map
                return tuple(flows + sums)

            out = lax.fori_loop(0, steps, back, tuple(exits) + rate_sums, unroll=5)
            return out[block:]

        rate_sums = lax.fori_loop(0, halves, half, (zero,) * block)
        for n in range(block):
            rate_out[first + n : first + n + 1, :] = jnp.sum(rate_sums[n], 0, keepdims=True)

        for g in range(groups):
            turns = slots[2 * g + first // block]
            if turns:

                @pl.when(group == g)
                def _(turns=turns):
                    for turn in turns:
                        halving.turn(turn)

    @pl.when(group == groups - 1)
    def _():
        result = pltpu.make_async_copy(summed_early, early_out, own_sem.at[0])
        result.start()
        result.wait()
        for n in range(STATE):
            b_out[:, n : n + 1] = jnp.sum(b_sum[n], -1, keepdims=True)
            c_out[:, n : n + 1] = jnp.sum(c_sum[n], -1, keepdims=True)


class Scan:
    def __init__(self, rows, channels, halves):
        self.rows, self.channels, self.halves = rows, channels, halves
        self.groups = channels // LANES
        row_spec = pl.BlockSpec((rows, LANES), lambda g: (0, g))
        fixed = lambda *shape: pl.BlockSpec(shape, lambda g: (0,) * len(shape))
        self.row_spec = row_spec
        self.break_spec = fixed(rows, LANES)
        self.map_spec = fixed(rows, STATE)
        self.rate_spec = pl.BlockSpec((STATE, LANES), lambda g: (0, g))
        self.part_spec = pl.BlockSpec((halves, STATE, CHUNKS, LANES), lambda g: (0, 0, 0, g))
        self.sum_spec = pl.BlockSpec((halves, CHUNKS, LANES), lambda g: (0, 0, g))
        self.tot_spec = pl.BlockSpec((STATE + CHUNKS, LANES), lambda g: (0, g))
        self.skip_spec = pl.BlockSpec((1, LANES), lambda g: (0, g))
        self.row_f32 = jax.ShapeDtypeStruct((rows, channels), jnp.float32)
        self.part_f32 = jax.ShapeDtypeStruct((halves, STATE, CHUNKS, channels), jnp.float32)
        self.sum_f32 = jax.ShapeDtypeStruct((halves, CHUNKS, channels), jnp.float32)
        self.tot_f32 = jax.ShapeDtypeStruct((STATE + CHUNKS, channels), jnp.float32)
        self.wide = pltpu.VMEM((STATE, rows, LANES), jnp.float32)

    def params(self):
        return pltpu.CompilerParams(
            dimension_semantics=("arbitrary",), vmem_limit_bytes=VMEM_LIMIT
        )

    def cost(self, per_element):
        count = self.rows * self.channels * STATE
        return pl.CostEstimate(
            flops=per_element * count, bytes_accessed=12 * self.rows * self.channels, transcendentals=count
        )

    def ends(self, reverse, step, drive, breaks, maps, rates):
        return pl.pallas_call(
            partial(ends_kernel, self.halves, reverse),
            grid=(self.groups,),
            in_specs=[self.row_spec, self.row_spec, self.break_spec, self.map_spec, self.rate_spec],
            out_specs=[self.part_spec, self.sum_spec, self.tot_spec],
            out_shape=[self.part_f32, self.sum_f32, self.tot_f32],
            scratch_shapes=[self.wide],
            compiler_params=self.params(),
            cost_estimate=self.cost(5),
            name="scan_ends_back" if reverse else "scan_ends",
        )(step, drive, breaks, maps, rates)

    def outputs(self, step, mixed, breaks, b_in, c_out, rates, part, sums, device, skip, gate):
        return pl.pallas_call(
            partial(outputs_kernel, self.halves),
            grid=(self.groups,),
            in_specs=[
                self.row_spec, self.row_spec, self.break_spec, self.map_spec, self.map_spec, self.rate_spec,
                self.part_spec, self.sum_spec, self.rate_spec, self.skip_spec, self.row_spec,
            ],
            out_specs=[self.row_spec, self.row_spec, self.part_spec],
            out_shape=[
                self.row_f32,
                jax.ShapeDtypeStruct((self.rows, self.channels), jnp.bfloat16),
                self.part_f32,
            ],
            scratch_shapes=[self.wide, self.wide],
            compiler_params=self.params(),
            cost_estimate=self.cost(7),
            name="scan_outputs",
        )(step, mixed, breaks, b_in, c_out, rates, part, sums, device, skip, gate)

    def grads(self, step, mixed, breaks, grad, b_in, c_out, rates, entry, part, sums, device, early):
        count = lax.axis_size("seq")
        width, total = early[0].shape[1], early[0].shape[0] + early[1].shape[0]
        chunk = 16 * count
        total = -(-total // chunk) * chunk
        early = (early[0], jnp.pad(early[1], ((0, total - early[0].shape[0] - early[1].shape[0]), (0, 0))))
        chunks = total // chunk
        anywhere = pl.BlockSpec(memory_space=pl.ANY)
        steps = self.rows // (self.halves * CHUNKS)
        block = STATE // 2
        return pl.pallas_call(
            partial(grads_kernel, self.halves, count, self.groups),
            grid=(self.groups,),
            in_specs=[
                self.row_spec, self.row_spec, self.break_spec, self.row_spec, self.map_spec, self.map_spec,
                self.rate_spec, self.part_spec, self.part_spec, self.sum_spec, self.rate_spec, anywhere, anywhere,
            ],
            out_specs=[self.row_spec, self.row_spec, self.map_spec, self.map_spec, self.rate_spec, anywhere],
            out_shape=[
                self.row_f32,
                self.row_f32,
                jax.ShapeDtypeStruct((self.rows, STATE), jnp.float32),
                jax.ShapeDtypeStruct((self.rows, STATE), jnp.float32),
                jax.ShapeDtypeStruct((STATE, self.channels), jnp.float32),
                jax.ShapeDtypeStruct((chunks, chunk, width), jnp.bfloat16),
            ],
            scratch_shapes=[
                self.wide, self.wide, self.wide, self.wide,
                pltpu.VMEM((steps, block, CHUNKS, LANES), jnp.float32),
                pltpu.VMEM((steps + 1, block, CHUNKS, LANES), jnp.float32),
                pltpu.VMEM((chunks, chunk, width), jnp.bfloat16),
                *sum_scratch(chunks, chunk, width, count)[1:2],
                pltpu.VMEM((chunks, chunk, width), jnp.bfloat16),
                *sum_scratch(chunks, chunk, width, count)[2:],
                pltpu.SemaphoreType.DMA((chunks + 2,)),
            ],
            compiler_params=pltpu.CompilerParams(
                dimension_semantics=("arbitrary",), vmem_limit_bytes=VMEM_LIMIT, collective_id=7,
                has_side_effects=True,
            ),
            cost_estimate=self.cost(20),
            name="scan_grads",
        )(step, mixed, breaks, grad, b_in, c_out, rates, entry, part, sums, device, *early)


def over_tokens(values):
    return jnp.sum(jnp.sum(values, 0), -1, keepdims=True)


def sinkhorn_kernel(place_ref, logit_ref, route_ref, gate_ref, scaled_ref, row_ref, column_ref):
    probs = jnp.exp(logit_ref[...])
    for sweep in range(SINK):
        column = over_tokens(probs)
        scaled = probs / column[None]
        row = jnp.sum(scaled, 1, keepdims=True)
        scaled_ref[sweep] = scaled
        row_ref[sweep] = row
        column_ref[sweep] = jnp.broadcast_to(column, column_ref.shape[1:])
        probs = scaled / row
    place = place_ref[0]
    own = scaled_ref[SINK - 1, place] / row_ref[SINK - 1, place]
    ids = lax.broadcasted_iota(jnp.int32, own.shape, 0)
    gate_ref[...] = EXPERTS * jnp.sum(jnp.where(ids == route_ref[...], own, 0.0), 0, keepdims=True)


def sinkhorn_back_kernel(place_ref, logit_ref, scaled_ref, row_ref, column_ref, grad_ref, out_ref, held):
    grad = grad_ref[...]
    for sweep in reversed(range(SINK)):
        scaled, row = scaled_ref[sweep], row_ref[sweep]
        inner = jnp.sum(grad * (scaled / row), 1, keepdims=True)
        grad = (grad - inner) / row
        along = over_tokens(grad * scaled)
        grad = (grad - along[None]) / column_ref[sweep][:, 0:1][None]
    held[...] = grad
    place = place_ref[0]
    out_ref[...] = held[place] * jnp.exp(logit_ref[place])


def in_vmem(count):
    return [pl.BlockSpec(memory_space=pltpu.SMEM)] + [pl.BlockSpec(memory_space=pltpu.VMEM)] * count


def sinkhorn(place, logits, routes):
    devices, experts, tokens = logits.shape
    f32 = lambda *shape: jax.ShapeDtypeStruct(shape, jnp.float32)
    return pl.pallas_call(
        sinkhorn_kernel,
        in_specs=in_vmem(2),
        out_specs=in_vmem(4)[1:],
        out_shape=[
            f32(1, tokens),
            f32(SINK, devices, experts, tokens),
            f32(SINK, devices, 1, tokens),
            f32(SINK, experts, LANES),
        ],
        compiler_params=pltpu.CompilerParams(vmem_limit_bytes=VMEM_LIMIT),
        name="sinkhorn",
    )(place, logits, routes)


def sinkhorn_back(place, logits, scaled, rows, columns, grad):
    devices, experts, tokens = logits.shape
    return pl.pallas_call(
        sinkhorn_back_kernel,
        in_specs=in_vmem(5),
        out_specs=in_vmem(1)[1],
        out_shape=jax.ShapeDtypeStruct((experts, tokens), jnp.float32),
        scratch_shapes=[pltpu.VMEM(logits.shape, jnp.float32)],
        compiler_params=pltpu.CompilerParams(vmem_limit_bytes=VMEM_LIMIT),
        name="sinkhorn_back",
    )(place, logits, scaled, rows, columns, grad)


def expert_kernel(
    side_ref, rows_ref, grad_ref, gate_ref, up_ref, down_ref, out_ref, back_ref, up_kept, up_sent, down_kept,
    down_sent, rows_t, grad_t, out_sum, back_sum, whole,
):
    step = pl.program_id(0)
    features = up_kept.shape[1]

    @pl.when(step == 0)
    def _():
        rows_t[...] = rows_ref[...].T
        grad_t[...] = (grad_ref[...].astype(jnp.float32) * gate_ref[...]).astype(jnp.bfloat16).T

    def parted(total, kept, sent):
        whole[...] = total
        first = side_ref[0] == 0
        for k in range(kept.shape[0]):
            low = whole[2 * k * features : (2 * k + 1) * features]
            high = whole[(2 * k + 1) * features : (2 * k + 2) * features]
            kept[k] = jnp.where(first, low, high).astype(kept.dtype)
            sent[k] = jnp.where(first, high, low).astype(sent.dtype)

    def dot(a, b, over=((1,), (0,))):
        return lax.dot_general(a, b, (over, ((), ())), preferred_element_type=jnp.float32)

    def joined(ref):
        for q in range(ref.shape[0]):
            for j in range(ref.shape[1]):
                first = (j * ref.shape[0] + q) * features
                whole[first : first + features] = ref[q, j].astype(jnp.float32)
        return whole[...].astype(jnp.bfloat16)

    across = ((1,), (1,))
    up, down = joined(up_ref), joined(down_ref)
    pre = dot(rows_ref[...], up)
    square = pre * pre
    bend = jnp.tanh(GELU_SCALE * (pre + GELU_CUBE * pre * square))
    half = 0.5 * (1.0 + bend)
    act = (pre * half).astype(jnp.bfloat16)
    slope = half + 0.5 * pre * (1.0 - bend * bend) * (GELU_SCALE + 3.0 * GELU_SCALE * GELU_CUBE * square)
    grad_pre = dot(grad_ref[...], down) * slope
    out_part, back_part = dot(act, down, across), dot(grad_pre.astype(jnp.bfloat16), up, across)

    @pl.when(step == 0)
    def _():
        out_sum[...] = out_part
        back_sum[...] = back_part

    @pl.when(step > 0)
    def _():
        out_sum[...] += out_part
        back_sum[...] += back_part

    parted(dot(grad_t[...], act), down_kept, down_sent)
    parted(dot(rows_t[...], (grad_pre * gate_ref[...]).astype(jnp.bfloat16)), up_kept, up_sent)

    @pl.when(step == pl.num_programs(0) - 1)
    def _():
        out_ref[...] = out_sum[...].astype(out_ref.dtype)
        back_ref[...] = back_sum[...].astype(back_ref.dtype)


def expert_passes(side, rows, grad, gate, up, down):
    count, width = rows.shape
    share, own, features, hidden = up.shape
    tile = 512
    blocks = width // (2 * features)
    fixed = lambda *shape: pl.BlockSpec(shape, lambda k: (0,) * len(shape))
    weight_spec = pl.BlockSpec((share, own, features, tile), lambda k: (0, 0, 0, k))
    part_spec = pl.BlockSpec((blocks, features, tile), lambda k: (0, 0, k))
    part_shape = jax.ShapeDtypeStruct((blocks, features, hidden), jnp.bfloat16)
    row_shape = jax.ShapeDtypeStruct((count, width), jnp.bfloat16)
    return pl.pallas_call(
        expert_kernel,
        grid=(hidden // tile,),
        in_specs=[
            pl.BlockSpec(memory_space=pltpu.SMEM), fixed(count, width), fixed(count, width), fixed(count, 1),
            weight_spec, weight_spec,
        ],
        out_specs=[fixed(count, width), fixed(count, width)] + [part_spec] * 4,
        out_shape=[row_shape, row_shape] + [part_shape] * 4,
        scratch_shapes=[
            pltpu.VMEM((width, count), jnp.bfloat16),
            pltpu.VMEM((width, count), jnp.bfloat16),
            pltpu.VMEM((count, width), jnp.float32),
            pltpu.VMEM((count, width), jnp.float32),
            pltpu.VMEM((width, tile), jnp.float32),
        ],
        compiler_params=pltpu.CompilerParams(
            dimension_semantics=("arbitrary",), vmem_limit_bytes=VMEM_LIMIT
        ),
        cost_estimate=pl.CostEstimate(
            flops=12 * count * width * hidden, bytes_accessed=8 * width * hidden, transcendentals=count * hidden
        ),
        name="expert_passes",
    )(side, rows, grad, gate, up, down)


def on_device(
    block_in,
    routes,
    doc_lengths,
    norm_gain,
    in_weight,
    conv_weight,
    conv_bias,
    xproj_weight,
    dt_weight,
    dt_bias,
    a_log,
    skip_gain,
    out_weight,
    moe_gain,
    router_weight,
    up_weight,
    down_weight,
    out_grad,
):
    tok_dev, model_width = block_in.shape
    chan_count = lax.axis_size("chan")
    chan_place, seq_place = lax.axis_index("chan"), lax.axis_index("seq")
    dev_ref = (seq_place * chan_count + chan_place).astype(jnp.int32).reshape(1)
    steps = tok_dev // CHUNKS
    tok_seq = tok_dev * chan_count
    channels = in_weight.shape[2]
    padded_channels = -(-channels // LANES) * LANES
    f32, bf16 = jnp.float32, jnp.bfloat16

    route_col = routes[:, 0]
    expert_ids = lax.broadcasted_iota(jnp.int32, (1, EXPERTS), 1)
    chosen = (route_col[:, None] == expert_ids).astype(bf16)
    row_ids = lax.broadcasted_iota(jnp.int32, (tok_dev, tok_dev), 0)
    col_ids = lax.broadcasted_iota(jnp.int32, (tok_dev, tok_dev), 1)
    counts = jnp.dot((col_ids <= row_ids).astype(bf16), chosen, preferred_element_type=f32)
    rank = (jnp.sum(counts * chosen.astype(f32), 1) - 1.0).astype(jnp.int32)
    capacity = tok_dev * 5 // (4 * EXPERTS) + 1
    capacity = -(-capacity // 16) * 16
    slot = to_steps(route_col * capacity + rank)
    route_steps = to_steps(route_col)
    slot_ids = lax.broadcasted_iota(jnp.int32, (1, EXPERTS * capacity), 1)
    placer = (slot[:, None] == slot_ids).astype(bf16)

    def pack(values):
        rows = jnp.einsum("ts,td->sd", placer, values, preferred_element_type=f32).astype(bf16)
        return rows.reshape(EXPERTS, capacity, model_width)

    def unpack(values):
        return jnp.einsum(
            "ts,sd->td",
            placer,
            values.reshape(EXPERTS * capacity, model_width),
            preferred_element_type=f32,
        )

    block_steps = to_steps(block_in)
    grad_steps = to_steps(out_grad)
    residual = block_steps.astype(f32)
    normed, norm_back = jax.vjp(norm_apply, residual, norm_gain)
    gathered = chan_rows(normed.astype(bf16))

    inner_b = jnp.dot(gathered, in_weight[0], preferred_element_type=f32).astype(bf16)
    gate_z = jnp.dot(gathered, in_weight[1], preferred_element_type=f32)

    shape4 = (chan_count, steps, CHUNKS)
    ids = [lax.broadcasted_iota(jnp.int32, shape4, axis) for axis in range(3)]
    position = seq_place * tok_seq + ids[0] * tok_dev + ids[2] * steps + ids[1]
    starts = jnp.cumsum(doc_lengths) - doc_lengths
    doc_first = jnp.max(
        jnp.where(starts <= position[..., None], starts, 0), axis=-1
    )
    reach = CONV - 1
    inner = inner_b.astype(f32).reshape(shape4 + (channels,))
    tails = jnp.swapaxes(inner[:, steps - reach :], 0, 1).reshape(reach, chan_count * CHUNKS, channels)
    previous = passed_along(tails[:, -1], "seq", 1)
    heads = jnp.concatenate([previous[:, None], tails[:, :-1]], 1)
    heads = jnp.swapaxes(heads.reshape(reach, chan_count, CHUNKS, channels), 0, 1)
    padded = jnp.concatenate([heads, inner], 1)
    masks = [
        (position - (reach - offset) >= doc_first).astype(f32)[..., None] for offset in range(CONV)
    ]
    conv_pre = conv_bias
    for offset in range(CONV):
        conv_pre = conv_pre + conv_weight[offset] * padded[:, offset : offset + steps] * masks[offset]
    conv_pre = conv_pre.reshape(tok_seq, channels)
    mixed_b = jax.nn.silu(conv_pre).astype(bf16)
    mixed = mixed_b.astype(f32)
    proj_all = proj_total(jnp.dot(mixed_b, xproj_weight, preferred_element_type=f32))
    low_rank = proj_all[:, :DT_RANK]
    b_in = proj_all[:, DT_RANK : DT_RANK + STATE]
    c_out = proj_all[:, DT_RANK + STATE :]
    step_pre = jnp.dot(low_rank, dt_weight, precision=HIGH) + dt_bias
    step_size = jax.nn.softplus(step_pre)

    def widened(values, axis=-1):
        more = padded_channels - channels
        if not more:
            return values
        pads = [(0, 0)] * values.ndim
        pads[axis] = (0, more)
        return jnp.pad(values, pads)

    scan = Scan(tok_seq, padded_channels, chan_count)
    decay_rates = jnp.exp(a_log)
    rates = widened((-LOG2E * decay_rates).T)
    breaks = jnp.any(position[..., None] == starts, axis=-1).astype(f32) * BREAK
    breaks = jnp.broadcast_to(breaks.reshape(tok_seq, 1), (tok_seq, LANES))
    step_w, mixed_w = widened(step_size), widened(mixed)
    part, sums, total = scan.ends(False, step_w, mixed_w, breaks, b_in, rates)
    device_entry = carried(total, rates, False)
    full_up = whole_expert(up_weight, None, device_entry)
    grad_arrived = expert_rows_early(after(pack(grad_steps), device_entry)).reshape(-1, model_width)
    scan_out, gated_b, entry = scan.outputs(
        step_w, mixed_w, breaks, b_in, c_out, rates, part, sums, device_entry,
        widened(skip_gain[None]), widened(gate_z),
    )
    scan_out, gated_b = scan_out[:, :channels], gated_b[:, :channels]
    full_down = whole_expert(down_weight, device_entry, gated_b)

    mixer_rows = chan_sums(
        lambda rows: jnp.dot(rows, out_weight, preferred_element_type=f32), gated_b
    )
    hidden_one = residual + mixer_rows
    moe_in, moe_back = jax.vjp(norm_apply, hidden_one, moe_gain)
    logits = jnp.einsum("td,de->et", moe_in, router_weight, precision=HIGH)
    every_logit = gathered_everywhere(logits)
    gate_row, scaled, row_totals, columns = sinkhorn(
        dev_ref, every_logit, route_steps.reshape(1, tok_dev)
    )
    gate = gate_row.reshape(tok_dev)

    gate_slots = jnp.einsum("ts,t->s", placer.astype(f32), gate, precision=HIGH)
    gate_slots = jnp.pad(gate_slots.reshape(EXPERTS, 1, capacity), ((0, 0), (0, 7), (0, LANES - capacity)))
    arrived, gate_arrived = expert_rows(1, pack(moe_in.astype(bf16)), gate_slots)
    arrived = arrived.reshape(-1, model_width)
    gate_arrived = gate_arrived[:, 0, :capacity].reshape(-1, 1)
    own, share = expert_groups()
    features, hidden = up_weight.shape[1:]
    side = lax.rem(seq_place, 2).astype(jnp.int32).reshape(1)
    expert_out, grad_rows_in, up_kept, up_sent, down_kept, down_sent = expert_passes(
        side, arrived, grad_arrived, gate_arrived, full_up, full_down
    )
    expert_grads = [
        added(kept, swapped(sent, "seq", 1)).reshape(own, share // 2, features, hidden)
        for kept, sent in ((up_kept, up_sent), (down_kept, down_sent))
    ]
    blocks = (EXPERTS, capacity, model_width)

    expert_back, grad_back = expert_rows(
        2, after(expert_out, *expert_grads).reshape(blocks), grad_rows_in.reshape(blocks)
    )
    for stage in range(1, share.bit_length() - 1):
        expert_grads = [halved(part, stage) for part in expert_grads]
    expert_tok = unpack(after(expert_back, *expert_grads))
    plain_grad_part = unpack(grad_back)
    up_part, down_part = expert_grads

    block_out = from_steps((hidden_one + gate[:, None] * expert_tok).astype(bf16))
    grad_two = grad_steps.astype(f32)
    grad_gate = jnp.sum(expert_tok * grad_two, 1)
    grad_probs = jnp.where(
        route_steps[None] == lax.broadcasted_iota(jnp.int32, (EXPERTS, 1), 0),
        EXPERTS * grad_gate[None],
        0.0,
    )
    every_grad = gathered_everywhere(grad_probs)
    up_grad = to_owners(after(up_part.reshape(own, *up_part.shape[2:]), every_grad))
    grad_logits = sinkhorn_back(dev_ref, every_logit, scaled, row_totals, columns, every_grad)
    router_grad = jnp.einsum("td,et->ed", moe_in, grad_logits, precision=HIGH)
    grad_moe_in = gate[:, None] * plain_grad_part + jnp.einsum(
        "et,de->td", grad_logits, router_weight, precision=HIGH
    )
    grad_hidden, moe_gain_grad = moe_back(grad_moe_in)
    grad_hidden = grad_hidden + grad_two

    grad_mix = chan_rows(grad_hidden.astype(bf16))
    grad_gated = jnp.einsum("td,ed->te", grad_mix, out_weight, preferred_element_type=f32)
    out_weight_grad = jnp.einsum("te,td->ed", gated_b, grad_mix, preferred_element_type=f32)
    grad_scan = grad_gated * jax.nn.silu(gate_z)
    grad_gate_z = (grad_gated * scan_out * silu_grad(gate_z)).astype(bf16)
    skip_grad = jnp.sum(grad_scan * mixed, 0)
    gate_weight_grad = jnp.einsum("td,te->de", gathered, grad_gate_z, preferred_element_type=f32)
    gains = jnp.concatenate([moe_gain_grad[None], router_grad], 0)
    gains = lax.psum(gains, "chan") if chan_count != 2 else gains + swapped(gains, "chan", 1)
    grad_scan_w = widened(grad_scan)
    back_part, back_sums, back_total = scan.ends(True, step_w, grad_scan_w, breaks, c_out, rates)
    back_entry = carried(after(back_total, up_grad), rates, True)
    step_grad, mixed_grad, b_grad, c_grad, rate_grad, early = scan.grads(
        step_w, mixed_w, breaks, grad_scan_w, b_in, c_out, rates, entry, back_part, back_sums,
        back_entry, (out_weight_grad.astype(bf16).reshape(-1, channels), gate_weight_grad.astype(bf16)),
    )
    early = early.reshape(-1, channels)
    down_grad = to_owners(after(down_part.reshape(own, *down_part.shape[2:]), step_grad))
    step_grad, mixed_grad = step_grad[:, :channels], mixed_grad[:, :channels]
    mixed_grad = mixed_grad + skip_gain * grad_scan
    a_log_rows = -decay_rates.T * rate_grad[:, :channels]
    step_pre_grad = step_grad * jax.nn.sigmoid(step_pre)
    dt_bias_grad = jnp.sum(step_pre_grad, 0)
    dt_weight_grad = jnp.einsum("tr,te->re", low_rank, step_pre_grad, precision=HIGH)
    rank_grad = jnp.einsum("te,re->tr", step_pre_grad, dt_weight, precision=HIGH)
    proj_grad_b = proj_total(jnp.concatenate([rank_grad, b_grad, c_grad], 1)).astype(bf16)
    mixed_grad = mixed_grad + jnp.einsum(
        "tp,ep->te", proj_grad_b, xproj_weight, preferred_element_type=f32
    )
    xproj_rows = jnp.einsum("te,tp->pe", mixed_b, proj_grad_b, preferred_element_type=f32)
    conv_grad = (mixed_grad * silu_grad(conv_pre)).reshape(shape4 + (channels,))
    conv_bias_grad = jnp.sum(conv_grad, (0, 1, 2))
    conv_weight_grad = jnp.stack(
        [
            jnp.sum(conv_grad * masks[offset] * padded[:, offset : offset + steps], (0, 1, 2))
            for offset in range(CONV)
        ]
    )
    padded_grad = 0.0
    for offset in range(CONV):
        padded_grad = padded_grad + jnp.pad(
            conv_weight[offset] * conv_grad * masks[offset],
            ((0, 0), (offset, reach - offset), (0, 0), (0, 0)),
        )
    head_grad = jnp.swapaxes(padded_grad[:, :reach], 0, 1).reshape(
        reach, chan_count * CHUNKS, channels
    )
    from_next = passed_along(head_grad[:, 0], "seq", -1)
    tail_grad = jnp.concatenate([head_grad[:, 1:], from_next[:, None]], 1)
    tail_grad = jnp.swapaxes(tail_grad.reshape(reach, chan_count, CHUNKS, channels), 0, 1)
    inner_grad = padded_grad[:, reach:] + jnp.pad(
        tail_grad, ((0, 0), (steps - reach, 0), (0, 0), (0, 0))
    )
    inner_grad_b = inner_grad.reshape(tok_seq, channels).astype(bf16)
    inner_weight_grad = jnp.einsum("td,te->de", gathered, inner_grad_b, preferred_element_type=f32)
    both_grad = jnp.concatenate([inner_grad_b, grad_gate_z], 1)
    normed_grad = chan_sums(
        lambda rows: jnp.dot(rows[:, :channels], in_weight[0].T, preferred_element_type=f32)
        + jnp.dot(rows[:, channels:], in_weight[1].T, preferred_element_type=f32),
        both_grad,
    )
    residual_grad, norm_gain_grad = norm_back(normed_grad)
    in_grad = from_steps(residual_grad + grad_hidden)

    norm_rows = norm_gain_grad[None]
    norm_rows = lax.psum(norm_rows, "chan") if chan_count != 2 else norm_rows + swapped(norm_rows, "chan", 1)
    pieces = (
        xproj_rows, dt_weight_grad, a_log_rows, conv_weight_grad, conv_bias_grad[None], dt_bias_grad[None],
        skip_grad[None], norm_rows.reshape(-1, channels), gains.reshape(-1, channels),
    )
    bounds = [sum(part.shape[0] for part in pieces[: k + 1]) for k in range(len(pieces) - 1)]
    inner_weight_grad, small = summed([after(inner_weight_grad.astype(bf16), down_grad), jnp.concatenate(pieces, 0)])
    early = after(early, small)
    out_weight_grad = early[:model_width].reshape(channels, model_width).astype(f32)
    gate_weight_grad = early[model_width : 2 * model_width].astype(f32)
    (
        xproj_rows, dt_weight_grad, a_log_rows, conv_weight_grad, conv_bias_grad, dt_bias_grad, skip_grad,
        norm_rows, gains,
    ) = jnp.split(small, bounds, 0)
    norm_gain_grad, gains = norm_rows.reshape(-1), gains.reshape(-1, model_width)
    xproj_grad, a_log_grad = xproj_rows.T, a_log_rows.T
    conv_bias_grad, dt_bias_grad, skip_grad = conv_bias_grad[0], dt_bias_grad[0], skip_grad[0]
    moe_gain_grad, router_grad = gains[0], gains[1:].T
    in_weight_grad = jnp.stack([inner_weight_grad, gate_weight_grad])
    return (
        block_out,
        in_grad,
        norm_gain_grad,
        in_weight_grad,
        conv_weight_grad,
        conv_bias_grad,
        xproj_grad,
        dt_weight_grad,
        dt_bias_grad,
        a_log_grad,
        skip_grad,
        out_weight_grad,
        moe_gain_grad,
        router_grad,
        up_grad.astype(f32),
        down_grad.astype(f32),
    )


def solution(mesh):
    in_specs = (
        P(("seq", "chan"), None),
        P(("seq", "chan"), None),
        P(),
        P(),
        P(None, None, "chan"),
        P(None, "chan"),
        P("chan"),
        P("chan", None),
        P(None, "chan"),
        P("chan"),
        P("chan", None),
        P("chan"),
        P("chan", None),
        P(),
        P(),
        P("chan", "seq", None),
        P("chan", "seq", None),
        P(("seq", "chan"), None),
    )
    out_specs = (
        P(("seq", "chan"), None),
        P(("seq", "chan"), None),
        P(),
        P(None, None, "chan"),
        P(None, "chan"),
        P("chan"),
        P("chan", None),
        P(None, "chan"),
        P("chan"),
        P("chan", None),
        P("chan"),
        P("chan", None),
        P(),
        P(),
        P("chan", "seq", None),
        P("chan", "seq", None),
    )
    return jax.shard_map(
        on_device, mesh=mesh, in_specs=in_specs, out_specs=out_specs, check_vma=False
    )
```

```python
from functools import partial

import jax
import jax.numpy as jnp
from jax import lax
from jax.experimental import pallas as pl
from jax.experimental.pallas import tpu as pltpu
from jax.sharding import PartitionSpec as P

STATE = 16
CONV = 4
DT_RANK = 72
EXPERTS = 8
SINK = 8
CHUNKS = 8
LANES = 128
VMEM_LIMIT = 56 * 1024 * 1024

EPS = 1e-05
HIGH = lax.Precision.HIGHEST
LOG2E = 1.4426950408889634
LN2 = 0.6931471805599453
BREAK = 1e30
MESH = pl.DeviceIdType.MESH
GELU_SCALE = 0.7978845608028654
GELU_CUBE = 0.044715


def passed_along(value, axis, steps):
    count = lax.axis_size(axis)
    leading, last = (max(0, -steps), min(count, count - steps))
    return lax.ppermute(value, axis, [(source, source + steps) for source in range(leading, last)])


def swapped(value, axis, bit):
    count = lax.axis_size(axis)
    return lax.ppermute(value, axis, [(source, source ^ bit) for source in range(count)])


def chan_rows(values):
    if lax.axis_size("chan") != 2:
        return lax.all_gather(values, "chan", axis=0, tiled=True)
    first = lax.axis_index("chan") == 0
    other = swapped(values, "chan", 1)
    return jnp.concatenate([jnp.where(first, values, other), jnp.where(first, other, values)], 0)


def chan_sums(term_fn, operand):
    count, place = lax.axis_size("chan"), lax.axis_index("chan")
    rows = operand.shape[0] // count
    if count != 2:
        return lax.psum_scatter(term_fn(operand), "chan", scatter_dimension=0, tiled=True)
    theirs = term_fn(lax.dynamic_slice_in_dim(operand, (1 - place) * rows, rows, 0))
    arrived = swapped(theirs.astype(jnp.bfloat16), "chan", 1)
    return term_fn(lax.dynamic_slice_in_dim(operand, place * rows, rows, 0)) + arrived.astype(
        jnp.float32
    )


def proj_total(values):
    if lax.axis_size("chan") != 2:
        return lax.psum(values, "chan")
    return values + swapped(values, "chan", 1)


def expert_groups():
    own = EXPERTS // lax.axis_size("chan")
    return own, lax.axis_size("seq") // own


def across_experts(values, axis, wait=None):
    own, share = expert_groups()
    place = lax.div(lax.axis_index("seq"), share)
    out = values
    for d in range(1, own):
        peer = lax.bitwise_xor(place, d)
        came = swapped(lax.dynamic_slice_in_dim(values, peer, 1, axis), "seq", d * share)
        if wait is not None:
            came = after(came, wait)
        out = lax.dynamic_update_slice_in_dim(out, came, peer, axis)
    return out


def to_owners(grad):
    own, share = expert_groups()
    if own == 1:
        return grad
    groups = [[k * share + q for k in range(own)] for q in range(share)]
    return lax.all_to_all(
        grad, "seq", split_axis=0, concat_axis=0, tiled=True, axis_index_groups=groups
    )


def expert_rows(ident, *arrays):
    return exchange(ident, arrays)


def whole_expert(weight, start, wait):
    own, share = expert_groups()
    features, hidden = weight.shape[1:]
    if start is not None:
        weight = after(weight, start)
    mine = across_experts(weight, 0, wait)
    groups = [[k * share + q for q in range(share)] for k in range(own)]
    return lax.all_gather(mine, "seq", axis_index_groups=groups)


def halved(grad, stage):
    own, share = expert_groups()
    bit = 1 << stage
    pairs = grad.reshape(own, grad.shape[1] // 2, 2, *grad.shape[2:])
    side = lax.rem(lax.div(lax.axis_index("seq"), bit), 2)
    sent = lax.dynamic_index_in_dim(pairs, 1 - side, 2, False)
    kept = lax.dynamic_index_in_dim(pairs, side, 2, False)
    came = swapped(sent, "seq", bit)
    return added(kept, came)


def added(kept, came):
    return (kept.astype(jnp.float32) + came.astype(jnp.float32)).astype(kept.dtype)


def after(value, *others):
    return lax.optimization_barrier((value,) + others)[0]


def lasting(microseconds):
    return pl.CostEstimate(flops=0, bytes_accessed=microseconds * 3_600_000, transcendentals=0)


def opposite(place, bit):
    return place + bit - 2 * bit * lax.rem(lax.div(place, bit), 2)


def greet(targets):
    barrier = pltpu.get_barrier_semaphore()
    for target in targets:
        pl.semaphore_signal(barrier, inc=1, device_id=target, device_id_type=MESH)
    pl.semaphore_wait(barrier, len(targets))


class Exchange:
    def __init__(self, own, share, chans, sources, results, send_sem, recv_sem, own_sem):
        seq, chan = lax.axis_index("seq"), lax.axis_index("chan")
        column = lax.rem(seq, share)
        me = chan * own + lax.div(seq, share)
        total = own * chans
        peers = [lax.rem(me + d, total) for d in range(1, total)]
        self.targets = [(lax.rem(peer, own) * share + column, lax.div(peer, own)) for peer in peers]
        self.copies = []
        for k, (source, result) in enumerate(zip(sources, results)):
            for d in range(total - 1):
                self.copies.append(
                    pltpu.make_async_remote_copy(
                        src_ref=source.at[peers[d]],
                        dst_ref=result.at[me],
                        send_sem=send_sem.at[k, d],
                        recv_sem=recv_sem.at[k, d],
                        device_id=self.targets[d],
                        device_id_type=MESH,
                    )
                )
            self.copies.append(pltpu.make_async_copy(source.at[me], result.at[me], own_sem.at[k]))

    def start(self):
        greet(self.targets)
        for copy in self.copies:
            copy.start()

    def wait(self):
        for copy in self.copies:
            copy.wait()


def exchange_scratch(count):
    others = expert_groups()[0] * lax.axis_size("chan") - 1
    return [
        pltpu.SemaphoreType.DMA((count, others)),
        pltpu.SemaphoreType.DMA((count, others)),
        pltpu.SemaphoreType.DMA((count,)),
    ]


def exchange_kernel(own, share, chans, count, *refs):
    rows = Exchange(own, share, chans, refs[:count], refs[count : 2 * count], *refs[2 * count :])
    rows.start()
    rows.wait()


def exchange(ident, arrays):
    own, share = expert_groups()
    chans, count = lax.axis_size("chan"), len(arrays)
    anywhere = pl.BlockSpec(memory_space=pl.ANY)
    return pl.pallas_call(
        partial(exchange_kernel, own, share, chans, count),
        in_specs=[anywhere] * count,
        out_specs=[anywhere] * count,
        out_shape=[jax.ShapeDtypeStruct(part.shape, part.dtype) for part in arrays],
        scratch_shapes=exchange_scratch(count),
        compiler_params=pltpu.CompilerParams(collective_id=ident, has_side_effects=True),
        cost_estimate=lasting(26 * count),
        name="expert_rows",
    )(*arrays)


def gather_kernel(devices, chans, passed, own_ref, *refs):
    every_ref, send_sem, recv_sem = refs[passed], refs[-2], refs[-1]
    me = lax.axis_index("seq") * chans + lax.axis_index("chan")
    barrier = pltpu.get_barrier_semaphore()

    def target(d):
        peer = lax.rem(me + d, devices)
        return (lax.div(peer, chans), lax.rem(peer, chans))

    def copy(d):
        return pltpu.make_async_remote_copy(
            src_ref=own_ref,
            dst_ref=every_ref.at[me],
            send_sem=send_sem.at[d - 1],
            recv_sem=recv_sem.at[d - 1],
            device_id=target(d),
            device_id_type=MESH,
        )

    def signal(d, carry):
        pl.semaphore_signal(barrier, inc=1, device_id=target(d), device_id_type=MESH)
        return carry

    def start(d, carry):
        copy(d).start()
        return carry

    def finish(d, carry):
        copy(d).wait()
        return carry

    lax.fori_loop(1, devices, signal, 0)
    every_ref[me] = own_ref[...]
    pl.semaphore_wait(barrier, devices - 1)
    lax.fori_loop(1, devices, start, 0)
    lax.fori_loop(1, devices, finish, 0)


def gathered_everywhere(ident, values, *passed):
    chans = lax.axis_size("chan")
    devices = lax.axis_size("seq") * chans
    vmem, anywhere = pl.BlockSpec(memory_space=pltpu.VMEM), pl.BlockSpec(memory_space=pl.ANY)
    out = pl.pallas_call(
        partial(gather_kernel, devices, chans, len(passed)),
        in_specs=[vmem] + [anywhere] * len(passed),
        out_specs=[vmem] + [anywhere] * len(passed),
        out_shape=[jax.ShapeDtypeStruct((devices,) + values.shape, values.dtype)]
        + [jax.ShapeDtypeStruct(part.shape, part.dtype) for part in passed],
        input_output_aliases={1 + k: 1 + k for k in range(len(passed))},
        scratch_shapes=[
            pltpu.SemaphoreType.DMA((devices - 1,)),
            pltpu.SemaphoreType.DMA((devices - 1,)),
        ],
        compiler_params=pltpu.CompilerParams(
            collective_id=ident, has_side_effects=True, vmem_limit_bytes=VMEM_LIMIT
        ),
        cost_estimate=lasting(12),
        name="gather_small",
    )(values, *passed)
    return out if passed else out[0]


def carry_kernel(count, reverse, total_ref, rate_ref, *refs):
    entry_ref, ends_out, ends_in, sums_out, sums_in, ends_sems, sums_sems = refs[-7:]
    me = lax.axis_index("seq")
    bits = [1 << k for k in range(count.bit_length() - 1)]
    greet([{"seq": opposite(me, bit)} for bit in bits])
    rates = rate_ref[...]
    ends, sums = total_ref[:STATE], total_ref[STATE : STATE + 1]
    before, before_sum = jnp.zeros_like(ends), jnp.zeros_like(sums)
    for k, bit in enumerate(bits):
        ends_out[k] = ends.astype(ends_out.dtype)
        sums_out[k] = sums
        copies = [
            pltpu.make_async_remote_copy(
                src_ref=out.at[k],
                dst_ref=into.at[k],
                send_sem=sems.at[0, k],
                recv_sem=sems.at[1, k],
                device_id={"seq": opposite(me, bit)},
                device_id_type=MESH,
            )
            for out, into, sems in ((ends_out, ends_in, ends_sems), (sums_out, sums_in, sums_sems))
        ]
        for copy in copies:
            copy.start()
        for copy in copies:
            copy.wait()
        their_ends, their_sums = ends_in[k].astype(jnp.float32), sums_in[k]
        theirs_first = lax.rem(lax.div(me, bit), 2) == (0 if reverse else 1)
        before = jnp.where(theirs_first, jnp.exp2(rates * before_sum) * their_ends + before, before)
        before_sum = jnp.where(theirs_first, before_sum + their_sums, before_sum)
        ends = jnp.where(
            theirs_first,
            jnp.exp2(rates * sums) * their_ends + ends,
            jnp.exp2(rates * their_sums) * ends + their_ends,
        )
        sums = sums + their_sums
    entry_ref[...] = before


def carried(total, rates, reverse, *needed):
    count = lax.axis_size("seq")
    rounds = count.bit_length() - 1
    channels = rates.shape[1]
    vmem = pl.BlockSpec(memory_space=pltpu.VMEM)
    return pl.pallas_call(
        partial(carry_kernel, count, reverse),
        in_specs=[vmem, vmem] + [pl.BlockSpec(memory_space=pl.ANY)] * len(needed),
        out_specs=vmem,
        out_shape=jax.ShapeDtypeStruct(rates.shape, jnp.float32),
        scratch_shapes=[
            pltpu.VMEM((rounds, STATE, channels), jnp.bfloat16),
            pltpu.VMEM((rounds, STATE, channels), jnp.bfloat16),
            pltpu.VMEM((rounds, 1, channels), jnp.float32),
            pltpu.VMEM((rounds, 1, channels), jnp.float32),
            pltpu.SemaphoreType.DMA((2, rounds)),
            pltpu.SemaphoreType.DMA((2, rounds)),
        ],
        compiler_params=pltpu.CompilerParams(
            collective_id=5 if reverse else 4, has_side_effects=True, vmem_limit_bytes=VMEM_LIMIT
        ),
        cost_estimate=lasting(14),
        name="carry_back" if reverse else "carry",
    )(total, rates, *needed)


class Halving:
    def __init__(self, count, held, incoming, result, send_sem, recv_sem):
        self.held, self.incoming, self.result = held, incoming, result
        self.send_sem, self.recv_sem = send_sem, recv_sem
        self.chunks, self.rows = held.shape[0], held.shape[1]
        me = lax.axis_index("seq")
        bits = [1 << k for k in range(count.bit_length() - 1)]
        self.rounds = len(bits)
        self.peers = [{"seq": opposite(me, bit)} for bit in bits]
        self.sides = [lax.rem(lax.div(me, bit), 2) for bit in bits]
        self.lows, self.lengths = [0], [self.rows]
        for side in self.sides:
            self.lengths.append(self.lengths[-1] // 2)
            self.lows.append(self.lows[-1] + side * self.lengths[-1])
        self.turns = 4 * self.rounds + self.chunks - 1

    def greet(self):
        barrier = pltpu.get_barrier_semaphore()
        for peer in self.peers:
            pl.semaphore_signal(barrier, inc=1, device_id=peer, device_id_type=MESH)

    def greeted(self):
        pl.semaphore_wait(pltpu.get_barrier_semaphore(), self.rounds)

    def span(self, k, other=False):
        low = self.lows[k]
        if other:
            low = self.lows[k - 1] + (1 - self.sides[k - 1]) * self.lengths[k]
        return pl.ds(pl.multiple_of(low, 16), self.lengths[k])

    def landing(self, step):
        return pl.ds(self.rows - self.lengths[step], self.lengths[step + 1])

    def copy(self, c, step):
        if step < self.rounds:
            k = step
            source = self.held.at[c, self.span(k + 1, True)]
            target = self.incoming.at[c, self.landing(step)]
        else:
            k = 2 * self.rounds - 1 - step
            source = target = self.result.at[c, self.span(k + 1)]
        return pltpu.make_async_remote_copy(
            src_ref=source,
            dst_ref=target,
            send_sem=self.send_sem.at[c, step],
            recv_sem=self.recv_sem.at[c, step],
            device_id=self.peers[k],
            device_id_type=MESH,
        )

    def start(self):
        self.copy(0, 0).start()

    def turn(self, turn):
        if turn + 1 < self.chunks:
            self.copy(turn + 1, 0).start()
        for c in range(self.chunks):
            step, odd = divmod(turn - c - 1, 2)
            if odd or not 0 <= step < 2 * self.rounds:
                continue
            self.copy(c, step).wait()
            if step < self.rounds:
                kept = self.span(step + 1)
                total = self.held[c, kept].astype(jnp.float32)
                total = total + self.incoming[c, self.landing(step)].astype(jnp.float32)
                target = self.held if step < self.rounds - 1 else self.result
                target[c, kept] = total.astype(target.dtype)
            if step < 2 * self.rounds - 1:
                self.copy(c, step + 1).start()


def sum_scratch(chunks, rows, width, count):
    steps = 2 * (count.bit_length() - 1)
    return [
        pltpu.VMEM((chunks, rows, width), jnp.bfloat16),
        pltpu.VMEM((chunks, rows, width), jnp.bfloat16),
        pltpu.SemaphoreType.DMA((chunks, steps)),
        pltpu.SemaphoreType.DMA((chunks, steps)),
    ]


def sum_kernel(count, places, sizes, *refs):
    parts, sum_ref = refs[: len(places)], refs[len(places)]
    held, incoming, send_sem, recv_sem = refs[len(places) + 1 :]
    halving = Halving(count, held, incoming, sum_ref, send_sem, recv_sem)
    rows = halving.rows
    halving.greet()
    used = max(place + size for place, size in zip(places, sizes))
    for c in range(halving.chunks):
        for part, place, size in zip(parts, places, sizes):
            low, high = max(place, c * rows), min(place + size, (c + 1) * rows)
            if low < high:
                held[c, low - c * rows : high - c * rows] = part[low - place : high - place].astype(held.dtype)
        if used < (c + 1) * rows:
            low = max(used - c * rows, 0)
            held[c, low:] = jnp.zeros((rows - low, held.shape[2]), held.dtype)
    halving.greeted()
    halving.start()
    for turn in range(halving.turns):
        halving.turn(turn)


def summed(parts):
    count = lax.axis_size("seq")
    width = parts[0].shape[1]
    sizes = [part.shape[0] for part in parts]
    places, used = [], 0
    for size in sizes:
        places.append(used)
        used += -(-size // 16) * 16
    chunk = 16 * count
    chunks = -(-used // chunk)
    vmem = pl.BlockSpec(memory_space=pltpu.VMEM)
    padded = [jnp.pad(part, ((0, -part.shape[0] % 16), (0, 0))) for part in parts]
    total = pl.pallas_call(
        partial(sum_kernel, count, places, [part.shape[0] for part in padded]),
        in_specs=[vmem] * len(parts),
        out_specs=vmem,
        out_shape=jax.ShapeDtypeStruct((chunks, chunk, width), jnp.bfloat16),
        scratch_shapes=sum_scratch(chunks, chunk, width, count),
        compiler_params=pltpu.CompilerParams(
            collective_id=6, has_side_effects=True, vmem_limit_bytes=VMEM_LIMIT
        ),
        cost_estimate=lasting(60),
        name="sum_late",
    )(*padded).reshape(chunks * chunk, width)
    return [total[place : place + size].astype(jnp.float32) for place, size in zip(places, sizes)]


def to_steps(values):
    rows = values.shape[0]
    parts = values.reshape((CHUNKS, rows // CHUNKS) + values.shape[1:])
    return jnp.swapaxes(parts, 0, 1).reshape(values.shape)


def from_steps(values):
    rows = values.shape[0]
    parts = values.reshape((rows // CHUNKS, CHUNKS) + values.shape[1:])
    return jnp.swapaxes(parts, 0, 1).reshape(values.shape)


def stacked(*parts):
    rows = sum(part.shape[0] for part in parts)
    whole = jnp.concatenate([part.astype(jnp.bfloat16) for part in parts], 0)
    return jnp.pad(whole, ((0, -rows % 16), (0, 0)))


def unstacked(whole, parts):
    out, first = [], 0
    for part in parts:
        out.append(whole[first : first + part.shape[0]].astype(jnp.float32))
        first += part.shape[0]
    return out


def norm_apply(values, gain):
    return values * lax.rsqrt(jnp.mean(values * values, -1, keepdims=True) + EPS) * gain


def silu_grad(values):
    sigma = jax.nn.sigmoid(values)
    return sigma * (1.0 + values * (1.0 - sigma))


def spread(target, source):
    for n in range(STATE):
        target[n] = jnp.broadcast_to(source[:, n : n + 1], target.shape[1:])


def full(row):
    return jnp.broadcast_to(row, (CHUNKS, LANES))


def shifted(values, by, down):
    sub = lax.broadcasted_iota(jnp.int32, (CHUNKS, LANES), 0)
    if down:
        return jnp.where(sub >= by, pltpu.roll(values, by, 0), 0.0)
    return jnp.where(sub < CHUNKS - by, pltpu.roll(values, CHUNKS - by, 0), 0.0)


def chunk_windows(sums, down):
    windows = []
    for by in (1, 2, 4):
        windows.append(sums)
        sums = sums + shifted(sums, by, down)
    return windows, sums


def chunk_prefix(ends, windows, rate, down):
    for by, window in zip((1, 2, 4), windows):
        ends = ends + jnp.exp2(rate * window) * shifted(ends, by, down)
    return ends


def ends_and_rows_kernel(halves, places, *refs):
    ins, source, outs, result, wide, sems = refs[:5], refs[5], refs[6:9], refs[9], refs[10], refs[11:]
    rows = Exchange(*places, [source], [result], *sems)

    @pl.when(pl.program_id(0) == 0)
    def _():
        rows.start()

    ends_kernel(halves, False, *ins, *outs, wide)

    @pl.when(pl.program_id(0) == pl.num_programs(0) - 1)
    def _():
        rows.wait()


def ends_kernel(halves, reverse, step_ref, drive_ref, break_ref, map_ref, rate_ref, part_ref, sum_ref, tot_ref, wide):
    rows = step_ref.shape[0]
    steps = rows // (halves * CHUNKS)

    @pl.when(pl.program_id(0) == 0)
    def _():
        spread(wide, map_ref)

    rates = [full(rate_ref[n : n + 1, :]) for n in range(STATE)]
    zero = jnp.zeros((CHUNKS, LANES), jnp.float32)

    def half(turn, carry):
        h = halves - 1 - turn if reverse else turn
        before_sum, before = carry[0], carry[1:]

        def body(k, state):
            s = steps - 1 - k if reverse else k
            at = pl.ds(pl.multiple_of((h * steps + s) * CHUNKS, CHUNKS), CHUNKS)
            step = step_ref[at, :]
            decay_step = step + break_ref[at, :]
            drive = drive_ref[at, :]
            if not reverse:
                drive = drive * step
            new = [state[0] + decay_step]
            for n in range(STATE):
                decay = jnp.exp2(decay_step * rates[n])
                if reverse:
                    new.append(decay * (state[n + 1] + drive * wide[n, at, :]))
                else:
                    new.append(decay * state[n + 1] + drive * wide[n, at, :])
            return tuple(new)

        out = lax.fori_loop(0, steps, body, (zero,) * (STATE + 1), unroll=10)
        windows, sums = chunk_windows(out[0], not reverse)
        prior = shifted(sums, 1, not reverse)
        last = slice(0, 1) if reverse else slice(CHUNKS - 1, CHUNKS)
        sum_ref[h] = prior + before_sum
        new = [before_sum + full(sums[last])]
        for n in range(STATE):
            joined = chunk_prefix(out[n + 1], windows, rates[n], not reverse)
            part_ref[h, n] = shifted(joined, 1, not reverse) + jnp.exp2(rates[n] * prior) * before[n]
            new.append(full(joined[last]) + jnp.exp2(rates[n] * full(sums[last])) * before[n])
        return tuple(new)

    total = lax.fori_loop(0, halves, half, (zero,) * (STATE + 1))
    for n in range(STATE):
        tot_ref[n : n + 1, :] = total[n + 1][0:1]
    tot_ref[STATE:, :] = total[0]


def outputs_kernel(
    halves, step_ref, mixed_ref, break_ref, b_ref, c_ref, rate_ref, part_ref, sum_ref, device,
    skip_ref, gate_ref, scan_ref, gated_ref, entry_ref, b_wide, c_wide,
):
    rows = step_ref.shape[0]
    steps = rows // (halves * CHUNKS)

    @pl.when(pl.program_id(0) == 0)
    def _():
        spread(b_wide, b_ref)
        spread(c_wide, c_ref)

    rates = [full(rate_ref[n : n + 1, :]) for n in range(STATE)]

    def half(h, carry):
        state = []
        for n in range(STATE):
            state.append(
                part_ref[h, n] + jnp.exp2(rates[n] * sum_ref[h]) * full(device[n : n + 1, :])
            )
            entry_ref[h, n] = state[n]

        def body(s, state):
            at = pl.ds(pl.multiple_of((h * steps + s) * CHUNKS, CHUNKS), CHUNKS)
            step = step_ref[at, :]
            decay_step = step + break_ref[at, :]
            drive = mixed_ref[at, :] * step
            total = None
            new = []
            for n in range(STATE):
                value = jnp.exp2(decay_step * rates[n]) * state[n] + drive * b_wide[n, at, :]
                term = value * c_wide[n, at, :]
                total = term if total is None else total + term
                new.append(value)
            scan_ref[at, :] = total
            return tuple(new)

        lax.fori_loop(0, steps, body, tuple(state), unroll=5)
        return carry

    lax.fori_loop(0, halves, half, 0)
    gate = gate_ref[...]
    out = scan_ref[...] + skip_ref[...] * mixed_ref[...]
    scan_ref[...] = out
    gated_ref[...] = (out * (gate * jax.nn.sigmoid(gate))).astype(gated_ref.dtype)


def early_fills(first, second, held, own_sem):
    rows, copies, place = held.shape[1], [], 0
    for part in (first, second):
        done = 0
        while done < part.shape[0]:
            c, low = (place + done) // rows, (place + done) % rows
            length = min(rows - low, part.shape[0] - done)
            copies.append(
                pltpu.make_async_copy(
                    part.at[pl.ds(done, length)], held.at[c, pl.ds(low, length)], own_sem.at[len(copies)]
                )
            )
            done += length
        place += part.shape[0]
    return copies


def grads_kernel(
    halves, count, groups, step_ref, mixed_ref, break_ref, grad_ref, b_ref, c_ref, rate_ref, entry_ref,
    part_ref, sum_ref, device, first_early, second_early, step_out, mixed_out, b_out, c_out, rate_out, early_out,
    b_wide, c_wide, b_sum, c_sum, decays, states, held, incoming, summed_early, send_sem, recv_sem, own_sem,
):
    rows = step_ref.shape[0]
    steps = rows // (halves * CHUNKS)
    group = pl.program_id(0)
    block = STATE // 2
    halving = Halving(count, held, incoming, summed_early, send_sem, recv_sem)
    slots = [[] for _ in range(2 * groups)]
    for turn in range(halving.turns):
        slots[turn * 2 * groups // halving.turns].append(turn)

    @pl.when(group == 0)
    def _():
        halving.greet()
        fills = early_fills(first_early, second_early, held, own_sem)
        for fill in fills:
            fill.start()
        for fill in fills:
            fill.wait()
        halving.greeted()
        halving.start()
        spread(b_wide, b_ref)
        spread(c_wide, c_ref)
        b_sum[...] = jnp.zeros_like(b_sum)
        c_sum[...] = jnp.zeros_like(c_sum)

    zero = jnp.zeros((CHUNKS, LANES), jnp.float32)

    for first in (0, block):
        rates = [full(rate_ref[first + n : first + n + 1, :]) for n in range(block)]

        def half(h, rate_sums):
            entry = []
            for n in range(block):
                entry.append(entry_ref[h, first + n])
                states[0, n] = entry[n]

            def ahead(s, state):
                at = pl.ds(pl.multiple_of((h * steps + s) * CHUNKS, CHUNKS), CHUNKS)
                step = step_ref[at, :]
                decay_step = step + break_ref[at, :]
                drive = mixed_ref[at, :] * step
                new = []
                for n in range(block):
                    decay = jnp.exp2(decay_step * rates[n])
                    value = decay * state[n] + drive * b_wide[first + n, at, :]
                    decays[s, n] = decay
                    states[s + 1, n] = value
                    new.append(value)
                return tuple(new)

            lax.fori_loop(0, steps, ahead, tuple(entry), unroll=10)

            exits = [
                part_ref[h, first + n]
                + jnp.exp2(rates[n] * sum_ref[h]) * full(device[first + n : first + n + 1, :])
                for n in range(block)
            ]

            def back(k, carry):
                s = steps - 1 - k
                at = pl.ds(pl.multiple_of((h * steps + s) * CHUNKS, CHUNKS), CHUNKS)
                step = step_ref[at, :]
                mixed = mixed_ref[at, :]
                grad = grad_ref[at, :]
                drive = mixed * step
                by_rate, by_map = zero, zero
                flows, sums = [], []
                for n in range(block):
                    b_now, c_now = b_wide[first + n, at, :], c_wide[first + n, at, :]
                    here = carry[n] + c_now * grad
                    flow = decays[s, n] * here
                    log_grad = flow * states[s, n]
                    by_rate = by_rate + rates[n] * log_grad
                    by_map = by_map + b_now * here
                    b_sum[first + n, at, :] += drive * here
                    c_sum[first + n, at, :] += grad * states[s + 1, n]
                    flows.append(flow)
                    sums.append(carry[block + n] + step * log_grad)
                by_rate = by_rate * LN2 + mixed * by_map
                by_map = step * by_map
                if first == 0:
                    step_out[at, :] = by_rate
                    mixed_out[at, :] = by_map
                else:
                    step_out[at, :] += by_rate
                    mixed_out[at, :] += by_map
                return tuple(flows + sums)

            out = lax.fori_loop(0, steps, back, tuple(exits) + rate_sums, unroll=5)
            return out[block:]

        rate_sums = lax.fori_loop(0, halves, half, (zero,) * block)
        for n in range(block):
            rate_out[first + n : first + n + 1, :] = jnp.sum(rate_sums[n], 0, keepdims=True)

        for g in range(groups):
            turns = slots[2 * g + first // block]
            if turns:

                @pl.when(group == g)
                def _(turns=turns):
                    for turn in turns:
                        halving.turn(turn)

    @pl.when(group == groups - 1)
    def _():
        result = pltpu.make_async_copy(summed_early, early_out, own_sem.at[0])
        result.start()
        result.wait()
        for n in range(STATE):
            b_out[:, n : n + 1] = jnp.sum(b_sum[n], -1, keepdims=True)
            c_out[:, n : n + 1] = jnp.sum(c_sum[n], -1, keepdims=True)


class Scan:
    def __init__(self, rows, channels, halves):
        self.rows, self.channels, self.halves = rows, channels, halves
        self.groups = channels // LANES
        row_spec = pl.BlockSpec((rows, LANES), lambda g: (0, g))
        fixed = lambda *shape: pl.BlockSpec(shape, lambda g: (0,) * len(shape))
        self.row_spec = row_spec
        self.break_spec = fixed(rows, LANES)
        self.map_spec = fixed(rows, STATE)
        self.rate_spec = pl.BlockSpec((STATE, LANES), lambda g: (0, g))
        self.part_spec = pl.BlockSpec((halves, STATE, CHUNKS, LANES), lambda g: (0, 0, 0, g))
        self.sum_spec = pl.BlockSpec((halves, CHUNKS, LANES), lambda g: (0, 0, g))
        self.tot_spec = pl.BlockSpec((STATE + CHUNKS, LANES), lambda g: (0, g))
        self.skip_spec = pl.BlockSpec((1, LANES), lambda g: (0, g))
        self.row_f32 = jax.ShapeDtypeStruct((rows, channels), jnp.float32)
        self.part_f32 = jax.ShapeDtypeStruct((halves, STATE, CHUNKS, channels), jnp.float32)
        self.sum_f32 = jax.ShapeDtypeStruct((halves, CHUNKS, channels), jnp.float32)
        self.tot_f32 = jax.ShapeDtypeStruct((STATE + CHUNKS, channels), jnp.float32)
        self.wide = pltpu.VMEM((STATE, rows, LANES), jnp.float32)

    def params(self):
        return pltpu.CompilerParams(
            dimension_semantics=("arbitrary",), vmem_limit_bytes=VMEM_LIMIT
        )

    def cost(self, per_element):
        count = self.rows * self.channels * STATE
        return pl.CostEstimate(
            flops=per_element * count, bytes_accessed=12 * self.rows * self.channels, transcendentals=count
        )

    def ends(self, step, drive, breaks, maps, rates, blocks=None):
        anywhere = [pl.BlockSpec(memory_space=pl.ANY)]
        forward = blocks is not None
        places = expert_groups() + (lax.axis_size("chan"),)
        kernel = partial(ends_and_rows_kernel, self.halves, places) if forward else partial(ends_kernel, self.halves, True)
        params = self.params()
        if forward:
            params = pltpu.CompilerParams(
                dimension_semantics=("arbitrary",), vmem_limit_bytes=VMEM_LIMIT, collective_id=8,
                has_side_effects=True,
            )
        return pl.pallas_call(
            kernel,
            grid=(self.groups,),
            in_specs=[self.row_spec, self.row_spec, self.break_spec, self.map_spec, self.rate_spec]
            + anywhere * forward,
            out_specs=[self.part_spec, self.sum_spec, self.tot_spec] + anywhere * forward,
            out_shape=[self.part_f32, self.sum_f32, self.tot_f32]
            + ([jax.ShapeDtypeStruct(blocks.shape, blocks.dtype)] if forward else []),
            scratch_shapes=[self.wide] + (exchange_scratch(1) if forward else []),
            compiler_params=params,
            cost_estimate=self.cost(5),
            name="scan_ends" if forward else "scan_ends_back",
        )(step, drive, breaks, maps, rates, *([blocks] if forward else []))

    def outputs(self, step, mixed, breaks, b_in, c_out, rates, part, sums, device, skip, gate):
        return pl.pallas_call(
            partial(outputs_kernel, self.halves),
            grid=(self.groups,),
            in_specs=[
                self.row_spec, self.row_spec, self.break_spec, self.map_spec, self.map_spec, self.rate_spec,
                self.part_spec, self.sum_spec, self.rate_spec, self.skip_spec, self.row_spec,
            ],
            out_specs=[self.row_spec, self.row_spec, self.part_spec],
            out_shape=[
                self.row_f32,
                jax.ShapeDtypeStruct((self.rows, self.channels), jnp.bfloat16),
                self.part_f32,
            ],
            scratch_shapes=[self.wide, self.wide],
            compiler_params=self.params(),
            cost_estimate=self.cost(7),
            name="scan_outputs",
        )(step, mixed, breaks, b_in, c_out, rates, part, sums, device, skip, gate)

    def grads(self, step, mixed, breaks, grad, b_in, c_out, rates, entry, part, sums, device, early):
        count = lax.axis_size("seq")
        width, total = early[0].shape[1], early[0].shape[0] + early[1].shape[0]
        chunk = 16 * count
        total = -(-total // chunk) * chunk
        early = (early[0], jnp.pad(early[1], ((0, total - early[0].shape[0] - early[1].shape[0]), (0, 0))))
        chunks = total // chunk
        anywhere = pl.BlockSpec(memory_space=pl.ANY)
        steps = self.rows // (self.halves * CHUNKS)
        block = STATE // 2
        return pl.pallas_call(
            partial(grads_kernel, self.halves, count, self.groups),
            grid=(self.groups,),
            in_specs=[
                self.row_spec, self.row_spec, self.break_spec, self.row_spec, self.map_spec, self.map_spec,
                self.rate_spec, self.part_spec, self.part_spec, self.sum_spec, self.rate_spec, anywhere, anywhere,
            ],
            out_specs=[self.row_spec, self.row_spec, self.map_spec, self.map_spec, self.rate_spec, anywhere],
            out_shape=[
                self.row_f32,
                self.row_f32,
                jax.ShapeDtypeStruct((self.rows, STATE), jnp.float32),
                jax.ShapeDtypeStruct((self.rows, STATE), jnp.float32),
                jax.ShapeDtypeStruct((STATE, self.channels), jnp.float32),
                jax.ShapeDtypeStruct((chunks, chunk, width), jnp.bfloat16),
            ],
            scratch_shapes=[
                self.wide, self.wide, self.wide, self.wide,
                pltpu.VMEM((steps, block, CHUNKS, LANES), jnp.float32),
                pltpu.VMEM((steps + 1, block, CHUNKS, LANES), jnp.float32),
                pltpu.VMEM((chunks, chunk, width), jnp.bfloat16),
                *sum_scratch(chunks, chunk, width, count)[1:2],
                pltpu.VMEM((chunks, chunk, width), jnp.bfloat16),
                *sum_scratch(chunks, chunk, width, count)[2:],
                pltpu.SemaphoreType.DMA((chunks + 2,)),
            ],
            compiler_params=pltpu.CompilerParams(
                dimension_semantics=("arbitrary",), vmem_limit_bytes=VMEM_LIMIT, collective_id=7,
                has_side_effects=True,
            ),
            cost_estimate=self.cost(20),
            name="scan_grads",
        )(step, mixed, breaks, grad, b_in, c_out, rates, entry, part, sums, device, *early)


def over_tokens(values):
    return jnp.sum(jnp.sum(values, 0), -1, keepdims=True)


def sinkhorn_kernel(place_ref, logit_ref, route_ref, gate_ref, scaled_ref, row_ref, column_ref):
    probs = jnp.exp(logit_ref[...])
    for sweep in range(SINK):
        column = over_tokens(probs)
        scaled = probs / column[None]
        row = jnp.sum(scaled, 1, keepdims=True)
        scaled_ref[sweep] = scaled
        row_ref[sweep] = row
        column_ref[sweep] = jnp.broadcast_to(column, column_ref.shape[1:])
        probs = scaled / row
    place = place_ref[0]
    own = scaled_ref[SINK - 1, place] / row_ref[SINK - 1, place]
    ids = lax.broadcasted_iota(jnp.int32, own.shape, 0)
    gate_ref[...] = EXPERTS * jnp.sum(jnp.where(ids == route_ref[...], own, 0.0), 0, keepdims=True)


def sinkhorn_back_kernel(place_ref, logit_ref, scaled_ref, row_ref, column_ref, grad_ref, out_ref, held):
    grad = grad_ref[...]
    for sweep in reversed(range(SINK)):
        scaled, row = scaled_ref[sweep], row_ref[sweep]
        inner = jnp.sum(grad * (scaled / row), 1, keepdims=True)
        grad = (grad - inner) / row
        along = over_tokens(grad * scaled)
        grad = (grad - along[None]) / column_ref[sweep][:, 0:1][None]
    held[...] = grad
    place = place_ref[0]
    out_ref[...] = held[place] * jnp.exp(logit_ref[place])


def in_vmem(count):
    return [pl.BlockSpec(memory_space=pltpu.SMEM)] + [pl.BlockSpec(memory_space=pltpu.VMEM)] * count


def sinkhorn(place, logits, routes):
    devices, experts, tokens = logits.shape
    f32 = lambda *shape: jax.ShapeDtypeStruct(shape, jnp.float32)
    return pl.pallas_call(
        sinkhorn_kernel,
        in_specs=in_vmem(2),
        out_specs=in_vmem(4)[1:],
        out_shape=[
            f32(1, tokens),
            f32(SINK, devices, experts, tokens),
            f32(SINK, devices, 1, tokens),
            f32(SINK, experts, LANES),
        ],
        compiler_params=pltpu.CompilerParams(vmem_limit_bytes=VMEM_LIMIT),
        name="sinkhorn",
    )(place, logits, routes)


def sinkhorn_back(place, logits, scaled, rows, columns, grad):
    devices, experts, tokens = logits.shape
    return pl.pallas_call(
        sinkhorn_back_kernel,
        in_specs=in_vmem(5),
        out_specs=in_vmem(1)[1],
        out_shape=jax.ShapeDtypeStruct((experts, tokens), jnp.float32),
        scratch_shapes=[pltpu.VMEM(logits.shape, jnp.float32)],
        compiler_params=pltpu.CompilerParams(vmem_limit_bytes=VMEM_LIMIT),
        name="sinkhorn_back",
    )(place, logits, scaled, rows, columns, grad)


def expert_kernel(
    share, rows_ref, grad_ref, gate_ref, up_ref, down_ref, out_ref, back_ref, up_kept, up_sent, down_kept,
    down_sent, rows_t, grad_t, out_sum, back_sum, whole, half, held, sent, came, send_sem, recv_sem,
):
    step, last = pl.program_id(0), pl.num_programs(0) - 1
    features = up_ref.shape[2]
    me = lax.axis_index("seq")
    side, next_side = lax.rem(me, 2), lax.rem(lax.div(me, 2), 2)
    peer = {"seq": opposite(me, 1)}

    def copy(k):
        return pltpu.make_async_remote_copy(
            src_ref=sent.at[k], dst_ref=came.at[k], send_sem=send_sem.at[k], recv_sem=recv_sem.at[k],
            device_id=peer, device_id_type=MESH,
        )

    @pl.when(step == 0)
    def _():
        greet([peer])
        rows_t[...] = rows_ref[...].T
        grad_t[...] = (grad_ref[...].astype(jnp.float32) * gate_ref[...]).astype(jnp.bfloat16).T

    def halved_rows(total, which):
        whole[...] = total
        for k in range(half.shape[0] // features):
            low = whole[2 * k * features : (2 * k + 1) * features]
            high = whole[(2 * k + 1) * features : (2 * k + 2) * features]
            half[k * features : (k + 1) * features] = jnp.where(which == 0, low, high)
        return half[...].astype(jnp.bfloat16)

    def dot(a, b, over=((1,), (0,))):
        return lax.dot_general(a, b, (over, ((), ())), preferred_element_type=jnp.float32)

    def joined(ref):
        for q in range(ref.shape[0]):
            for j in range(ref.shape[1]):
                first = (j * ref.shape[0] + q) * features
                whole[first : first + features] = ref[q, j].astype(jnp.float32)
        return whole[...].astype(jnp.bfloat16)

    def send(k, total):
        held[k] = halved_rows(total, side)
        sent[k] = halved_rows(total, 1 - side)
        copy(k).start()

    @pl.when(step < last)
    def _():
        across = ((1,), (1,))
        up, down = joined(up_ref), joined(down_ref)
        pre = dot(rows_ref[...], up)
        square = pre * pre
        bend = jnp.tanh(GELU_SCALE * (pre + GELU_CUBE * pre * square))
        rise = 0.5 * (1.0 + bend)
        act = (pre * rise).astype(jnp.bfloat16)
        slope = rise + 0.5 * pre * (1.0 - bend * bend) * (GELU_SCALE + 3.0 * GELU_SCALE * GELU_CUBE * square)
        grad_pre = dot(grad_ref[...], down) * slope
        out_part, back_part = dot(act, down, across), dot(grad_pre.astype(jnp.bfloat16), up, across)

        @pl.when(step == 0)
        def _():
            out_sum[...] = out_part
            back_sum[...] = back_part

        @pl.when(step > 0)
        def _():
            out_sum[...] += out_part
            back_sum[...] += back_part

        send(2 * step, dot(grad_t[...], act))
        send(2 * step + 1, dot(rows_t[...], (grad_pre * gate_ref[...]).astype(jnp.bfloat16)))

    @pl.when(step > 0)
    def _():
        for odd, kept_ref, sent_ref in ((0, down_kept, down_sent), (1, up_kept, up_sent)):
            k = 2 * (step - 1) + odd
            copy(k).wait()
            total = held[k].astype(jnp.float32) + came[k].astype(jnp.float32)
            half[...] = total
            for g in range(half.shape[0] // (2 * features)):
                low = half[2 * g * features : (2 * g + 1) * features]
                high = half[(2 * g + 1) * features : (2 * g + 2) * features]
                kept_ref[g] = jnp.where(next_side == 0, low, high).astype(kept_ref.dtype)
                sent_ref[g] = jnp.where(next_side == 0, high, low).astype(sent_ref.dtype)

    @pl.when(step == last)
    def _():
        out_ref[...] = out_sum[...].astype(out_ref.dtype)
        back_ref[...] = back_sum[...].astype(back_ref.dtype)


def expert_passes(rows, grad, gate, up, down):
    count, width = rows.shape
    share, own, features, hidden = up.shape
    tile = 512
    tiles = hidden // tile
    blocks = width // (4 * features)
    fixed = lambda *shape: pl.BlockSpec(shape, lambda k: (0,) * len(shape))
    weight_spec = pl.BlockSpec(
        (share, own, features, tile), lambda k: (0, 0, 0, jnp.minimum(k, tiles - 1))
    )
    part_spec = pl.BlockSpec((blocks, features, tile), lambda k: (0, 0, jnp.maximum(k - 1, 0)))
    part_shape = jax.ShapeDtypeStruct((blocks, features, hidden), jnp.bfloat16)
    row_shape = jax.ShapeDtypeStruct((count, width), jnp.bfloat16)
    return pl.pallas_call(
        partial(expert_kernel, share),
        grid=(tiles + 1,),
        in_specs=[
            fixed(count, width), fixed(count, width), fixed(count, 1), weight_spec, weight_spec,
        ],
        out_specs=[fixed(count, width), fixed(count, width)] + [part_spec] * 4,
        out_shape=[row_shape, row_shape] + [part_shape] * 4,
        scratch_shapes=[
            pltpu.VMEM((width, count), jnp.bfloat16),
            pltpu.VMEM((width, count), jnp.bfloat16),
            pltpu.VMEM((count, width), jnp.float32),
            pltpu.VMEM((count, width), jnp.float32),
            pltpu.VMEM((width, tile), jnp.float32),
            pltpu.VMEM((width // 2, tile), jnp.float32),
            pltpu.VMEM((2 * tiles, width // 2, tile), jnp.bfloat16),
            pltpu.VMEM((2 * tiles, width // 2, tile), jnp.bfloat16),
            pltpu.VMEM((2 * tiles, width // 2, tile), jnp.bfloat16),
            pltpu.SemaphoreType.DMA((2 * tiles,)),
            pltpu.SemaphoreType.DMA((2 * tiles,)),
        ],
        compiler_params=pltpu.CompilerParams(
            dimension_semantics=("arbitrary",), vmem_limit_bytes=VMEM_LIMIT, collective_id=9,
            has_side_effects=True,
        ),
        cost_estimate=pl.CostEstimate(
            flops=12 * count * width * hidden, bytes_accessed=8 * width * hidden, transcendentals=count * hidden
        ),
        name="expert_passes",
    )(rows, grad, gate, up, down)


def on_device(
    block_in,
    routes,
    doc_lengths,
    norm_gain,
    in_weight,
    conv_weight,
    conv_bias,
    xproj_weight,
    dt_weight,
    dt_bias,
    a_log,
    skip_gain,
    out_weight,
    moe_gain,
    router_weight,
    up_weight,
    down_weight,
    out_grad,
):
    tok_dev, model_width = block_in.shape
    chan_count = lax.axis_size("chan")
    chan_place, seq_place = lax.axis_index("chan"), lax.axis_index("seq")
    dev_ref = (seq_place * chan_count + chan_place).astype(jnp.int32).reshape(1)
    steps = tok_dev // CHUNKS
    tok_seq = tok_dev * chan_count
    channels = in_weight.shape[2]
    padded_channels = -(-channels // LANES) * LANES
    f32, bf16 = jnp.float32, jnp.bfloat16

    route_col = routes[:, 0]
    expert_ids = lax.broadcasted_iota(jnp.int32, (1, EXPERTS), 1)
    chosen = (route_col[:, None] == expert_ids).astype(bf16)
    row_ids = lax.broadcasted_iota(jnp.int32, (tok_dev, tok_dev), 0)
    col_ids = lax.broadcasted_iota(jnp.int32, (tok_dev, tok_dev), 1)
    counts = jnp.dot((col_ids <= row_ids).astype(bf16), chosen, preferred_element_type=f32)
    rank = (jnp.sum(counts * chosen.astype(f32), 1) - 1.0).astype(jnp.int32)
    capacity = tok_dev * 5 // (4 * EXPERTS) + 1
    capacity = -(-capacity // 16) * 16
    slot = to_steps(route_col * capacity + rank)
    route_steps = to_steps(route_col)
    slot_ids = lax.broadcasted_iota(jnp.int32, (1, EXPERTS * capacity), 1)
    placer = (slot[:, None] == slot_ids).astype(bf16)

    def pack(values):
        rows = jnp.einsum("ts,td->sd", placer, values, preferred_element_type=f32).astype(bf16)
        return rows.reshape(EXPERTS, capacity, model_width)

    def unpack(values):
        return jnp.einsum(
            "ts,sd->td",
            placer,
            values.reshape(EXPERTS * capacity, model_width),
            preferred_element_type=f32,
        )

    block_steps = to_steps(block_in)
    grad_steps = to_steps(out_grad)
    residual = block_steps.astype(f32)
    normed, norm_back = jax.vjp(norm_apply, residual, norm_gain)
    gathered = chan_rows(normed.astype(bf16))

    inner_b = jnp.dot(gathered, in_weight[0], preferred_element_type=f32).astype(bf16)
    gate_z = jnp.dot(gathered, in_weight[1], preferred_element_type=f32)

    shape4 = (chan_count, steps, CHUNKS)
    ids = [lax.broadcasted_iota(jnp.int32, shape4, axis) for axis in range(3)]
    position = seq_place * tok_seq + ids[0] * tok_dev + ids[2] * steps + ids[1]
    starts = jnp.cumsum(doc_lengths) - doc_lengths
    doc_first = jnp.max(
        jnp.where(starts <= position[..., None], starts, 0), axis=-1
    )
    reach = CONV - 1
    inner = inner_b.astype(f32).reshape(shape4 + (channels,))
    tails = jnp.swapaxes(inner[:, steps - reach :], 0, 1).reshape(reach, chan_count * CHUNKS, channels)
    previous = passed_along(tails[:, -1], "seq", 1)
    heads = jnp.concatenate([previous[:, None], tails[:, :-1]], 1)
    heads = jnp.swapaxes(heads.reshape(reach, chan_count, CHUNKS, channels), 0, 1)
    padded = jnp.concatenate([heads, inner], 1)
    masks = [
        (position - (reach - offset) >= doc_first).astype(f32)[..., None] for offset in range(CONV)
    ]
    conv_pre = conv_bias
    for offset in range(CONV):
        conv_pre = conv_pre + conv_weight[offset] * padded[:, offset : offset + steps] * masks[offset]
    conv_pre = conv_pre.reshape(tok_seq, channels)
    mixed_b = jax.nn.silu(conv_pre).astype(bf16)
    mixed = mixed_b.astype(f32)
    proj_all = proj_total(jnp.dot(mixed_b, xproj_weight, preferred_element_type=f32))
    low_rank = proj_all[:, :DT_RANK]
    b_in = proj_all[:, DT_RANK : DT_RANK + STATE]
    c_out = proj_all[:, DT_RANK + STATE :]
    step_pre = jnp.dot(low_rank, dt_weight, precision=HIGH) + dt_bias
    step_size = jax.nn.softplus(step_pre)

    def widened(values, axis=-1):
        more = padded_channels - channels
        if not more:
            return values
        pads = [(0, 0)] * values.ndim
        pads[axis] = (0, more)
        return jnp.pad(values, pads)

    scan = Scan(tok_seq, padded_channels, chan_count)
    decay_rates = jnp.exp(a_log)
    rates = widened((-LOG2E * decay_rates).T)
    breaks = jnp.any(position[..., None] == starts, axis=-1).astype(f32) * BREAK
    breaks = jnp.broadcast_to(breaks.reshape(tok_seq, 1), (tok_seq, LANES))
    step_w, mixed_w = widened(step_size), widened(mixed)
    part, sums, total, grad_arrived = scan.ends(step_w, mixed_w, breaks, b_in, rates, pack(grad_steps))
    grad_arrived = grad_arrived.reshape(-1, model_width)
    device_entry = carried(total, rates, False)
    full_up = whole_expert(up_weight, None, device_entry)
    scan_out, gated_b, entry = scan.outputs(
        step_w, mixed_w, breaks, b_in, c_out, rates, part, sums, device_entry,
        widened(skip_gain[None]), widened(gate_z),
    )
    scan_out, gated_b = scan_out[:, :channels], gated_b[:, :channels]
    full_down = whole_expert(down_weight, device_entry, gated_b)

    mixer_rows = chan_sums(
        lambda rows: jnp.dot(rows, out_weight, preferred_element_type=f32), gated_b
    )
    hidden_one = residual + mixer_rows
    moe_in, moe_back = jax.vjp(norm_apply, hidden_one, moe_gain)
    logits = jnp.einsum("td,de->et", moe_in, router_weight, precision=HIGH)
    every_logit = gathered_everywhere(3, logits)
    gate_row, scaled, row_totals, columns = sinkhorn(
        dev_ref, every_logit, route_steps.reshape(1, tok_dev)
    )
    gate = gate_row.reshape(tok_dev)

    gate_slots = jnp.einsum("ts,t->s", placer.astype(f32), gate, precision=HIGH)
    gate_slots = jnp.pad(gate_slots.reshape(EXPERTS, 1, capacity), ((0, 0), (0, 7), (0, LANES - capacity)))
    arrived, gate_arrived = expert_rows(1, pack(moe_in.astype(bf16)), gate_slots)
    arrived = arrived.reshape(-1, model_width)
    gate_arrived = gate_arrived[:, 0, :capacity].reshape(-1, 1)
    own, share = expert_groups()
    features, hidden = up_weight.shape[1:]
    expert_out, grad_rows_in, up_kept, up_sent, down_kept, down_sent = expert_passes(
        arrived, grad_arrived, gate_arrived, full_up, full_down
    )
    blocks = (EXPERTS, capacity, model_width)
    expert_back, grad_back = expert_rows(2, expert_out.reshape(blocks), grad_rows_in.reshape(blocks))
    expert_grads = [
        added(kept, swapped(sent, "seq", 2)).reshape(own, share // 4, features, hidden)
        for kept, sent in ((up_kept, up_sent), (down_kept, down_sent))
    ]
    for stage in range(2, share.bit_length() - 1):
        expert_grads = [halved(part, stage) for part in expert_grads]
    expert_tok = unpack(expert_back)
    plain_grad_part = unpack(grad_back)
    up_part, down_part = expert_grads

    block_out = from_steps((hidden_one + gate[:, None] * expert_tok).astype(bf16))
    grad_two = grad_steps.astype(f32)
    grad_gate = jnp.sum(expert_tok * grad_two, 1)
    grad_probs = jnp.where(
        route_steps[None] == lax.broadcasted_iota(jnp.int32, (EXPERTS, 1), 0),
        EXPERTS * grad_gate[None],
        0.0,
    )
    every_grad, up_part = gathered_everywhere(10, grad_probs, up_part)
    up_grad = to_owners(up_part.reshape(own, *up_part.shape[2:]))
    grad_logits = sinkhorn_back(dev_ref, every_logit, scaled, row_totals, columns, every_grad)
    router_grad = jnp.einsum("td,et->ed", moe_in, grad_logits, precision=HIGH)
    grad_moe_in = gate[:, None] * plain_grad_part + jnp.einsum(
        "et,de->td", grad_logits, router_weight, precision=HIGH
    )
    grad_hidden, moe_gain_grad = moe_back(grad_moe_in)
    grad_hidden = grad_hidden + grad_two

    grad_mix = chan_rows(grad_hidden.astype(bf16))
    grad_gated = jnp.einsum("td,ed->te", grad_mix, out_weight, preferred_element_type=f32)
    out_weight_grad = jnp.einsum("te,td->ed", gated_b, grad_mix, preferred_element_type=f32)
    grad_scan = grad_gated * jax.nn.silu(gate_z)
    grad_gate_z = (grad_gated * scan_out * silu_grad(gate_z)).astype(bf16)
    skip_grad = jnp.sum(grad_scan * mixed, 0)
    gate_weight_grad = jnp.einsum("td,te->de", gathered, grad_gate_z, preferred_element_type=f32)
    gains = jnp.concatenate([moe_gain_grad[None], router_grad], 0)
    gains = lax.psum(gains, "chan") if chan_count != 2 else gains + swapped(gains, "chan", 1)
    grad_scan_w = widened(grad_scan)
    back_part, back_sums, back_total = scan.ends(step_w, grad_scan_w, breaks, c_out, rates)
    back_entry = carried(back_total, rates, True, up_grad, down_part)
    step_grad, mixed_grad, b_grad, c_grad, rate_grad, early = scan.grads(
        step_w, mixed_w, breaks, grad_scan_w, b_in, c_out, rates, entry, back_part, back_sums,
        back_entry, (out_weight_grad.astype(bf16).reshape(-1, channels), gate_weight_grad.astype(bf16)),
    )
    early = early.reshape(-1, channels)
    down_grad = to_owners(after(down_part.reshape(own, *down_part.shape[2:]), step_grad))
    step_grad, mixed_grad = step_grad[:, :channels], mixed_grad[:, :channels]
    mixed_grad = mixed_grad + skip_gain * grad_scan
    a_log_rows = -decay_rates.T * rate_grad[:, :channels]
    step_pre_grad = step_grad * jax.nn.sigmoid(step_pre)
    dt_bias_grad = jnp.sum(step_pre_grad, 0)
    dt_weight_grad = jnp.einsum("tr,te->re", low_rank, step_pre_grad, precision=HIGH)
    rank_grad = jnp.einsum("te,re->tr", step_pre_grad, dt_weight, precision=HIGH)
    proj_grad_b = proj_total(jnp.concatenate([rank_grad, b_grad, c_grad], 1)).astype(bf16)
    mixed_grad = mixed_grad + jnp.einsum(
        "tp,ep->te", proj_grad_b, xproj_weight, preferred_element_type=f32
    )
    xproj_rows = jnp.einsum("te,tp->pe", mixed_b, proj_grad_b, preferred_element_type=f32)
    conv_grad = (mixed_grad * silu_grad(conv_pre)).reshape(shape4 + (channels,))
    conv_bias_grad = jnp.sum(conv_grad, (0, 1, 2))
    conv_weight_grad = jnp.stack(
        [
            jnp.sum(conv_grad * masks[offset] * padded[:, offset : offset + steps], (0, 1, 2))
            for offset in range(CONV)
        ]
    )
    padded_grad = 0.0
    for offset in range(CONV):
        padded_grad = padded_grad + jnp.pad(
            conv_weight[offset] * conv_grad * masks[offset],
            ((0, 0), (offset, reach - offset), (0, 0), (0, 0)),
        )
    head_grad = jnp.swapaxes(padded_grad[:, :reach], 0, 1).reshape(
        reach, chan_count * CHUNKS, channels
    )
    from_next = passed_along(head_grad[:, 0], "seq", -1)
    tail_grad = jnp.concatenate([head_grad[:, 1:], from_next[:, None]], 1)
    tail_grad = jnp.swapaxes(tail_grad.reshape(reach, chan_count, CHUNKS, channels), 0, 1)
    inner_grad = padded_grad[:, reach:] + jnp.pad(
        tail_grad, ((0, 0), (steps - reach, 0), (0, 0), (0, 0))
    )
    inner_grad_b = inner_grad.reshape(tok_seq, channels).astype(bf16)
    inner_weight_grad = jnp.einsum("td,te->de", gathered, inner_grad_b, preferred_element_type=f32)
    both_grad = jnp.concatenate([inner_grad_b, grad_gate_z], 1)
    normed_grad = chan_sums(
        lambda rows: jnp.dot(rows[:, :channels], in_weight[0].T, preferred_element_type=f32)
        + jnp.dot(rows[:, channels:], in_weight[1].T, preferred_element_type=f32),
        both_grad,
    )
    residual_grad, norm_gain_grad = norm_back(normed_grad)
    in_grad = from_steps(residual_grad + grad_hidden)

    norm_rows = norm_gain_grad[None]
    norm_rows = lax.psum(norm_rows, "chan") if chan_count != 2 else norm_rows + swapped(norm_rows, "chan", 1)
    pieces = (
        xproj_rows, dt_weight_grad, a_log_rows, conv_weight_grad, conv_bias_grad[None], dt_bias_grad[None],
        skip_grad[None], norm_rows.reshape(-1, channels), gains.reshape(-1, channels),
    )
    bounds = [sum(part.shape[0] for part in pieces[: k + 1]) for k in range(len(pieces) - 1)]
    inner_weight_grad, small = summed([after(inner_weight_grad.astype(bf16), down_grad), jnp.concatenate(pieces, 0)])
    out_weight_grad = early[:model_width].reshape(channels, model_width).astype(f32)
    gate_weight_grad = early[model_width : 2 * model_width].astype(f32)
    (
        xproj_rows, dt_weight_grad, a_log_rows, conv_weight_grad, conv_bias_grad, dt_bias_grad, skip_grad,
        norm_rows, gains,
    ) = jnp.split(small, bounds, 0)
    norm_gain_grad, gains = norm_rows.reshape(-1), gains.reshape(-1, model_width)
    xproj_grad, a_log_grad = xproj_rows.T, a_log_rows.T
    conv_bias_grad, dt_bias_grad, skip_grad = conv_bias_grad[0], dt_bias_grad[0], skip_grad[0]
    moe_gain_grad, router_grad = gains[0], gains[1:].T
    in_weight_grad = jnp.stack([inner_weight_grad, gate_weight_grad])
    return (
        block_out,
        in_grad,
        norm_gain_grad,
        in_weight_grad,
        conv_weight_grad,
        conv_bias_grad,
        xproj_grad,
        dt_weight_grad,
        dt_bias_grad,
        a_log_grad,
        skip_grad,
        out_weight_grad,
        moe_gain_grad,
        router_grad,
        up_grad.astype(f32),
        down_grad.astype(f32),
    )


def solution(mesh):
    in_specs = (
        P(("seq", "chan"), None),
        P(("seq", "chan"), None),
        P(),
        P(),
        P(None, None, "chan"),
        P(None, "chan"),
        P("chan"),
        P("chan", None),
        P(None, "chan"),
        P("chan"),
        P("chan", None),
        P("chan"),
        P("chan", None),
        P(),
        P(),
        P("chan", "seq", None),
        P("chan", "seq", None),
        P(("seq", "chan"), None),
    )
    out_specs = (
        P(("seq", "chan"), None),
        P(("seq", "chan"), None),
        P(),
        P(None, None, "chan"),
        P(None, "chan"),
        P("chan"),
        P("chan", None),
        P(None, "chan"),
        P("chan"),
        P("chan", None),
        P("chan"),
        P("chan", None),
        P(),
        P(),
        P("chan", "seq", None),
        P("chan", "seq", None),
    )
    return jax.shard_map(
        on_device, mesh=mesh, in_specs=in_specs, out_specs=out_specs, check_vma=False
    )
```

```python
from functools import partial

import jax
import jax.numpy as jnp
from jax import lax
from jax.experimental import pallas as pl
from jax.experimental.pallas import tpu as pltpu
from jax.sharding import PartitionSpec as P

STATE = 16
CONV = 4
DT_RANK = 72
EXPERTS = 8
SINK = 8
CHUNKS = 8
LANES = 128
VMEM_LIMIT = 56 * 1024 * 1024

EPS = 1e-05
HIGH = lax.Precision.HIGHEST
LOG2E = 1.4426950408889634
LN2 = 0.6931471805599453
BREAK = 1e30
MESH = pl.DeviceIdType.MESH
GELU_SCALE = 0.7978845608028654
GELU_CUBE = 0.044715


def passed_along(value, axis, steps):
    count = lax.axis_size(axis)
    leading, last = (max(0, -steps), min(count, count - steps))
    return lax.ppermute(value, axis, [(source, source + steps) for source in range(leading, last)])


def swapped(value, axis, bit):
    count = lax.axis_size(axis)
    return lax.ppermute(value, axis, [(source, source ^ bit) for source in range(count)])


def chan_rows(values):
    if lax.axis_size("chan") != 2:
        return lax.all_gather(values, "chan", axis=0, tiled=True)
    first = lax.axis_index("chan") == 0
    other = swapped(values, "chan", 1)
    return jnp.concatenate([jnp.where(first, values, other), jnp.where(first, other, values)], 0)


def chan_sums(term_fn, operand):
    count, place = lax.axis_size("chan"), lax.axis_index("chan")
    rows = operand.shape[0] // count
    if count != 2:
        return lax.psum_scatter(term_fn(operand), "chan", scatter_dimension=0, tiled=True)
    theirs = term_fn(lax.dynamic_slice_in_dim(operand, (1 - place) * rows, rows, 0))
    arrived = swapped(theirs.astype(jnp.bfloat16), "chan", 1)
    return term_fn(lax.dynamic_slice_in_dim(operand, place * rows, rows, 0)) + arrived.astype(
        jnp.float32
    )


def proj_total(values):
    if lax.axis_size("chan") != 2:
        return lax.psum(values, "chan")
    return values + swapped(values, "chan", 1)


def expert_groups():
    own = EXPERTS // lax.axis_size("chan")
    return own, lax.axis_size("seq") // own


def across_experts(values, axis, wait=None):
    own, share = expert_groups()
    place = lax.div(lax.axis_index("seq"), share)
    out = values
    for d in range(1, own):
        peer = lax.bitwise_xor(place, d)
        came = swapped(lax.dynamic_slice_in_dim(values, peer, 1, axis), "seq", d * share)
        if wait is not None:
            came = after(came, wait)
        out = lax.dynamic_update_slice_in_dim(out, came, peer, axis)
    return out


def to_owners(grad):
    own, share = expert_groups()
    if own == 1:
        return grad
    groups = [[k * share + q for k in range(own)] for q in range(share)]
    return lax.all_to_all(
        grad, "seq", split_axis=0, concat_axis=0, tiled=True, axis_index_groups=groups
    )


def expert_rows(ident, *arrays):
    return exchange(ident, arrays)


def whole_expert(weight, start, wait):
    own, share = expert_groups()
    features, hidden = weight.shape[1:]
    if start is not None:
        weight = after(weight, start)
    mine = across_experts(weight, 0, wait)
    groups = [[k * share + q for q in range(share)] for k in range(own)]
    return lax.all_gather(mine, "seq", axis_index_groups=groups)


def halved(grad, stage):
    own, share = expert_groups()
    bit = 1 << stage
    pairs = grad.reshape(own, grad.shape[1] // 2, 2, *grad.shape[2:])
    side = lax.rem(lax.div(lax.axis_index("seq"), bit), 2)
    sent = lax.dynamic_index_in_dim(pairs, 1 - side, 2, False)
    kept = lax.dynamic_index_in_dim(pairs, side, 2, False)
    came = swapped(sent, "seq", bit)
    return added(kept, came)


def added(kept, came):
    return (kept.astype(jnp.float32) + came.astype(jnp.float32)).astype(kept.dtype)


def after(value, *others):
    return lax.optimization_barrier((value,) + others)[0]


def lasting(microseconds):
    return pl.CostEstimate(flops=0, bytes_accessed=microseconds * 3_600_000, transcendentals=0)


def opposite(place, bit):
    return place + bit - 2 * bit * lax.rem(lax.div(place, bit), 2)


def greet(targets):
    barrier = pltpu.get_barrier_semaphore()
    for target in targets:
        pl.semaphore_signal(barrier, inc=1, device_id=target, device_id_type=MESH)
    pl.semaphore_wait(barrier, len(targets))


class Exchange:
    def __init__(self, own, share, chans, sources, results, send_sem, recv_sem, own_sem):
        seq, chan = lax.axis_index("seq"), lax.axis_index("chan")
        column = lax.rem(seq, share)
        me = chan * own + lax.div(seq, share)
        total = own * chans
        peers = [lax.rem(me + d, total) for d in range(1, total)]
        self.targets = [(lax.rem(peer, own) * share + column, lax.div(peer, own)) for peer in peers]
        self.copies = []
        for k, (source, result) in enumerate(zip(sources, results)):
            for d in range(total - 1):
                self.copies.append(
                    pltpu.make_async_remote_copy(
                        src_ref=source.at[peers[d]],
                        dst_ref=result.at[me],
                        send_sem=send_sem.at[k, d],
                        recv_sem=recv_sem.at[k, d],
                        device_id=self.targets[d],
                        device_id_type=MESH,
                    )
                )
            self.copies.append(pltpu.make_async_copy(source.at[me], result.at[me], own_sem.at[k]))

    def start(self):
        greet(self.targets)
        for copy in self.copies:
            copy.start()

    def wait(self):
        for copy in self.copies:
            copy.wait()


def exchange_scratch(count):
    others = expert_groups()[0] * lax.axis_size("chan") - 1
    return [
        pltpu.SemaphoreType.DMA((count, others)),
        pltpu.SemaphoreType.DMA((count, others)),
        pltpu.SemaphoreType.DMA((count,)),
    ]


def exchange_kernel(own, share, chans, count, *refs):
    rows = Exchange(own, share, chans, refs[:count], refs[count : 2 * count], *refs[2 * count :])
    rows.start()
    rows.wait()


def exchange(ident, arrays):
    own, share = expert_groups()
    chans, count = lax.axis_size("chan"), len(arrays)
    anywhere = pl.BlockSpec(memory_space=pl.ANY)
    return pl.pallas_call(
        partial(exchange_kernel, own, share, chans, count),
        in_specs=[anywhere] * count,
        out_specs=[anywhere] * count,
        out_shape=[jax.ShapeDtypeStruct(part.shape, part.dtype) for part in arrays],
        scratch_shapes=exchange_scratch(count),
        compiler_params=pltpu.CompilerParams(collective_id=ident, has_side_effects=True),
        cost_estimate=lasting(26 * count),
        name="expert_rows",
    )(*arrays)


class Gather:
    def __init__(self, devices, chans, own_ref, every_ref, send_sem, recv_sem):
        self.devices, self.chans = devices, chans
        self.own_ref, self.every_ref = own_ref, every_ref
        self.send_sem, self.recv_sem = send_sem, recv_sem
        self.me = lax.axis_index("seq") * chans + lax.axis_index("chan")

    def target(self, d):
        peer = lax.rem(self.me + d, self.devices)
        return (lax.div(peer, self.chans), lax.rem(peer, self.chans))

    def copy(self, d):
        return pltpu.make_async_remote_copy(
            src_ref=self.own_ref,
            dst_ref=self.every_ref.at[self.me],
            send_sem=self.send_sem.at[d - 1],
            recv_sem=self.recv_sem.at[d - 1],
            device_id=self.target(d),
            device_id_type=MESH,
        )

    def each(self, act):
        def turn(d, carry):
            act(d)
            return carry

        lax.fori_loop(1, self.devices, turn, 0)

    def greet(self):
        barrier = pltpu.get_barrier_semaphore()
        self.each(
            lambda d: pl.semaphore_signal(barrier, inc=1, device_id=self.target(d), device_id_type=MESH)
        )
        self.every_ref[self.me] = self.own_ref[...]
        pl.semaphore_wait(barrier, self.devices - 1)

    def start(self):
        self.each(lambda d: self.copy(d).start())

    def wait(self):
        self.each(lambda d: self.copy(d).wait())


def gather_kernel(devices, chans, passed, own_ref, *refs):
    gather = Gather(devices, chans, own_ref, refs[passed], refs[-2], refs[-1])
    gather.greet()
    gather.start()
    gather.wait()


def rows_and_gather_kernel(
    places, devices, source, own_ref, result, every_ref, rows_send, rows_recv, rows_own, send_sem, recv_sem
):
    gather = Gather(devices, places[2], own_ref, every_ref, send_sem, recv_sem)
    rows = Exchange(*places, [source], [result], rows_send, rows_recv, rows_own)
    gather.greet()
    gather.start()
    for copy in rows.copies:
        copy.start()
    gather.wait()
    rows.wait()


def rows_and_gather(packed, values):
    chans = lax.axis_size("chan")
    devices = lax.axis_size("seq") * chans
    vmem, anywhere = pl.BlockSpec(memory_space=pltpu.VMEM), pl.BlockSpec(memory_space=pl.ANY)
    return pl.pallas_call(
        partial(rows_and_gather_kernel, expert_groups() + (chans,), devices),
        in_specs=[anywhere, vmem],
        out_specs=[anywhere, vmem],
        out_shape=[
            jax.ShapeDtypeStruct(packed.shape, packed.dtype),
            jax.ShapeDtypeStruct((devices,) + values.shape, values.dtype),
        ],
        scratch_shapes=exchange_scratch(1)
        + [pltpu.SemaphoreType.DMA((devices - 1,)), pltpu.SemaphoreType.DMA((devices - 1,))],
        compiler_params=pltpu.CompilerParams(
            collective_id=1, has_side_effects=True, vmem_limit_bytes=VMEM_LIMIT
        ),
        cost_estimate=lasting(34),
        name="rows_and_gather",
    )(packed, values)


def gathered_everywhere(ident, values, *passed):
    chans = lax.axis_size("chan")
    devices = lax.axis_size("seq") * chans
    vmem, anywhere = pl.BlockSpec(memory_space=pltpu.VMEM), pl.BlockSpec(memory_space=pl.ANY)
    out = pl.pallas_call(
        partial(gather_kernel, devices, chans, len(passed)),
        in_specs=[vmem] + [anywhere] * len(passed),
        out_specs=[vmem] + [anywhere] * len(passed),
        out_shape=[jax.ShapeDtypeStruct((devices,) + values.shape, values.dtype)]
        + [jax.ShapeDtypeStruct(part.shape, part.dtype) for part in passed],
        input_output_aliases={1 + k: 1 + k for k in range(len(passed))},
        scratch_shapes=[
            pltpu.SemaphoreType.DMA((devices - 1,)),
            pltpu.SemaphoreType.DMA((devices - 1,)),
        ],
        compiler_params=pltpu.CompilerParams(
            collective_id=ident, has_side_effects=True, vmem_limit_bytes=VMEM_LIMIT
        ),
        cost_estimate=lasting(12),
        name="gather_small",
    )(values, *passed)
    return out if passed else out[0]


def carry_kernel(count, reverse, total_ref, rate_ref, *refs):
    entry_ref, ends_out, ends_in, sums_out, sums_in, ends_sems, sums_sems = refs[-7:]
    me = lax.axis_index("seq")
    bits = [1 << k for k in range(count.bit_length() - 1)]
    greet([{"seq": opposite(me, bit)} for bit in bits])
    rates = rate_ref[...]
    ends, sums = total_ref[:STATE], total_ref[STATE : STATE + 1]
    before, before_sum = jnp.zeros_like(ends), jnp.zeros_like(sums)
    for k, bit in enumerate(bits):
        ends_out[k] = ends.astype(ends_out.dtype)
        sums_out[k] = sums
        copies = [
            pltpu.make_async_remote_copy(
                src_ref=out.at[k],
                dst_ref=into.at[k],
                send_sem=sems.at[0, k],
                recv_sem=sems.at[1, k],
                device_id={"seq": opposite(me, bit)},
                device_id_type=MESH,
            )
            for out, into, sems in ((ends_out, ends_in, ends_sems), (sums_out, sums_in, sums_sems))
        ]
        for copy in copies:
            copy.start()
        for copy in copies:
            copy.wait()
        their_ends, their_sums = ends_in[k].astype(jnp.float32), sums_in[k]
        theirs_first = lax.rem(lax.div(me, bit), 2) == (0 if reverse else 1)
        before = jnp.where(theirs_first, jnp.exp2(rates * before_sum) * their_ends + before, before)
        before_sum = jnp.where(theirs_first, before_sum + their_sums, before_sum)
        ends = jnp.where(
            theirs_first,
            jnp.exp2(rates * sums) * their_ends + ends,
            jnp.exp2(rates * their_sums) * ends + their_ends,
        )
        sums = sums + their_sums
    entry_ref[...] = before


def carried(total, rates, reverse, *needed):
    count = lax.axis_size("seq")
    rounds = count.bit_length() - 1
    channels = rates.shape[1]
    vmem = pl.BlockSpec(memory_space=pltpu.VMEM)
    return pl.pallas_call(
        partial(carry_kernel, count, reverse),
        in_specs=[vmem, vmem] + [pl.BlockSpec(memory_space=pl.ANY)] * len(needed),
        out_specs=vmem,
        out_shape=jax.ShapeDtypeStruct(rates.shape, jnp.float32),
        scratch_shapes=[
            pltpu.VMEM((rounds, STATE, channels), jnp.bfloat16),
            pltpu.VMEM((rounds, STATE, channels), jnp.bfloat16),
            pltpu.VMEM((rounds, 1, channels), jnp.float32),
            pltpu.VMEM((rounds, 1, channels), jnp.float32),
            pltpu.SemaphoreType.DMA((2, rounds)),
            pltpu.SemaphoreType.DMA((2, rounds)),
        ],
        compiler_params=pltpu.CompilerParams(
            collective_id=5 if reverse else 4, has_side_effects=True, vmem_limit_bytes=VMEM_LIMIT
        ),
        cost_estimate=lasting(14),
        name="carry_back" if reverse else "carry",
    )(total, rates, *needed)


class Halving:
    def __init__(self, count, held, incoming, result, send_sem, recv_sem):
        self.held, self.incoming, self.result = held, incoming, result
        self.send_sem, self.recv_sem = send_sem, recv_sem
        self.chunks, self.rows = held.shape[0], held.shape[1]
        me = lax.axis_index("seq")
        bits = [1 << k for k in range(count.bit_length() - 1)]
        self.rounds = len(bits)
        self.peers = [{"seq": opposite(me, bit)} for bit in bits]
        self.sides = [lax.rem(lax.div(me, bit), 2) for bit in bits]
        self.lows, self.lengths = [0], [self.rows]
        for side in self.sides:
            self.lengths.append(self.lengths[-1] // 2)
            self.lows.append(self.lows[-1] + side * self.lengths[-1])
        self.turns = 4 * self.rounds + self.chunks - 1

    def greet(self):
        barrier = pltpu.get_barrier_semaphore()
        for peer in self.peers:
            pl.semaphore_signal(barrier, inc=1, device_id=peer, device_id_type=MESH)

    def greeted(self):
        pl.semaphore_wait(pltpu.get_barrier_semaphore(), self.rounds)

    def span(self, k, other=False):
        low = self.lows[k]
        if other:
            low = self.lows[k - 1] + (1 - self.sides[k - 1]) * self.lengths[k]
        return pl.ds(pl.multiple_of(low, 16), self.lengths[k])

    def landing(self, step):
        return pl.ds(self.rows - self.lengths[step], self.lengths[step + 1])

    def copy(self, c, step):
        if step < self.rounds:
            k = step
            source = self.held.at[c, self.span(k + 1, True)]
            target = self.incoming.at[c, self.landing(step)]
        else:
            k = 2 * self.rounds - 1 - step
            source = target = self.result.at[c, self.span(k + 1)]
        return pltpu.make_async_remote_copy(
            src_ref=source,
            dst_ref=target,
            send_sem=self.send_sem.at[c, step],
            recv_sem=self.recv_sem.at[c, step],
            device_id=self.peers[k],
            device_id_type=MESH,
        )

    def start(self):
        self.copy(0, 0).start()

    def turn(self, turn):
        if turn + 1 < self.chunks:
            self.copy(turn + 1, 0).start()
        for c in range(self.chunks):
            step, odd = divmod(turn - c - 1, 2)
            if odd or not 0 <= step < 2 * self.rounds:
                continue
            self.copy(c, step).wait()
            if step < self.rounds:
                kept = self.span(step + 1)
                total = self.held[c, kept].astype(jnp.float32)
                total = total + self.incoming[c, self.landing(step)].astype(jnp.float32)
                target = self.held if step < self.rounds - 1 else self.result
                target[c, kept] = total.astype(target.dtype)
            if step < 2 * self.rounds - 1:
                self.copy(c, step + 1).start()


def sum_scratch(chunks, rows, width, count):
    steps = 2 * (count.bit_length() - 1)
    return [
        pltpu.VMEM((chunks, rows, width), jnp.bfloat16),
        pltpu.VMEM((chunks, rows, width), jnp.bfloat16),
        pltpu.SemaphoreType.DMA((chunks, steps)),
        pltpu.SemaphoreType.DMA((chunks, steps)),
    ]


def sum_kernel(count, places, sizes, *refs):
    parts, sum_ref = refs[: len(places)], refs[len(places)]
    held, incoming, send_sem, recv_sem = refs[len(places) + 1 :]
    halving = Halving(count, held, incoming, sum_ref, send_sem, recv_sem)
    rows = halving.rows
    halving.greet()
    used = max(place + size for place, size in zip(places, sizes))
    for c in range(halving.chunks):
        for part, place, size in zip(parts, places, sizes):
            low, high = max(place, c * rows), min(place + size, (c + 1) * rows)
            if low < high:
                held[c, low - c * rows : high - c * rows] = part[low - place : high - place].astype(held.dtype)
        if used < (c + 1) * rows:
            low = max(used - c * rows, 0)
            held[c, low:] = jnp.zeros((rows - low, held.shape[2]), held.dtype)
    halving.greeted()
    halving.start()
    for turn in range(halving.turns):
        halving.turn(turn)


def summed(parts):
    count = lax.axis_size("seq")
    width = parts[0].shape[1]
    sizes = [part.shape[0] for part in parts]
    places, used = [], 0
    for size in sizes:
        places.append(used)
        used += -(-size // 16) * 16
    chunk = 16 * count
    chunks = -(-used // chunk)
    vmem = pl.BlockSpec(memory_space=pltpu.VMEM)
    padded = [jnp.pad(part, ((0, -part.shape[0] % 16), (0, 0))) for part in parts]
    total = pl.pallas_call(
        partial(sum_kernel, count, places, [part.shape[0] for part in padded]),
        in_specs=[vmem] * len(parts),
        out_specs=vmem,
        out_shape=jax.ShapeDtypeStruct((chunks, chunk, width), jnp.bfloat16),
        scratch_shapes=sum_scratch(chunks, chunk, width, count),
        compiler_params=pltpu.CompilerParams(
            collective_id=6, has_side_effects=True, vmem_limit_bytes=VMEM_LIMIT
        ),
        cost_estimate=lasting(60),
        name="sum_late",
    )(*padded).reshape(chunks * chunk, width)
    return [total[place : place + size].astype(jnp.float32) for place, size in zip(places, sizes)]


def to_steps(values):
    rows = values.shape[0]
    parts = values.reshape((CHUNKS, rows // CHUNKS) + values.shape[1:])
    return jnp.swapaxes(parts, 0, 1).reshape(values.shape)


def from_steps(values):
    rows = values.shape[0]
    parts = values.reshape((rows // CHUNKS, CHUNKS) + values.shape[1:])
    return jnp.swapaxes(parts, 0, 1).reshape(values.shape)


def stacked(*parts):
    rows = sum(part.shape[0] for part in parts)
    whole = jnp.concatenate([part.astype(jnp.bfloat16) for part in parts], 0)
    return jnp.pad(whole, ((0, -rows % 16), (0, 0)))


def unstacked(whole, parts):
    out, first = [], 0
    for part in parts:
        out.append(whole[first : first + part.shape[0]].astype(jnp.float32))
        first += part.shape[0]
    return out


def norm_apply(values, gain):
    return values * lax.rsqrt(jnp.mean(values * values, -1, keepdims=True) + EPS) * gain


def silu_grad(values):
    sigma = jax.nn.sigmoid(values)
    return sigma * (1.0 + values * (1.0 - sigma))


def spread(target, source):
    for n in range(STATE):
        target[n] = jnp.broadcast_to(source[:, n : n + 1], target.shape[1:])


def full(row):
    return jnp.broadcast_to(row, (CHUNKS, LANES))


def shifted(values, by, down):
    sub = lax.broadcasted_iota(jnp.int32, (CHUNKS, LANES), 0)
    if down:
        return jnp.where(sub >= by, pltpu.roll(values, by, 0), 0.0)
    return jnp.where(sub < CHUNKS - by, pltpu.roll(values, CHUNKS - by, 0), 0.0)


def chunk_windows(sums, down):
    windows = []
    for by in (1, 2, 4):
        windows.append(sums)
        sums = sums + shifted(sums, by, down)
    return windows, sums


def chunk_prefix(ends, windows, rate, down):
    for by, window in zip((1, 2, 4), windows):
        ends = ends + jnp.exp2(rate * window) * shifted(ends, by, down)
    return ends


def ends_and_rows_kernel(halves, places, *refs):
    ins, sources, outs, results, wide, sems = refs[:5], refs[5:7], refs[7:10], refs[10:12], refs[12], refs[13:]
    rows = Exchange(*places, sources, results, *sems)

    @pl.when(pl.program_id(0) == 0)
    def _():
        rows.start()

    ends_kernel(halves, False, *ins, *outs, wide)

    @pl.when(pl.program_id(0) == pl.num_programs(0) - 1)
    def _():
        rows.wait()


def ends_kernel(halves, reverse, step_ref, drive_ref, break_ref, map_ref, rate_ref, part_ref, sum_ref, tot_ref, wide):
    rows = step_ref.shape[0]
    steps = rows // (halves * CHUNKS)

    @pl.when(pl.program_id(0) == 0)
    def _():
        spread(wide, map_ref)

    rates = [full(rate_ref[n : n + 1, :]) for n in range(STATE)]
    zero = jnp.zeros((CHUNKS, LANES), jnp.float32)

    def half(turn, carry):
        h = halves - 1 - turn if reverse else turn
        before_sum, before = carry[0], carry[1:]

        def body(k, state):
            s = steps - 1 - k if reverse else k
            at = pl.ds(pl.multiple_of((h * steps + s) * CHUNKS, CHUNKS), CHUNKS)
            step = step_ref[at, :]
            decay_step = step + break_ref[at, :]
            drive = drive_ref[at, :]
            if not reverse:
                drive = drive * step
            new = [state[0] + decay_step]
            for n in range(STATE):
                decay = jnp.exp2(decay_step * rates[n])
                if reverse:
                    new.append(decay * (state[n + 1] + drive * wide[n, at, :]))
                else:
                    new.append(decay * state[n + 1] + drive * wide[n, at, :])
            return tuple(new)

        out = lax.fori_loop(0, steps, body, (zero,) * (STATE + 1), unroll=10)
        windows, sums = chunk_windows(out[0], not reverse)
        prior = shifted(sums, 1, not reverse)
        last = slice(0, 1) if reverse else slice(CHUNKS - 1, CHUNKS)
        sum_ref[h] = prior + before_sum
        new = [before_sum + full(sums[last])]
        for n in range(STATE):
            joined = chunk_prefix(out[n + 1], windows, rates[n], not reverse)
            part_ref[h, n] = shifted(joined, 1, not reverse) + jnp.exp2(rates[n] * prior) * before[n]
            new.append(full(joined[last]) + jnp.exp2(rates[n] * full(sums[last])) * before[n])
        return tuple(new)

    total = lax.fori_loop(0, halves, half, (zero,) * (STATE + 1))
    for n in range(STATE):
        tot_ref[n : n + 1, :] = total[n + 1][0:1]
    tot_ref[STATE:, :] = total[0]


def outputs_kernel(
    halves, step_ref, mixed_ref, break_ref, b_ref, c_ref, rate_ref, part_ref, sum_ref, device,
    skip_ref, gate_ref, scan_ref, gated_ref, entry_ref, b_wide, c_wide,
):
    rows = step_ref.shape[0]
    steps = rows // (halves * CHUNKS)

    @pl.when(pl.program_id(0) == 0)
    def _():
        spread(b_wide, b_ref)
        spread(c_wide, c_ref)

    rates = [full(rate_ref[n : n + 1, :]) for n in range(STATE)]

    def half(h, carry):
        state = []
        for n in range(STATE):
            state.append(
                part_ref[h, n] + jnp.exp2(rates[n] * sum_ref[h]) * full(device[n : n + 1, :])
            )
            entry_ref[h, n] = state[n]

        def body(s, state):
            at = pl.ds(pl.multiple_of((h * steps + s) * CHUNKS, CHUNKS), CHUNKS)
            step = step_ref[at, :]
            decay_step = step + break_ref[at, :]
            drive = mixed_ref[at, :] * step
            total = None
            new = []
            for n in range(STATE):
                value = jnp.exp2(decay_step * rates[n]) * state[n] + drive * b_wide[n, at, :]
                term = value * c_wide[n, at, :]
                total = term if total is None else total + term
                new.append(value)
            scan_ref[at, :] = total
            return tuple(new)

        lax.fori_loop(0, steps, body, tuple(state), unroll=5)
        return carry

    lax.fori_loop(0, halves, half, 0)
    gate = gate_ref[...]
    out = scan_ref[...] + skip_ref[...] * mixed_ref[...]
    scan_ref[...] = out
    gated_ref[...] = (out * (gate * jax.nn.sigmoid(gate))).astype(gated_ref.dtype)


def early_fills(first, second, held, own_sem):
    rows, copies, place = held.shape[1], [], 0
    for part in (first, second):
        done = 0
        while done < part.shape[0]:
            c, low = (place + done) // rows, (place + done) % rows
            length = min(rows - low, part.shape[0] - done)
            copies.append(
                pltpu.make_async_copy(
                    part.at[pl.ds(done, length)], held.at[c, pl.ds(low, length)], own_sem.at[len(copies)]
                )
            )
            done += length
        place += part.shape[0]
    return copies


def grads_kernel(
    halves, count, groups, step_ref, mixed_ref, break_ref, grad_ref, b_ref, c_ref, rate_ref, entry_ref,
    part_ref, sum_ref, device, first_early, second_early, step_out, mixed_out, b_out, c_out, rate_out, early_out,
    b_wide, c_wide, b_sum, c_sum, decays, states, held, incoming, summed_early, send_sem, recv_sem, own_sem,
):
    rows = step_ref.shape[0]
    steps = rows // (halves * CHUNKS)
    group = pl.program_id(0)
    block = STATE // 2
    halving = Halving(count, held, incoming, summed_early, send_sem, recv_sem)
    slots = [[] for _ in range(2 * groups)]
    for turn in range(halving.turns):
        slots[turn * 2 * groups // halving.turns].append(turn)

    @pl.when(group == 0)
    def _():
        halving.greet()
        fills = early_fills(first_early, second_early, held, own_sem)
        for fill in fills:
            fill.start()
        spread(b_wide, b_ref)
        for fill in fills:
            fill.wait()
        halving.greeted()
        halving.start()
        spread(c_wide, c_ref)
        b_sum[...] = jnp.zeros_like(b_sum)
        c_sum[...] = jnp.zeros_like(c_sum)

    zero = jnp.zeros((CHUNKS, LANES), jnp.float32)

    for first in (0, block):
        rates = [full(rate_ref[first + n : first + n + 1, :]) for n in range(block)]

        def half(h, rate_sums):
            entry = []
            for n in range(block):
                entry.append(entry_ref[h, first + n])
                states[0, n] = entry[n]

            def ahead(s, state):
                at = pl.ds(pl.multiple_of((h * steps + s) * CHUNKS, CHUNKS), CHUNKS)
                step = step_ref[at, :]
                decay_step = step + break_ref[at, :]
                drive = mixed_ref[at, :] * step
                new = []
                for n in range(block):
                    decay = jnp.exp2(decay_step * rates[n])
                    value = decay * state[n] + drive * b_wide[first + n, at, :]
                    decays[s, n] = decay
                    states[s + 1, n] = value
                    new.append(value)
                return tuple(new)

            lax.fori_loop(0, steps, ahead, tuple(entry), unroll=10)

            exits = [
                part_ref[h, first + n]
                + jnp.exp2(rates[n] * sum_ref[h]) * full(device[first + n : first + n + 1, :])
                for n in range(block)
            ]

            def back(k, carry):
                s = steps - 1 - k
                at = pl.ds(pl.multiple_of((h * steps + s) * CHUNKS, CHUNKS), CHUNKS)
                step = step_ref[at, :]
                mixed = mixed_ref[at, :]
                grad = grad_ref[at, :]
                drive = mixed * step
                by_rate, by_map = zero, zero
                flows, sums = [], []
                for n in range(block):
                    b_now, c_now = b_wide[first + n, at, :], c_wide[first + n, at, :]
                    here = carry[n] + c_now * grad
                    flow = decays[s, n] * here
                    log_grad = flow * states[s, n]
                    by_rate = by_rate + rates[n] * log_grad
                    by_map = by_map + b_now * here
                    b_sum[first + n, at, :] += drive * here
                    c_sum[first + n, at, :] += grad * states[s + 1, n]
                    flows.append(flow)
                    sums.append(carry[block + n] + step * log_grad)
                by_rate = by_rate * LN2 + mixed * by_map
                by_map = step * by_map
                if first == 0:
                    step_out[at, :] = by_rate
                    mixed_out[at, :] = by_map
                else:
                    step_out[at, :] += by_rate
                    mixed_out[at, :] += by_map
                return tuple(flows + sums)

            out = lax.fori_loop(0, steps, back, tuple(exits) + rate_sums, unroll=5)
            return out[block:]

        rate_sums = lax.fori_loop(0, halves, half, (zero,) * block)
        for n in range(block):
            rate_out[first + n : first + n + 1, :] = jnp.sum(rate_sums[n], 0, keepdims=True)

        for g in range(groups):
            turns = slots[2 * g + first // block]
            if turns:

                @pl.when(group == g)
                def _(turns=turns):
                    for turn in turns:
                        halving.turn(turn)

    @pl.when(group == groups - 1)
    def _():
        result = pltpu.make_async_copy(summed_early, early_out, own_sem.at[0])
        result.start()
        result.wait()
        for n in range(STATE):
            b_out[:, n : n + 1] = jnp.sum(b_sum[n], -1, keepdims=True)
            c_out[:, n : n + 1] = jnp.sum(c_sum[n], -1, keepdims=True)


class Scan:
    def __init__(self, rows, channels, halves):
        self.rows, self.channels, self.halves = rows, channels, halves
        self.groups = channels // LANES
        row_spec = pl.BlockSpec((rows, LANES), lambda g: (0, g))
        fixed = lambda *shape: pl.BlockSpec(shape, lambda g: (0,) * len(shape))
        self.row_spec = row_spec
        self.break_spec = fixed(rows, LANES)
        self.map_spec = fixed(rows, STATE)
        self.rate_spec = pl.BlockSpec((STATE, LANES), lambda g: (0, g))
        self.part_spec = pl.BlockSpec((halves, STATE, CHUNKS, LANES), lambda g: (0, 0, 0, g))
        self.sum_spec = pl.BlockSpec((halves, CHUNKS, LANES), lambda g: (0, 0, g))
        self.tot_spec = pl.BlockSpec((STATE + CHUNKS, LANES), lambda g: (0, g))
        self.skip_spec = pl.BlockSpec((1, LANES), lambda g: (0, g))
        self.row_f32 = jax.ShapeDtypeStruct((rows, channels), jnp.float32)
        self.part_f32 = jax.ShapeDtypeStruct((halves, STATE, CHUNKS, channels), jnp.float32)
        self.sum_f32 = jax.ShapeDtypeStruct((halves, CHUNKS, channels), jnp.float32)
        self.tot_f32 = jax.ShapeDtypeStruct((STATE + CHUNKS, channels), jnp.float32)
        self.wide = pltpu.VMEM((STATE, rows, LANES), jnp.float32)

    def params(self):
        return pltpu.CompilerParams(
            dimension_semantics=("arbitrary",), vmem_limit_bytes=VMEM_LIMIT
        )

    def cost(self, per_element):
        count = self.rows * self.channels * STATE
        return pl.CostEstimate(
            flops=per_element * count, bytes_accessed=12 * self.rows * self.channels, transcendentals=count
        )

    def ends(self, step, drive, breaks, maps, rates, blocks=None):
        anywhere = [pl.BlockSpec(memory_space=pl.ANY)] * 2
        forward = blocks is not None
        places = expert_groups() + (lax.axis_size("chan"),)
        kernel = partial(ends_and_rows_kernel, self.halves, places) if forward else partial(ends_kernel, self.halves, True)
        params = self.params()
        if forward:
            params = pltpu.CompilerParams(
                dimension_semantics=("arbitrary",), vmem_limit_bytes=VMEM_LIMIT, collective_id=8,
                has_side_effects=True,
            )
        return pl.pallas_call(
            kernel,
            grid=(self.groups,),
            in_specs=[self.row_spec, self.row_spec, self.break_spec, self.map_spec, self.rate_spec]
            + anywhere * forward,
            out_specs=[self.part_spec, self.sum_spec, self.tot_spec] + anywhere * forward,
            out_shape=[self.part_f32, self.sum_f32, self.tot_f32]
            + ([jax.ShapeDtypeStruct(part.shape, part.dtype) for part in blocks] if forward else []),
            scratch_shapes=[self.wide] + (exchange_scratch(2) if forward else []),
            compiler_params=params,
            cost_estimate=self.cost(5),
            name="scan_ends" if forward else "scan_ends_back",
        )(step, drive, breaks, maps, rates, *(blocks if forward else []))

    def outputs(self, step, mixed, breaks, b_in, c_out, rates, part, sums, device, skip, gate):
        return pl.pallas_call(
            partial(outputs_kernel, self.halves),
            grid=(self.groups,),
            in_specs=[
                self.row_spec, self.row_spec, self.break_spec, self.map_spec, self.map_spec, self.rate_spec,
                self.part_spec, self.sum_spec, self.rate_spec, self.skip_spec, self.row_spec,
            ],
            out_specs=[self.row_spec, self.row_spec, self.part_spec],
            out_shape=[
                self.row_f32,
                jax.ShapeDtypeStruct((self.rows, self.channels), jnp.bfloat16),
                self.part_f32,
            ],
            scratch_shapes=[self.wide, self.wide],
            compiler_params=self.params(),
            cost_estimate=self.cost(7),
            name="scan_outputs",
        )(step, mixed, breaks, b_in, c_out, rates, part, sums, device, skip, gate)

    def grads(self, step, mixed, breaks, grad, b_in, c_out, rates, entry, part, sums, device, early):
        count = lax.axis_size("seq")
        width, total = early[0].shape[1], early[0].shape[0] + early[1].shape[0]
        chunk = 16 * count
        total = -(-total // chunk) * chunk
        early = (early[0], jnp.pad(early[1], ((0, total - early[0].shape[0] - early[1].shape[0]), (0, 0))))
        chunks = total // chunk
        anywhere = pl.BlockSpec(memory_space=pl.ANY)
        steps = self.rows // (self.halves * CHUNKS)
        block = STATE // 2
        return pl.pallas_call(
            partial(grads_kernel, self.halves, count, self.groups),
            grid=(self.groups,),
            in_specs=[
                self.row_spec, self.row_spec, self.break_spec, self.row_spec, self.map_spec, self.map_spec,
                self.rate_spec, self.part_spec, self.part_spec, self.sum_spec, self.rate_spec, anywhere, anywhere,
            ],
            out_specs=[self.row_spec, self.row_spec, self.map_spec, self.map_spec, self.rate_spec, anywhere],
            out_shape=[
                self.row_f32,
                self.row_f32,
                jax.ShapeDtypeStruct((self.rows, STATE), jnp.float32),
                jax.ShapeDtypeStruct((self.rows, STATE), jnp.float32),
                jax.ShapeDtypeStruct((STATE, self.channels), jnp.float32),
                jax.ShapeDtypeStruct((chunks, chunk, width), jnp.bfloat16),
            ],
            scratch_shapes=[
                self.wide, self.wide, self.wide, self.wide,
                pltpu.VMEM((steps, block, CHUNKS, LANES), jnp.float32),
                pltpu.VMEM((steps + 1, block, CHUNKS, LANES), jnp.float32),
                pltpu.VMEM((chunks, chunk, width), jnp.bfloat16),
                *sum_scratch(chunks, chunk, width, count)[1:2],
                pltpu.VMEM((chunks, chunk, width), jnp.bfloat16),
                *sum_scratch(chunks, chunk, width, count)[2:],
                pltpu.SemaphoreType.DMA((chunks + 2,)),
            ],
            compiler_params=pltpu.CompilerParams(
                dimension_semantics=("arbitrary",), vmem_limit_bytes=VMEM_LIMIT, collective_id=7,
                has_side_effects=True,
            ),
            cost_estimate=self.cost(20),
            name="scan_grads",
        )(step, mixed, breaks, grad, b_in, c_out, rates, entry, part, sums, device, *early)


def over_tokens(values):
    return jnp.sum(jnp.sum(values, 0), -1, keepdims=True)


def sinkhorn_kernel(place_ref, logit_ref, route_ref, gate_ref, scaled_ref, row_ref, column_ref, every_ref):
    probs = jnp.exp(logit_ref[...])
    for sweep in range(SINK):
        column = over_tokens(probs)
        scaled = probs / column[None]
        row = jnp.sum(scaled, 1, keepdims=True)
        scaled_ref[sweep] = scaled
        row_ref[sweep] = row
        column_ref[sweep] = jnp.broadcast_to(column, column_ref.shape[1:])
        probs = scaled / row
    ids = lax.broadcasted_iota(jnp.int32, probs.shape, 1)
    every_ref[...] = EXPERTS * jnp.sum(jnp.where(ids == place_ref[1], probs, 0.0), 1, keepdims=True)
    place = place_ref[0]
    own = scaled_ref[SINK - 1, place] / row_ref[SINK - 1, place]
    ids = lax.broadcasted_iota(jnp.int32, own.shape, 0)
    gate_ref[...] = EXPERTS * jnp.sum(jnp.where(ids == route_ref[...], own, 0.0), 0, keepdims=True)


def sinkhorn_back_kernel(place_ref, logit_ref, scaled_ref, row_ref, column_ref, grad_ref, out_ref, held):
    grad = grad_ref[...]
    for sweep in reversed(range(SINK)):
        scaled, row = scaled_ref[sweep], row_ref[sweep]
        inner = jnp.sum(grad * (scaled / row), 1, keepdims=True)
        grad = (grad - inner) / row
        along = over_tokens(grad * scaled)
        grad = (grad - along[None]) / column_ref[sweep][:, 0:1][None]
    held[...] = grad
    place = place_ref[0]
    out_ref[...] = held[place] * jnp.exp(logit_ref[place])


def in_vmem(count):
    return [pl.BlockSpec(memory_space=pltpu.SMEM)] + [pl.BlockSpec(memory_space=pltpu.VMEM)] * count


def sinkhorn(place, logits, routes):
    devices, experts, tokens = logits.shape
    f32 = lambda *shape: jax.ShapeDtypeStruct(shape, jnp.float32)
    return pl.pallas_call(
        sinkhorn_kernel,
        in_specs=in_vmem(2),
        out_specs=in_vmem(5)[1:],
        out_shape=[
            f32(1, tokens),
            f32(SINK, devices, experts, tokens),
            f32(SINK, devices, 1, tokens),
            f32(SINK, experts, LANES),
            f32(devices, 1, tokens),
        ],
        compiler_params=pltpu.CompilerParams(vmem_limit_bytes=VMEM_LIMIT),
        name="sinkhorn",
    )(place, logits, routes)


def sinkhorn_back(place, logits, scaled, rows, columns, grad):
    devices, experts, tokens = logits.shape
    return pl.pallas_call(
        sinkhorn_back_kernel,
        in_specs=in_vmem(5),
        out_specs=in_vmem(1)[1],
        out_shape=jax.ShapeDtypeStruct((experts, tokens), jnp.float32),
        scratch_shapes=[pltpu.VMEM(logits.shape, jnp.float32)],
        compiler_params=pltpu.CompilerParams(vmem_limit_bytes=VMEM_LIMIT),
        name="sinkhorn_back",
    )(place, logits, scaled, rows, columns, grad)


def expert_kernel(
    share, rows_ref, grad_ref, gate_ref, up_ref, down_ref, out_ref, back_ref, up_kept, up_sent, down_kept,
    down_sent, rows_t, grad_t, out_sum, back_sum, whole, half, held, sent, came, send_sem, recv_sem,
):
    step, last = pl.program_id(0), pl.num_programs(0) - 1
    features = up_ref.shape[2]
    me = lax.axis_index("seq")
    side, next_side = lax.rem(me, 2), lax.rem(lax.div(me, 2), 2)
    peer = {"seq": opposite(me, 1)}

    def copy(k):
        return pltpu.make_async_remote_copy(
            src_ref=sent.at[k], dst_ref=came.at[k], send_sem=send_sem.at[k], recv_sem=recv_sem.at[k],
            device_id=peer, device_id_type=MESH,
        )

    @pl.when(step == 0)
    def _():
        greet([peer])
        rows_t[...] = rows_ref[...].T
        grad_t[...] = (grad_ref[...].astype(jnp.float32) * gate_ref[...]).astype(jnp.bfloat16).T

    def halved_rows(total, which):
        whole[...] = total
        for k in range(half.shape[0] // features):
            low = whole[2 * k * features : (2 * k + 1) * features]
            high = whole[(2 * k + 1) * features : (2 * k + 2) * features]
            half[k * features : (k + 1) * features] = jnp.where(which == 0, low, high)
        return half[...].astype(jnp.bfloat16)

    def dot(a, b, over=((1,), (0,))):
        return lax.dot_general(a, b, (over, ((), ())), preferred_element_type=jnp.float32)

    def joined(ref):
        for q in range(ref.shape[0]):
            for j in range(ref.shape[1]):
                first = (j * ref.shape[0] + q) * features
                whole[first : first + features] = ref[q, j].astype(jnp.float32)
        return whole[...].astype(jnp.bfloat16)

    def send(k, total):
        held[k] = halved_rows(total, side)
        sent[k] = halved_rows(total, 1 - side)
        copy(k).start()

    @pl.when(step < last)
    def _():
        across = ((1,), (1,))
        up, down = joined(up_ref), joined(down_ref)
        pre = dot(rows_ref[...], up)
        square = pre * pre
        bend = jnp.tanh(GELU_SCALE * (pre + GELU_CUBE * pre * square))
        rise = 0.5 * (1.0 + bend)
        act = (pre * rise).astype(jnp.bfloat16)
        slope = rise + 0.5 * pre * (1.0 - bend * bend) * (GELU_SCALE + 3.0 * GELU_SCALE * GELU_CUBE * square)
        grad_pre = dot(grad_ref[...], down) * slope
        out_part, back_part = dot(act, down, across), dot(grad_pre.astype(jnp.bfloat16), up, across)

        @pl.when(step == 0)
        def _():
            out_sum[...] = out_part
            back_sum[...] = back_part

        @pl.when(step > 0)
        def _():
            out_sum[...] += out_part
            back_sum[...] += back_part

        send(2 * step, dot(grad_t[...], act))
        send(2 * step + 1, dot(rows_t[...], (grad_pre * gate_ref[...]).astype(jnp.bfloat16)))

    @pl.when(step > 0)
    def _():
        for odd, kept_ref, sent_ref in ((0, down_kept, down_sent), (1, up_kept, up_sent)):
            k = 2 * (step - 1) + odd
            copy(k).wait()
            total = held[k].astype(jnp.float32) + came[k].astype(jnp.float32)
            half[...] = total
            for g in range(half.shape[0] // (2 * features)):
                low = half[2 * g * features : (2 * g + 1) * features]
                high = half[(2 * g + 1) * features : (2 * g + 2) * features]
                kept_ref[g] = jnp.where(next_side == 0, low, high).astype(kept_ref.dtype)
                sent_ref[g] = jnp.where(next_side == 0, high, low).astype(sent_ref.dtype)

    @pl.when(step == last)
    def _():
        out_ref[...] = out_sum[...].astype(out_ref.dtype)
        back_ref[...] = back_sum[...].astype(back_ref.dtype)


def expert_passes(rows, grad, gate, up, down):
    count, width = rows.shape
    share, own, features, hidden = up.shape
    tile = 512
    tiles = hidden // tile
    blocks = width // (4 * features)
    fixed = lambda *shape: pl.BlockSpec(shape, lambda k: (0,) * len(shape))
    weight_spec = pl.BlockSpec(
        (share, own, features, tile), lambda k: (0, 0, 0, jnp.minimum(k, tiles - 1))
    )
    part_spec = pl.BlockSpec((blocks, features, tile), lambda k: (0, 0, jnp.maximum(k - 1, 0)))
    part_shape = jax.ShapeDtypeStruct((blocks, features, hidden), jnp.bfloat16)
    row_shape = jax.ShapeDtypeStruct((count, width), jnp.bfloat16)
    return pl.pallas_call(
        partial(expert_kernel, share),
        grid=(tiles + 1,),
        in_specs=[
            fixed(count, width), fixed(count, width), fixed(count, 1), weight_spec, weight_spec,
        ],
        out_specs=[fixed(count, width), fixed(count, width)] + [part_spec] * 4,
        out_shape=[row_shape, row_shape] + [part_shape] * 4,
        scratch_shapes=[
            pltpu.VMEM((width, count), jnp.bfloat16),
            pltpu.VMEM((width, count), jnp.bfloat16),
            pltpu.VMEM((count, width), jnp.float32),
            pltpu.VMEM((count, width), jnp.float32),
            pltpu.VMEM((width, tile), jnp.float32),
            pltpu.VMEM((width // 2, tile), jnp.float32),
            pltpu.VMEM((2 * tiles, width // 2, tile), jnp.bfloat16),
            pltpu.VMEM((2 * tiles, width // 2, tile), jnp.bfloat16),
            pltpu.VMEM((2 * tiles, width // 2, tile), jnp.bfloat16),
            pltpu.SemaphoreType.DMA((2 * tiles,)),
            pltpu.SemaphoreType.DMA((2 * tiles,)),
        ],
        compiler_params=pltpu.CompilerParams(
            dimension_semantics=("arbitrary",), vmem_limit_bytes=VMEM_LIMIT, collective_id=9,
            has_side_effects=True,
        ),
        cost_estimate=pl.CostEstimate(
            flops=12 * count * width * hidden, bytes_accessed=8 * width * hidden, transcendentals=count * hidden
        ),
        name="expert_passes",
    )(rows, grad, gate, up, down)


def on_device(
    block_in,
    routes,
    doc_lengths,
    norm_gain,
    in_weight,
    conv_weight,
    conv_bias,
    xproj_weight,
    dt_weight,
    dt_bias,
    a_log,
    skip_gain,
    out_weight,
    moe_gain,
    router_weight,
    up_weight,
    down_weight,
    out_grad,
):
    tok_dev, model_width = block_in.shape
    chan_count = lax.axis_size("chan")
    chan_place, seq_place = lax.axis_index("chan"), lax.axis_index("seq")
    own, share = expert_groups()
    held_expert = chan_place * own + seq_place // share
    dev_ref = jnp.stack([seq_place * chan_count + chan_place, held_expert]).astype(jnp.int32)
    steps = tok_dev // CHUNKS
    tok_seq = tok_dev * chan_count
    channels = in_weight.shape[2]
    padded_channels = -(-channels // LANES) * LANES
    f32, bf16 = jnp.float32, jnp.bfloat16

    route_col = routes[:, 0]
    expert_ids = lax.broadcasted_iota(jnp.int32, (1, EXPERTS), 1)
    chosen = (route_col[:, None] == expert_ids).astype(bf16)
    row_ids = lax.broadcasted_iota(jnp.int32, (tok_dev, tok_dev), 0)
    col_ids = lax.broadcasted_iota(jnp.int32, (tok_dev, tok_dev), 1)
    counts = jnp.dot((col_ids <= row_ids).astype(bf16), chosen, preferred_element_type=f32)
    rank = (jnp.sum(counts * chosen.astype(f32), 1) - 1.0).astype(jnp.int32)
    capacity = tok_dev * 5 // (4 * EXPERTS) + 1
    capacity = -(-capacity // 16) * 16
    slot = to_steps(route_col * capacity + rank)
    route_steps = to_steps(route_col)
    slot_ids = lax.broadcasted_iota(jnp.int32, (1, EXPERTS * capacity), 1)
    placer = (slot[:, None] == slot_ids).astype(bf16)

    def pack(values):
        rows = jnp.einsum("ts,td->sd", placer, values, preferred_element_type=f32).astype(bf16)
        return rows.reshape(EXPERTS, capacity, model_width)

    def unpack(values):
        return jnp.einsum(
            "ts,sd->td",
            placer,
            values.reshape(EXPERTS * capacity, model_width),
            preferred_element_type=f32,
        )

    block_steps = to_steps(block_in)
    grad_steps = to_steps(out_grad)
    residual = block_steps.astype(f32)
    normed, norm_back = jax.vjp(norm_apply, residual, norm_gain)
    gathered = chan_rows(normed.astype(bf16))

    inner_b = jnp.dot(gathered, in_weight[0], preferred_element_type=f32).astype(bf16)
    gate_z = jnp.dot(gathered, in_weight[1], preferred_element_type=f32)

    shape4 = (chan_count, steps, CHUNKS)
    ids = [lax.broadcasted_iota(jnp.int32, shape4, axis) for axis in range(3)]
    position = seq_place * tok_seq + ids[0] * tok_dev + ids[2] * steps + ids[1]
    starts = jnp.cumsum(doc_lengths) - doc_lengths
    doc_first = jnp.max(
        jnp.where(starts <= position[..., None], starts, 0), axis=-1
    )
    reach = CONV - 1
    inner = inner_b.astype(f32).reshape(shape4 + (channels,))
    tails = jnp.swapaxes(inner[:, steps - reach :], 0, 1).reshape(reach, chan_count * CHUNKS, channels)
    previous = passed_along(tails[:, -1], "seq", 1)
    heads = jnp.concatenate([previous[:, None], tails[:, :-1]], 1)
    heads = jnp.swapaxes(heads.reshape(reach, chan_count, CHUNKS, channels), 0, 1)
    padded = jnp.concatenate([heads, inner], 1)
    masks = [
        (position - (reach - offset) >= doc_first).astype(f32)[..., None] for offset in range(CONV)
    ]
    conv_pre = conv_bias
    for offset in range(CONV):
        conv_pre = conv_pre + conv_weight[offset] * padded[:, offset : offset + steps] * masks[offset]
    conv_pre = conv_pre.reshape(tok_seq, channels)
    mixed_b = jax.nn.silu(conv_pre).astype(bf16)
    mixed = mixed_b.astype(f32)
    proj_all = proj_total(jnp.dot(mixed_b, xproj_weight, preferred_element_type=f32))
    low_rank = proj_all[:, :DT_RANK]
    b_in = proj_all[:, DT_RANK : DT_RANK + STATE]
    c_out = proj_all[:, DT_RANK + STATE :]
    step_pre = jnp.dot(low_rank, dt_weight, precision=HIGH) + dt_bias
    step_size = jax.nn.softplus(step_pre)

    def widened(values, axis=-1):
        more = padded_channels - channels
        if not more:
            return values
        pads = [(0, 0)] * values.ndim
        pads[axis] = (0, more)
        return jnp.pad(values, pads)

    scan = Scan(tok_seq, padded_channels, chan_count)
    decay_rates = jnp.exp(a_log)
    rates = widened((-LOG2E * decay_rates).T)
    breaks = jnp.any(position[..., None] == starts, axis=-1).astype(f32) * BREAK
    breaks = jnp.broadcast_to(breaks.reshape(tok_seq, 1), (tok_seq, LANES))
    step_w, mixed_w = widened(step_size), widened(mixed)
    token_slots = jnp.einsum(
        "ts,t->s", placer.astype(f32), 1.0 + lax.broadcasted_iota(f32, (tok_dev,), 0), precision=HIGH
    )
    token_slots = jnp.pad(token_slots.reshape(EXPERTS, 1, capacity), ((0, 0), (0, 7), (0, LANES - capacity)))
    part, sums, total, grad_arrived, token_arrived = scan.ends(
        step_w, mixed_w, breaks, b_in, rates, (pack(grad_steps), token_slots)
    )
    grad_arrived = grad_arrived.reshape(-1, model_width)
    device_entry = carried(total, rates, False)
    full_up = whole_expert(up_weight, None, device_entry)
    scan_out, gated_b, entry = scan.outputs(
        step_w, mixed_w, breaks, b_in, c_out, rates, part, sums, device_entry,
        widened(skip_gain[None]), widened(gate_z),
    )
    scan_out, gated_b = scan_out[:, :channels], gated_b[:, :channels]
    full_down = whole_expert(down_weight, device_entry, gated_b)

    mixer_rows = chan_sums(
        lambda rows: jnp.dot(rows, out_weight, preferred_element_type=f32), gated_b
    )
    hidden_one = residual + mixer_rows
    moe_in, moe_back = jax.vjp(norm_apply, hidden_one, moe_gain)
    logits = jnp.einsum("td,de->et", moe_in, router_weight, precision=HIGH)
    arrived, every_logit = rows_and_gather(pack(moe_in.astype(bf16)), logits)
    gate_row, scaled, row_totals, columns, every_gate = sinkhorn(
        dev_ref, every_logit, route_steps.reshape(1, tok_dev)
    )
    gate = gate_row.reshape(tok_dev)

    arrived = arrived.reshape(-1, model_width)
    senders = lax.dynamic_index_in_dim(
        every_gate.reshape(own, share, chan_count, tok_dev), seq_place % share, 1, False
    )
    senders = jnp.swapaxes(senders, 0, 1).reshape(EXPERTS, 1, tok_dev)
    token_ids = 1.0 + lax.broadcasted_iota(f32, (1, 1, tok_dev), 2)
    gate_arrived = jnp.sum(
        jnp.where(token_arrived[:, 0, :capacity, None] == token_ids, senders, 0.0), -1
    ).reshape(-1, 1)
    features, hidden = up_weight.shape[1:]
    expert_out, grad_rows_in, up_kept, up_sent, down_kept, down_sent = expert_passes(
        arrived, grad_arrived, gate_arrived, full_up, full_down
    )
    blocks = (EXPERTS, capacity, model_width)
    expert_back, grad_back = expert_rows(2, expert_out.reshape(blocks), grad_rows_in.reshape(blocks))
    expert_grads = [
        added(kept, swapped(sent, "seq", 2)).reshape(own, share // 4, features, hidden)
        for kept, sent in ((up_kept, up_sent), (down_kept, down_sent))
    ]
    for stage in range(2, share.bit_length() - 1):
        expert_grads = [halved(part, stage) for part in expert_grads]
    expert_tok = unpack(expert_back)
    plain_grad_part = unpack(grad_back)
    up_part, down_part = expert_grads

    block_out = from_steps((hidden_one + gate[:, None] * expert_tok).astype(bf16))
    grad_two = grad_steps.astype(f32)
    grad_gate = jnp.sum(expert_tok * grad_two, 1)
    grad_probs = jnp.where(
        route_steps[None] == lax.broadcasted_iota(jnp.int32, (EXPERTS, 1), 0),
        EXPERTS * grad_gate[None],
        0.0,
    )
    every_grad, up_part = gathered_everywhere(10, grad_probs, up_part)
    up_grad = to_owners(up_part.reshape(own, *up_part.shape[2:]))
    grad_logits = sinkhorn_back(dev_ref, every_logit, scaled, row_totals, columns, every_grad)
    router_grad = jnp.einsum("td,et->ed", moe_in, grad_logits, precision=HIGH)
    grad_moe_in = gate[:, None] * plain_grad_part + jnp.einsum(
        "et,de->td", grad_logits, router_weight, precision=HIGH
    )
    grad_hidden, moe_gain_grad = moe_back(grad_moe_in)
    grad_hidden = grad_hidden + grad_two

    grad_mix = chan_rows(grad_hidden.astype(bf16))
    grad_gated = jnp.einsum("td,ed->te", grad_mix, out_weight, preferred_element_type=f32)
    out_weight_grad = jnp.einsum("te,td->ed", gated_b, grad_mix, preferred_element_type=f32)
    grad_scan = grad_gated * jax.nn.silu(gate_z)
    grad_gate_z = (grad_gated * scan_out * silu_grad(gate_z)).astype(bf16)
    skip_grad = jnp.sum(grad_scan * mixed, 0)
    gate_weight_grad = jnp.einsum("td,te->de", gathered, grad_gate_z, preferred_element_type=f32)
    gains = jnp.concatenate([moe_gain_grad[None], router_grad], 0)
    gains = lax.psum(gains, "chan") if chan_count != 2 else gains + swapped(gains, "chan", 1)
    grad_scan_w = widened(grad_scan)
    back_part, back_sums, back_total = scan.ends(step_w, grad_scan_w, breaks, c_out, rates)
    back_entry = carried(back_total, rates, True, up_grad, down_part)
    step_grad, mixed_grad, b_grad, c_grad, rate_grad, early = scan.grads(
        step_w, mixed_w, breaks, grad_scan_w, b_in, c_out, rates, entry, back_part, back_sums,
        back_entry, (out_weight_grad.astype(bf16).reshape(-1, channels), gate_weight_grad.astype(bf16)),
    )
    early = early.reshape(-1, channels)
    down_grad = to_owners(after(down_part.reshape(own, *down_part.shape[2:]), step_grad))
    step_grad, mixed_grad = step_grad[:, :channels], mixed_grad[:, :channels]
    mixed_grad = mixed_grad + skip_gain * grad_scan
    a_log_rows = -decay_rates.T * rate_grad[:, :channels]
    step_pre_grad = step_grad * jax.nn.sigmoid(step_pre)
    dt_bias_grad = jnp.sum(step_pre_grad, 0)
    dt_weight_grad = jnp.einsum("tr,te->re", low_rank, step_pre_grad, precision=HIGH)
    rank_grad = jnp.einsum("te,re->tr", step_pre_grad, dt_weight, precision=HIGH)
    proj_grad_b = proj_total(jnp.concatenate([rank_grad, b_grad, c_grad], 1)).astype(bf16)
    mixed_grad = mixed_grad + jnp.einsum(
        "tp,ep->te", proj_grad_b, xproj_weight, preferred_element_type=f32
    )
    xproj_rows = jnp.einsum("te,tp->pe", mixed_b, proj_grad_b, preferred_element_type=f32)
    conv_grad = (mixed_grad * silu_grad(conv_pre)).reshape(shape4 + (channels,))
    conv_bias_grad = jnp.sum(conv_grad, (0, 1, 2))
    conv_weight_grad = jnp.stack(
        [
            jnp.sum(conv_grad * masks[offset] * padded[:, offset : offset + steps], (0, 1, 2))
            for offset in range(CONV)
        ]
    )
    padded_grad = 0.0
    for offset in range(CONV):
        padded_grad = padded_grad + jnp.pad(
            conv_weight[offset] * conv_grad * masks[offset],
            ((0, 0), (offset, reach - offset), (0, 0), (0, 0)),
        )
    head_grad = jnp.swapaxes(padded_grad[:, :reach], 0, 1).reshape(
        reach, chan_count * CHUNKS, channels
    )
    from_next = passed_along(head_grad[:, 0], "seq", -1)
    tail_grad = jnp.concatenate([head_grad[:, 1:], from_next[:, None]], 1)
    tail_grad = jnp.swapaxes(tail_grad.reshape(reach, chan_count, CHUNKS, channels), 0, 1)
    inner_grad = padded_grad[:, reach:] + jnp.pad(
        tail_grad, ((0, 0), (steps - reach, 0), (0, 0), (0, 0))
    )
    inner_grad_b = inner_grad.reshape(tok_seq, channels).astype(bf16)
    inner_weight_grad = jnp.einsum("td,te->de", gathered, inner_grad_b, preferred_element_type=f32)
    both_grad = jnp.concatenate([inner_grad_b, grad_gate_z], 1)
    normed_grad = chan_sums(
        lambda rows: jnp.dot(rows[:, :channels], in_weight[0].T, preferred_element_type=f32)
        + jnp.dot(rows[:, channels:], in_weight[1].T, preferred_element_type=f32),
        both_grad,
    )
    residual_grad, norm_gain_grad = norm_back(normed_grad)
    in_grad = from_steps(residual_grad + grad_hidden)

    norm_rows = norm_gain_grad[None]
    norm_rows = lax.psum(norm_rows, "chan") if chan_count != 2 else norm_rows + swapped(norm_rows, "chan", 1)
    pieces = (
        xproj_rows, dt_weight_grad, a_log_rows, conv_weight_grad, conv_bias_grad[None], dt_bias_grad[None],
        skip_grad[None], norm_rows.reshape(-1, channels), gains.reshape(-1, channels),
    )
    bounds = [sum(part.shape[0] for part in pieces[: k + 1]) for k in range(len(pieces) - 1)]
    inner_weight_grad, small = summed([after(inner_weight_grad.astype(bf16), down_grad), jnp.concatenate(pieces, 0)])
    out_weight_grad = early[:model_width].reshape(channels, model_width).astype(f32)
    gate_weight_grad = early[model_width : 2 * model_width].astype(f32)
    (
        xproj_rows, dt_weight_grad, a_log_rows, conv_weight_grad, conv_bias_grad, dt_bias_grad, skip_grad,
        norm_rows, gains,
    ) = jnp.split(small, bounds, 0)
    norm_gain_grad, gains = norm_rows.reshape(-1), gains.reshape(-1, model_width)
    xproj_grad, a_log_grad = xproj_rows.T, a_log_rows.T
    conv_bias_grad, dt_bias_grad, skip_grad = conv_bias_grad[0], dt_bias_grad[0], skip_grad[0]
    moe_gain_grad, router_grad = gains[0], gains[1:].T
    in_weight_grad = jnp.stack([inner_weight_grad, gate_weight_grad])
    return (
        block_out,
        in_grad,
        norm_gain_grad,
        in_weight_grad,
        conv_weight_grad,
        conv_bias_grad,
        xproj_grad,
        dt_weight_grad,
        dt_bias_grad,
        a_log_grad,
        skip_grad,
        out_weight_grad,
        moe_gain_grad,
        router_grad,
        up_grad.astype(f32),
        down_grad.astype(f32),
    )


def solution(mesh):
    in_specs = (
        P(("seq", "chan"), None),
        P(("seq", "chan"), None),
        P(),
        P(),
        P(None, None, "chan"),
        P(None, "chan"),
        P("chan"),
        P("chan", None),
        P(None, "chan"),
        P("chan"),
        P("chan", None),
        P("chan"),
        P("chan", None),
        P(),
        P(),
        P("chan", "seq", None),
        P("chan", "seq", None),
        P(("seq", "chan"), None),
    )
    out_specs = (
        P(("seq", "chan"), None),
        P(("seq", "chan"), None),
        P(),
        P(None, None, "chan"),
        P(None, "chan"),
        P("chan"),
        P("chan", None),
        P(None, "chan"),
        P("chan"),
        P("chan", None),
        P("chan"),
        P("chan", None),
        P(),
        P(),
        P("chan", "seq", None),
        P("chan", "seq", None),
    )
    return jax.shard_map(
        on_device, mesh=mesh, in_specs=in_specs, out_specs=out_specs, check_vma=False
    )
```

```python
from functools import partial

import jax
import jax.numpy as jnp
from jax import lax
from jax.experimental import pallas as pl
from jax.experimental.pallas import tpu as pltpu
from jax.sharding import PartitionSpec as P

STATE = 16
CONV = 4
DT_RANK = 72
EXPERTS = 8
SINK = 8
CHUNKS = 8
LANES = 128
VMEM_LIMIT = 56 * 1024 * 1024

EPS = 1e-05
HIGH = lax.Precision.HIGHEST
LOG2E = 1.4426950408889634
LN2 = 0.6931471805599453
BREAK = 1e30
MESH = pl.DeviceIdType.MESH
GELU_SCALE = 0.7978845608028654
GELU_CUBE = 0.044715


def passed_along(value, axis, steps):
    count = lax.axis_size(axis)
    leading, last = (max(0, -steps), min(count, count - steps))
    return lax.ppermute(value, axis, [(source, source + steps) for source in range(leading, last)])


def swapped(value, axis, bit):
    count = lax.axis_size(axis)
    return lax.ppermute(value, axis, [(source, source ^ bit) for source in range(count)])


def chan_rows(values):
    if lax.axis_size("chan") != 2:
        return lax.all_gather(values, "chan", axis=0, tiled=True)
    first = lax.axis_index("chan") == 0
    other = swapped(values, "chan", 1)
    return jnp.concatenate([jnp.where(first, values, other), jnp.where(first, other, values)], 0)


def chan_sums(term_fn, operand):
    count, place = lax.axis_size("chan"), lax.axis_index("chan")
    rows = operand.shape[0] // count
    if count != 2:
        return lax.psum_scatter(term_fn(operand), "chan", scatter_dimension=0, tiled=True)
    theirs = term_fn(lax.dynamic_slice_in_dim(operand, (1 - place) * rows, rows, 0))
    arrived = swapped(theirs.astype(jnp.bfloat16), "chan", 1)
    return term_fn(lax.dynamic_slice_in_dim(operand, place * rows, rows, 0)) + arrived.astype(
        jnp.float32
    )


def proj_total(values):
    if lax.axis_size("chan") != 2:
        return lax.psum(values, "chan")
    return values + swapped(values, "chan", 1)


def expert_groups():
    own = EXPERTS // lax.axis_size("chan")
    return own, lax.axis_size("seq") // own


def across_experts(values, axis, wait=None):
    own, share = expert_groups()
    place = lax.div(lax.axis_index("seq"), share)
    out = values
    for d in range(1, own):
        peer = lax.bitwise_xor(place, d)
        came = swapped(lax.dynamic_slice_in_dim(values, peer, 1, axis), "seq", d * share)
        if wait is not None:
            came = after(came, wait)
        out = lax.dynamic_update_slice_in_dim(out, came, peer, axis)
    return out


def to_owners(grad):
    own, share = expert_groups()
    if own == 1:
        return grad
    groups = [[k * share + q for k in range(own)] for q in range(share)]
    return lax.all_to_all(
        grad, "seq", split_axis=0, concat_axis=0, tiled=True, axis_index_groups=groups
    )


def expert_rows(ident, *arrays):
    return exchange(ident, arrays)


def whole_expert(weight, start, wait):
    own, share = expert_groups()
    features, hidden = weight.shape[1:]
    if start is not None:
        weight = after(weight, start)
    mine = across_experts(weight, 0, wait)
    groups = [[k * share + q for q in range(share)] for k in range(own)]
    return lax.all_gather(mine, "seq", axis_index_groups=groups)


def halved(grad, stage):
    own, share = expert_groups()
    bit = 1 << stage
    pairs = grad.reshape(own, grad.shape[1] // 2, 2, *grad.shape[2:])
    side = lax.rem(lax.div(lax.axis_index("seq"), bit), 2)
    sent = lax.dynamic_index_in_dim(pairs, 1 - side, 2, False)
    kept = lax.dynamic_index_in_dim(pairs, side, 2, False)
    came = swapped(sent, "seq", bit)
    return added(kept, came)


def added(kept, came):
    return (kept.astype(jnp.float32) + came.astype(jnp.float32)).astype(kept.dtype)


def after(value, *others):
    return lax.optimization_barrier((value,) + others)[0]


def lasting(microseconds):
    return pl.CostEstimate(flops=0, bytes_accessed=microseconds * 3_600_000, transcendentals=0)


def opposite(place, bit):
    return place + bit - 2 * bit * lax.rem(lax.div(place, bit), 2)


def greet(targets):
    barrier = pltpu.get_barrier_semaphore()
    for target in targets:
        pl.semaphore_signal(barrier, inc=1, device_id=target, device_id_type=MESH)
    pl.semaphore_wait(barrier, len(targets))


class Exchange:
    def __init__(self, own, share, chans, sources, results, send_sem, recv_sem, own_sem):
        seq, chan = lax.axis_index("seq"), lax.axis_index("chan")
        column = lax.rem(seq, share)
        me = chan * own + lax.div(seq, share)
        total = own * chans
        peers = [lax.rem(me + d, total) for d in range(1, total)]
        self.targets = [(lax.rem(peer, own) * share + column, lax.div(peer, own)) for peer in peers]
        self.copies = []
        for k, (source, result) in enumerate(zip(sources, results)):
            for d in range(total - 1):
                self.copies.append(
                    pltpu.make_async_remote_copy(
                        src_ref=source.at[peers[d]],
                        dst_ref=result.at[me],
                        send_sem=send_sem.at[k, d],
                        recv_sem=recv_sem.at[k, d],
                        device_id=self.targets[d],
                        device_id_type=MESH,
                    )
                )
            self.copies.append(pltpu.make_async_copy(source.at[me], result.at[me], own_sem.at[k]))

    def start(self):
        greet(self.targets)
        for copy in self.copies:
            copy.start()

    def wait(self):
        for copy in self.copies:
            copy.wait()


def exchange_scratch(count):
    others = expert_groups()[0] * lax.axis_size("chan") - 1
    return [
        pltpu.SemaphoreType.DMA((count, others)),
        pltpu.SemaphoreType.DMA((count, others)),
        pltpu.SemaphoreType.DMA((count,)),
    ]


def exchange_kernel(own, share, chans, count, *refs):
    rows = Exchange(own, share, chans, refs[:count], refs[count : 2 * count], *refs[2 * count :])
    rows.start()
    rows.wait()


def exchange(ident, arrays):
    own, share = expert_groups()
    chans, count = lax.axis_size("chan"), len(arrays)
    anywhere = pl.BlockSpec(memory_space=pl.ANY)
    return pl.pallas_call(
        partial(exchange_kernel, own, share, chans, count),
        in_specs=[anywhere] * count,
        out_specs=[anywhere] * count,
        out_shape=[jax.ShapeDtypeStruct(part.shape, part.dtype) for part in arrays],
        scratch_shapes=exchange_scratch(count),
        compiler_params=pltpu.CompilerParams(collective_id=ident, has_side_effects=True),
        cost_estimate=lasting(26 * count),
        name="expert_rows",
    )(*arrays)


class Gather:
    def __init__(self, devices, chans, own_ref, every_ref, send_sem, recv_sem):
        self.devices, self.chans = devices, chans
        self.own_ref, self.every_ref = own_ref, every_ref
        self.send_sem, self.recv_sem = send_sem, recv_sem
        self.me = lax.axis_index("seq") * chans + lax.axis_index("chan")

    def target(self, d):
        peer = lax.rem(self.me + d, self.devices)
        return (lax.div(peer, self.chans), lax.rem(peer, self.chans))

    def copy(self, d):
        return pltpu.make_async_remote_copy(
            src_ref=self.own_ref,
            dst_ref=self.every_ref.at[self.me],
            send_sem=self.send_sem.at[d - 1],
            recv_sem=self.recv_sem.at[d - 1],
            device_id=self.target(d),
            device_id_type=MESH,
        )

    def each(self, act):
        def turn(d, carry):
            act(d)
            return carry

        lax.fori_loop(1, self.devices, turn, 0)

    def greet(self):
        barrier = pltpu.get_barrier_semaphore()
        self.each(
            lambda d: pl.semaphore_signal(barrier, inc=1, device_id=self.target(d), device_id_type=MESH)
        )
        self.every_ref[self.me] = self.own_ref[...]
        pl.semaphore_wait(barrier, self.devices - 1)

    def start(self):
        self.each(lambda d: self.copy(d).start())

    def wait(self):
        self.each(lambda d: self.copy(d).wait())


def gather_kernel(devices, chans, passed, own_ref, *refs):
    gather = Gather(devices, chans, own_ref, refs[passed], refs[-2], refs[-1])
    gather.greet()
    gather.start()
    gather.wait()


def rows_and_gather_kernel(
    places, devices, source, own_ref, result, every_ref, rows_send, rows_recv, rows_own, send_sem, recv_sem
):
    gather = Gather(devices, places[2], own_ref, every_ref, send_sem, recv_sem)
    rows = Exchange(*places, [source], [result], rows_send, rows_recv, rows_own)
    gather.greet()
    gather.start()
    for copy in rows.copies:
        copy.start()
    gather.wait()
    rows.wait()


def rows_and_gather(packed, values):
    chans = lax.axis_size("chan")
    devices = lax.axis_size("seq") * chans
    vmem, anywhere = pl.BlockSpec(memory_space=pltpu.VMEM), pl.BlockSpec(memory_space=pl.ANY)
    return pl.pallas_call(
        partial(rows_and_gather_kernel, expert_groups() + (chans,), devices),
        in_specs=[anywhere, vmem],
        out_specs=[anywhere, vmem],
        out_shape=[
            jax.ShapeDtypeStruct(packed.shape, packed.dtype),
            jax.ShapeDtypeStruct((devices,) + values.shape, values.dtype),
        ],
        scratch_shapes=exchange_scratch(1)
        + [pltpu.SemaphoreType.DMA((devices - 1,)), pltpu.SemaphoreType.DMA((devices - 1,))],
        compiler_params=pltpu.CompilerParams(
            collective_id=1, has_side_effects=True, vmem_limit_bytes=VMEM_LIMIT
        ),
        cost_estimate=lasting(34),
        name="rows_and_gather",
    )(packed, values)


def gathered_everywhere(ident, values, *passed):
    chans = lax.axis_size("chan")
    devices = lax.axis_size("seq") * chans
    vmem, anywhere = pl.BlockSpec(memory_space=pltpu.VMEM), pl.BlockSpec(memory_space=pl.ANY)
    out = pl.pallas_call(
        partial(gather_kernel, devices, chans, len(passed)),
        in_specs=[vmem] + [anywhere] * len(passed),
        out_specs=[vmem] + [anywhere] * len(passed),
        out_shape=[jax.ShapeDtypeStruct((devices,) + values.shape, values.dtype)]
        + [jax.ShapeDtypeStruct(part.shape, part.dtype) for part in passed],
        input_output_aliases={1 + k: 1 + k for k in range(len(passed))},
        scratch_shapes=[
            pltpu.SemaphoreType.DMA((devices - 1,)),
            pltpu.SemaphoreType.DMA((devices - 1,)),
        ],
        compiler_params=pltpu.CompilerParams(
            collective_id=ident, has_side_effects=True, vmem_limit_bytes=VMEM_LIMIT
        ),
        cost_estimate=lasting(12),
        name="gather_small",
    )(values, *passed)
    return out if passed else out[0]


def carry_kernel(count, reverse, total_ref, rate_ref, *refs):
    entry_ref, ends_out, ends_in, sums_out, sums_in, ends_sems, sums_sems = refs[-7:]
    me = lax.axis_index("seq")
    bits = [1 << k for k in range(count.bit_length() - 1)]
    greet([{"seq": opposite(me, bit)} for bit in bits])
    rates = rate_ref[...]
    ends, sums = total_ref[:STATE], total_ref[STATE : STATE + 1]
    before, before_sum = jnp.zeros_like(ends), jnp.zeros_like(sums)
    for k, bit in enumerate(bits):
        ends_out[k] = ends.astype(ends_out.dtype)
        sums_out[k] = sums
        copies = [
            pltpu.make_async_remote_copy(
                src_ref=out.at[k],
                dst_ref=into.at[k],
                send_sem=sems.at[0, k],
                recv_sem=sems.at[1, k],
                device_id={"seq": opposite(me, bit)},
                device_id_type=MESH,
            )
            for out, into, sems in ((ends_out, ends_in, ends_sems), (sums_out, sums_in, sums_sems))
        ]
        for copy in copies:
            copy.start()
        for copy in copies:
            copy.wait()
        their_ends, their_sums = ends_in[k].astype(jnp.float32), sums_in[k]
        theirs_first = lax.rem(lax.div(me, bit), 2) == (0 if reverse else 1)
        before = jnp.where(theirs_first, jnp.exp2(rates * before_sum) * their_ends + before, before)
        before_sum = jnp.where(theirs_first, before_sum + their_sums, before_sum)
        ends = jnp.where(
            theirs_first,
            jnp.exp2(rates * sums) * their_ends + ends,
            jnp.exp2(rates * their_sums) * ends + their_ends,
        )
        sums = sums + their_sums
    entry_ref[...] = before


def carried(total, rates, reverse, *needed):
    count = lax.axis_size("seq")
    rounds = count.bit_length() - 1
    channels = rates.shape[1]
    vmem = pl.BlockSpec(memory_space=pltpu.VMEM)
    return pl.pallas_call(
        partial(carry_kernel, count, reverse),
        in_specs=[vmem, vmem] + [pl.BlockSpec(memory_space=pl.ANY)] * len(needed),
        out_specs=vmem,
        out_shape=jax.ShapeDtypeStruct(rates.shape, jnp.float32),
        scratch_shapes=[
            pltpu.VMEM((rounds, STATE, channels), jnp.bfloat16),
            pltpu.VMEM((rounds, STATE, channels), jnp.bfloat16),
            pltpu.VMEM((rounds, 1, channels), jnp.float32),
            pltpu.VMEM((rounds, 1, channels), jnp.float32),
            pltpu.SemaphoreType.DMA((2, rounds)),
            pltpu.SemaphoreType.DMA((2, rounds)),
        ],
        compiler_params=pltpu.CompilerParams(
            collective_id=5 if reverse else 4, has_side_effects=True, vmem_limit_bytes=VMEM_LIMIT
        ),
        cost_estimate=lasting(14),
        name="carry_back" if reverse else "carry",
    )(total, rates, *needed)


class Halving:
    def __init__(self, count, held, incoming, result, send_sem, recv_sem):
        self.held, self.incoming, self.result = held, incoming, result
        self.send_sem, self.recv_sem = send_sem, recv_sem
        self.chunks, self.rows = held.shape[0], held.shape[1]
        me = lax.axis_index("seq")
        bits = [1 << k for k in range(count.bit_length() - 1)]
        self.rounds = len(bits)
        self.peers = [{"seq": opposite(me, bit)} for bit in bits]
        self.sides = [lax.rem(lax.div(me, bit), 2) for bit in bits]
        self.lows, self.lengths = [0], [self.rows]
        for side in self.sides:
            self.lengths.append(self.lengths[-1] // 2)
            self.lows.append(self.lows[-1] + side * self.lengths[-1])
        self.turns = 4 * self.rounds + self.chunks - 1

    def greet(self):
        barrier = pltpu.get_barrier_semaphore()
        for peer in self.peers:
            pl.semaphore_signal(barrier, inc=1, device_id=peer, device_id_type=MESH)

    def greeted(self):
        pl.semaphore_wait(pltpu.get_barrier_semaphore(), self.rounds)

    def span(self, k, other=False):
        low = self.lows[k]
        if other:
            low = self.lows[k - 1] + (1 - self.sides[k - 1]) * self.lengths[k]
        return pl.ds(pl.multiple_of(low, 16), self.lengths[k])

    def landing(self, step):
        return pl.ds(self.rows - self.lengths[step], self.lengths[step + 1])

    def copy(self, c, step):
        if step < self.rounds:
            k = step
            source = self.held.at[c, self.span(k + 1, True)]
            target = self.incoming.at[c, self.landing(step)]
        else:
            k = 2 * self.rounds - 1 - step
            source = target = self.result.at[c, self.span(k + 1)]
        return pltpu.make_async_remote_copy(
            src_ref=source,
            dst_ref=target,
            send_sem=self.send_sem.at[c, step],
            recv_sem=self.recv_sem.at[c, step],
            device_id=self.peers[k],
            device_id_type=MESH,
        )

    def start(self):
        self.copy(0, 0).start()

    def turn(self, turn):
        if turn + 1 < self.chunks:
            self.copy(turn + 1, 0).start()
        for c in range(self.chunks):
            step, odd = divmod(turn - c - 1, 2)
            if odd or not 0 <= step < 2 * self.rounds:
                continue
            self.copy(c, step).wait()
            if step < self.rounds:
                kept = self.span(step + 1)
                total = self.held[c, kept].astype(jnp.float32)
                total = total + self.incoming[c, self.landing(step)].astype(jnp.float32)
                target = self.held if step < self.rounds - 1 else self.result
                target[c, kept] = total.astype(target.dtype)
            if step < 2 * self.rounds - 1:
                self.copy(c, step + 1).start()


def sum_scratch(chunks, rows, width, count):
    steps = 2 * (count.bit_length() - 1)
    return [
        pltpu.VMEM((chunks, rows, width), jnp.bfloat16),
        pltpu.VMEM((chunks, rows, width), jnp.bfloat16),
        pltpu.SemaphoreType.DMA((chunks, steps)),
        pltpu.SemaphoreType.DMA((chunks, steps)),
    ]


def sum_kernel(count, places, sizes, *refs):
    parts, sum_ref = refs[: len(places)], refs[len(places)]
    held, incoming, send_sem, recv_sem = refs[len(places) + 1 :]
    halving = Halving(count, held, incoming, sum_ref, send_sem, recv_sem)
    rows = halving.rows
    halving.greet()
    used = max(place + size for place, size in zip(places, sizes))
    for c in range(halving.chunks):
        for part, place, size in zip(parts, places, sizes):
            low, high = max(place, c * rows), min(place + size, (c + 1) * rows)
            if low < high:
                held[c, low - c * rows : high - c * rows] = part[low - place : high - place].astype(held.dtype)
        if used < (c + 1) * rows:
            low = max(used - c * rows, 0)
            held[c, low:] = jnp.zeros((rows - low, held.shape[2]), held.dtype)
    halving.greeted()
    halving.start()
    for turn in range(halving.turns):
        halving.turn(turn)


def summed(parts):
    count = lax.axis_size("seq")
    width = parts[0].shape[1]
    sizes = [part.shape[0] for part in parts]
    places, used = [], 0
    for size in sizes:
        places.append(used)
        used += -(-size // 16) * 16
    chunk = 16 * count
    chunks = -(-used // chunk)
    vmem = pl.BlockSpec(memory_space=pltpu.VMEM)
    padded = [jnp.pad(part, ((0, -part.shape[0] % 16), (0, 0))) for part in parts]
    total = pl.pallas_call(
        partial(sum_kernel, count, places, [part.shape[0] for part in padded]),
        in_specs=[vmem] * len(parts),
        out_specs=vmem,
        out_shape=jax.ShapeDtypeStruct((chunks, chunk, width), jnp.bfloat16),
        scratch_shapes=sum_scratch(chunks, chunk, width, count),
        compiler_params=pltpu.CompilerParams(
            collective_id=6, has_side_effects=True, vmem_limit_bytes=VMEM_LIMIT
        ),
        cost_estimate=lasting(60),
        name="sum_late",
    )(*padded).reshape(chunks * chunk, width)
    return [total[place : place + size].astype(jnp.float32) for place, size in zip(places, sizes)]


def to_steps(values):
    rows = values.shape[0]
    parts = values.reshape((CHUNKS, rows // CHUNKS) + values.shape[1:])
    return jnp.swapaxes(parts, 0, 1).reshape(values.shape)


def from_steps(values):
    rows = values.shape[0]
    parts = values.reshape((rows // CHUNKS, CHUNKS) + values.shape[1:])
    return jnp.swapaxes(parts, 0, 1).reshape(values.shape)


def stacked(*parts):
    rows = sum(part.shape[0] for part in parts)
    whole = jnp.concatenate([part.astype(jnp.bfloat16) for part in parts], 0)
    return jnp.pad(whole, ((0, -rows % 16), (0, 0)))


def unstacked(whole, parts):
    out, first = [], 0
    for part in parts:
        out.append(whole[first : first + part.shape[0]].astype(jnp.float32))
        first += part.shape[0]
    return out


def norm_apply(values, gain):
    return values * lax.rsqrt(jnp.mean(values * values, -1, keepdims=True) + EPS) * gain


def silu_grad(values):
    sigma = jax.nn.sigmoid(values)
    return sigma * (1.0 + values * (1.0 - sigma))


def spread(target, source):
    for n in range(STATE):
        target[n] = jnp.broadcast_to(source[:, n : n + 1], target.shape[1:])


def full(row):
    return jnp.broadcast_to(row, (CHUNKS, LANES))


def shifted(values, by, down):
    sub = lax.broadcasted_iota(jnp.int32, (CHUNKS, LANES), 0)
    if down:
        return jnp.where(sub >= by, pltpu.roll(values, by, 0), 0.0)
    return jnp.where(sub < CHUNKS - by, pltpu.roll(values, CHUNKS - by, 0), 0.0)


def chunk_windows(sums, down):
    windows = []
    for by in (1, 2, 4):
        windows.append(sums)
        sums = sums + shifted(sums, by, down)
    return windows, sums


def chunk_prefix(ends, windows, rate, down):
    for by, window in zip((1, 2, 4), windows):
        ends = ends + jnp.exp2(rate * window) * shifted(ends, by, down)
    return ends


def ends_and_rows_kernel(halves, places, *refs):
    ins, sources, outs, results, wide, sems = refs[:5], refs[5:7], refs[7:10], refs[10:12], refs[12], refs[13:]
    rows = Exchange(*places, sources, results, *sems)

    @pl.when(pl.program_id(0) == 0)
    def _():
        rows.start()

    ends_kernel(halves, False, *ins, *outs, wide)

    @pl.when(pl.program_id(0) == pl.num_programs(0) - 1)
    def _():
        rows.wait()


def ends_kernel(halves, reverse, step_ref, drive_ref, break_ref, map_ref, rate_ref, part_ref, sum_ref, tot_ref, wide):
    rows = step_ref.shape[0]
    steps = rows // (halves * CHUNKS)

    @pl.when(pl.program_id(0) == 0)
    def _():
        spread(wide, map_ref)

    rates = [full(rate_ref[n : n + 1, :]) for n in range(STATE)]
    zero = jnp.zeros((CHUNKS, LANES), jnp.float32)

    def half(turn, carry):
        h = halves - 1 - turn if reverse else turn
        before_sum, before = carry[0], carry[1:]

        def body(k, state):
            s = steps - 1 - k if reverse else k
            at = pl.ds(pl.multiple_of((h * steps + s) * CHUNKS, CHUNKS), CHUNKS)
            step = step_ref[at, :]
            decay_step = step + break_ref[at, :]
            drive = drive_ref[at, :]
            if not reverse:
                drive = drive * step
            new = [state[0] + decay_step]
            for n in range(STATE):
                decay = jnp.exp2(decay_step * rates[n])
                if reverse:
                    new.append(decay * (state[n + 1] + drive * wide[n, at, :]))
                else:
                    new.append(decay * state[n + 1] + drive * wide[n, at, :])
            return tuple(new)

        out = lax.fori_loop(0, steps, body, (zero,) * (STATE + 1), unroll=10)
        windows, sums = chunk_windows(out[0], not reverse)
        prior = shifted(sums, 1, not reverse)
        last = slice(0, 1) if reverse else slice(CHUNKS - 1, CHUNKS)
        sum_ref[h] = prior + before_sum
        new = [before_sum + full(sums[last])]
        for n in range(STATE):
            joined = chunk_prefix(out[n + 1], windows, rates[n], not reverse)
            part_ref[h, n] = shifted(joined, 1, not reverse) + jnp.exp2(rates[n] * prior) * before[n]
            new.append(full(joined[last]) + jnp.exp2(rates[n] * full(sums[last])) * before[n])
        return tuple(new)

    total = lax.fori_loop(0, halves, half, (zero,) * (STATE + 1))
    for n in range(STATE):
        tot_ref[n : n + 1, :] = total[n + 1][0:1]
    tot_ref[STATE:, :] = total[0]


def outputs_kernel(
    halves, step_ref, mixed_ref, break_ref, b_ref, c_ref, rate_ref, part_ref, sum_ref, device,
    skip_ref, gate_ref, scan_ref, gated_ref, entry_ref, b_wide, c_wide,
):
    rows = step_ref.shape[0]
    steps = rows // (halves * CHUNKS)

    @pl.when(pl.program_id(0) == 0)
    def _():
        spread(b_wide, b_ref)
        spread(c_wide, c_ref)

    rates = [full(rate_ref[n : n + 1, :]) for n in range(STATE)]

    def half(h, carry):
        state = []
        for n in range(STATE):
            state.append(
                part_ref[h, n] + jnp.exp2(rates[n] * sum_ref[h]) * full(device[n : n + 1, :])
            )
            entry_ref[h, n] = state[n]

        def body(s, state):
            at = pl.ds(pl.multiple_of((h * steps + s) * CHUNKS, CHUNKS), CHUNKS)
            step = step_ref[at, :]
            decay_step = step + break_ref[at, :]
            drive = mixed_ref[at, :] * step
            total = None
            new = []
            for n in range(STATE):
                value = jnp.exp2(decay_step * rates[n]) * state[n] + drive * b_wide[n, at, :]
                term = value * c_wide[n, at, :]
                total = term if total is None else total + term
                new.append(value)
            scan_ref[at, :] = total
            return tuple(new)

        lax.fori_loop(0, steps, body, tuple(state), unroll=5)
        return carry

    lax.fori_loop(0, halves, half, 0)
    gate = gate_ref[...]
    out = scan_ref[...] + skip_ref[...] * mixed_ref[...]
    scan_ref[...] = out
    gated_ref[...] = (out * (gate * jax.nn.sigmoid(gate))).astype(gated_ref.dtype)


def early_fills(first, second, held, own_sem):
    rows, copies, place = held.shape[1], [], 0
    for part in (first, second):
        done = 0
        while done < part.shape[0]:
            c, low = (place + done) // rows, (place + done) % rows
            length = min(rows - low, part.shape[0] - done)
            copies.append(
                pltpu.make_async_copy(
                    part.at[pl.ds(done, length)], held.at[c, pl.ds(low, length)], own_sem.at[len(copies)]
                )
            )
            done += length
        place += part.shape[0]
    return copies


def grads_kernel(
    halves, count, groups, step_ref, mixed_ref, break_ref, grad_ref, b_ref, c_ref, rate_ref, entry_ref,
    part_ref, sum_ref, device, first_early, second_early, step_out, mixed_out, b_out, c_out, rate_out, early_out,
    b_wide, c_wide, b_sum, c_sum, decays, states, held, incoming, summed_early, send_sem, recv_sem, own_sem,
):
    rows = step_ref.shape[0]
    steps = rows // (halves * CHUNKS)
    group = pl.program_id(0)
    block = STATE // 2
    halving = Halving(count, held, incoming, summed_early, send_sem, recv_sem)
    slots = [[] for _ in range(2 * groups)]
    for turn in range(halving.turns):
        slots[turn * 2 * groups // halving.turns].append(turn)

    @pl.when(group == 0)
    def _():
        halving.greet()
        fills = early_fills(first_early, second_early, held, own_sem)
        for fill in fills:
            fill.start()
        spread(b_wide, b_ref)
        for fill in fills:
            fill.wait()
        halving.greeted()
        halving.start()
        spread(c_wide, c_ref)
        b_sum[...] = jnp.zeros_like(b_sum)
        c_sum[...] = jnp.zeros_like(c_sum)

    zero = jnp.zeros((CHUNKS, LANES), jnp.float32)

    for first in (0, block):
        rates = [full(rate_ref[first + n : first + n + 1, :]) for n in range(block)]

        def half(h, rate_sums):
            entry = []
            for n in range(block):
                entry.append(entry_ref[h, first + n])
                states[0, n] = entry[n]

            def ahead(s, state):
                at = pl.ds(pl.multiple_of((h * steps + s) * CHUNKS, CHUNKS), CHUNKS)
                step = step_ref[at, :]
                decay_step = step + break_ref[at, :]
                drive = mixed_ref[at, :] * step
                new = []
                for n in range(block):
                    decay = jnp.exp2(decay_step * rates[n])
                    value = decay * state[n] + drive * b_wide[first + n, at, :]
                    decays[s, n] = decay
                    states[s + 1, n] = value
                    new.append(value)
                return tuple(new)

            lax.fori_loop(0, steps, ahead, tuple(entry), unroll=10)

            exits = [
                part_ref[h, first + n]
                + jnp.exp2(rates[n] * sum_ref[h]) * full(device[first + n : first + n + 1, :])
                for n in range(block)
            ]

            def back(k, carry):
                s = steps - 1 - k
                at = pl.ds(pl.multiple_of((h * steps + s) * CHUNKS, CHUNKS), CHUNKS)
                step = step_ref[at, :]
                mixed = mixed_ref[at, :]
                grad = grad_ref[at, :]
                drive = mixed * step
                by_rate, by_map = zero, zero
                flows, sums = [], []
                for n in range(block):
                    b_now, c_now = b_wide[first + n, at, :], c_wide[first + n, at, :]
                    here = carry[n] + c_now * grad
                    flow = decays[s, n] * here
                    log_grad = flow * states[s, n]
                    by_rate = by_rate + rates[n] * log_grad
                    by_map = by_map + b_now * here
                    b_sum[first + n, at, :] += drive * here
                    c_sum[first + n, at, :] += grad * states[s + 1, n]
                    flows.append(flow)
                    sums.append(carry[block + n] + step * log_grad)
                by_rate = by_rate * LN2 + mixed * by_map
                by_map = step * by_map
                if first == 0:
                    step_out[at, :] = by_rate
                    mixed_out[at, :] = by_map
                else:
                    step_out[at, :] += by_rate
                    mixed_out[at, :] += by_map
                return tuple(flows + sums)

            out = lax.fori_loop(0, steps, back, tuple(exits) + rate_sums, unroll=5)
            return out[block:]

        rate_sums = lax.fori_loop(0, halves, half, (zero,) * block)
        for n in range(block):
            rate_out[first + n : first + n + 1, :] = jnp.sum(rate_sums[n], 0, keepdims=True)

        for g in range(groups):
            turns = slots[2 * g + first // block]
            if turns:

                @pl.when(group == g)
                def _(turns=turns):
                    for turn in turns:
                        halving.turn(turn)

    @pl.when(group == groups - 1)
    def _():
        result = pltpu.make_async_copy(summed_early, early_out, own_sem.at[0])
        result.start()
        result.wait()
        for n in range(STATE):
            b_out[:, n : n + 1] = jnp.sum(b_sum[n], -1, keepdims=True)
            c_out[:, n : n + 1] = jnp.sum(c_sum[n], -1, keepdims=True)


class Scan:
    def __init__(self, rows, channels, halves):
        self.rows, self.channels, self.halves = rows, channels, halves
        self.groups = channels // LANES
        row_spec = pl.BlockSpec((rows, LANES), lambda g: (0, g))
        fixed = lambda *shape: pl.BlockSpec(shape, lambda g: (0,) * len(shape))
        self.row_spec = row_spec
        self.break_spec = fixed(rows, LANES)
        self.map_spec = fixed(rows, STATE)
        self.rate_spec = pl.BlockSpec((STATE, LANES), lambda g: (0, g))
        self.part_spec = pl.BlockSpec((halves, STATE, CHUNKS, LANES), lambda g: (0, 0, 0, g))
        self.sum_spec = pl.BlockSpec((halves, CHUNKS, LANES), lambda g: (0, 0, g))
        self.tot_spec = pl.BlockSpec((STATE + CHUNKS, LANES), lambda g: (0, g))
        self.skip_spec = pl.BlockSpec((1, LANES), lambda g: (0, g))
        self.row_f32 = jax.ShapeDtypeStruct((rows, channels), jnp.float32)
        self.part_f32 = jax.ShapeDtypeStruct((halves, STATE, CHUNKS, channels), jnp.float32)
        self.sum_f32 = jax.ShapeDtypeStruct((halves, CHUNKS, channels), jnp.float32)
        self.tot_f32 = jax.ShapeDtypeStruct((STATE + CHUNKS, channels), jnp.float32)
        self.wide = pltpu.VMEM((STATE, rows, LANES), jnp.float32)

    def params(self):
        return pltpu.CompilerParams(
            dimension_semantics=("arbitrary",), vmem_limit_bytes=VMEM_LIMIT
        )

    def cost(self, per_element):
        count = self.rows * self.channels * STATE
        return pl.CostEstimate(
            flops=per_element * count, bytes_accessed=12 * self.rows * self.channels, transcendentals=count
        )

    def ends(self, step, drive, breaks, maps, rates, blocks=None):
        anywhere = [pl.BlockSpec(memory_space=pl.ANY)] * 2
        forward = blocks is not None
        places = expert_groups() + (lax.axis_size("chan"),)
        kernel = partial(ends_and_rows_kernel, self.halves, places) if forward else partial(ends_kernel, self.halves, True)
        params = self.params()
        if forward:
            params = pltpu.CompilerParams(
                dimension_semantics=("arbitrary",), vmem_limit_bytes=VMEM_LIMIT, collective_id=8,
                has_side_effects=True,
            )
        return pl.pallas_call(
            kernel,
            grid=(self.groups,),
            in_specs=[self.row_spec, self.row_spec, self.break_spec, self.map_spec, self.rate_spec]
            + anywhere * forward,
            out_specs=[self.part_spec, self.sum_spec, self.tot_spec] + anywhere * forward,
            out_shape=[self.part_f32, self.sum_f32, self.tot_f32]
            + ([jax.ShapeDtypeStruct(part.shape, part.dtype) for part in blocks] if forward else []),
            scratch_shapes=[self.wide] + (exchange_scratch(2) if forward else []),
            compiler_params=params,
            cost_estimate=self.cost(5),
            name="scan_ends" if forward else "scan_ends_back",
        )(step, drive, breaks, maps, rates, *(blocks if forward else []))

    def outputs(self, step, mixed, breaks, b_in, c_out, rates, part, sums, device, skip, gate):
        return pl.pallas_call(
            partial(outputs_kernel, self.halves),
            grid=(self.groups,),
            in_specs=[
                self.row_spec, self.row_spec, self.break_spec, self.map_spec, self.map_spec, self.rate_spec,
                self.part_spec, self.sum_spec, self.rate_spec, self.skip_spec, self.row_spec,
            ],
            out_specs=[self.row_spec, self.row_spec, self.part_spec],
            out_shape=[
                self.row_f32,
                jax.ShapeDtypeStruct((self.rows, self.channels), jnp.bfloat16),
                self.part_f32,
            ],
            scratch_shapes=[self.wide, self.wide],
            compiler_params=self.params(),
            cost_estimate=self.cost(7),
            name="scan_outputs",
        )(step, mixed, breaks, b_in, c_out, rates, part, sums, device, skip, gate)

    def grads(self, step, mixed, breaks, grad, b_in, c_out, rates, entry, part, sums, device, early):
        count = lax.axis_size("seq")
        width, total = early[0].shape[1], early[0].shape[0] + early[1].shape[0]
        chunk = 16 * count
        total = -(-total // chunk) * chunk
        early = (early[0], jnp.pad(early[1], ((0, total - early[0].shape[0] - early[1].shape[0]), (0, 0))))
        chunks = total // chunk
        anywhere = pl.BlockSpec(memory_space=pl.ANY)
        steps = self.rows // (self.halves * CHUNKS)
        block = STATE // 2
        return pl.pallas_call(
            partial(grads_kernel, self.halves, count, self.groups),
            grid=(self.groups,),
            in_specs=[
                self.row_spec, self.row_spec, self.break_spec, self.row_spec, self.map_spec, self.map_spec,
                self.rate_spec, self.part_spec, self.part_spec, self.sum_spec, self.rate_spec, anywhere, anywhere,
            ],
            out_specs=[self.row_spec, self.row_spec, self.map_spec, self.map_spec, self.rate_spec, anywhere],
            out_shape=[
                self.row_f32,
                self.row_f32,
                jax.ShapeDtypeStruct((self.rows, STATE), jnp.float32),
                jax.ShapeDtypeStruct((self.rows, STATE), jnp.float32),
                jax.ShapeDtypeStruct((STATE, self.channels), jnp.float32),
                jax.ShapeDtypeStruct((chunks, chunk, width), jnp.bfloat16),
            ],
            scratch_shapes=[
                self.wide, self.wide, self.wide, self.wide,
                pltpu.VMEM((steps, block, CHUNKS, LANES), jnp.float32),
                pltpu.VMEM((steps + 1, block, CHUNKS, LANES), jnp.float32),
                pltpu.VMEM((chunks, chunk, width), jnp.bfloat16),
                *sum_scratch(chunks, chunk, width, count)[1:2],
                pltpu.VMEM((chunks, chunk, width), jnp.bfloat16),
                *sum_scratch(chunks, chunk, width, count)[2:],
                pltpu.SemaphoreType.DMA((chunks + 2,)),
            ],
            compiler_params=pltpu.CompilerParams(
                dimension_semantics=("arbitrary",), vmem_limit_bytes=VMEM_LIMIT, collective_id=7,
                has_side_effects=True,
            ),
            cost_estimate=self.cost(20),
            name="scan_grads",
        )(step, mixed, breaks, grad, b_in, c_out, rates, entry, part, sums, device, *early)


def over_tokens(values):
    return jnp.sum(jnp.sum(values, 0), -1, keepdims=True)


def sinkhorn_kernel(place_ref, logit_ref, route_ref, gate_ref, scaled_ref, row_ref, column_ref, every_ref):
    probs = jnp.exp(logit_ref[...])
    for sweep in range(SINK):
        column = over_tokens(probs)
        scaled = probs / column[None]
        row = jnp.sum(scaled, 1, keepdims=True)
        scaled_ref[sweep] = scaled
        row_ref[sweep] = row
        column_ref[sweep] = jnp.broadcast_to(column, column_ref.shape[1:])
        probs = scaled / row
    ids = lax.broadcasted_iota(jnp.int32, probs.shape, 1)
    every_ref[...] = EXPERTS * jnp.sum(jnp.where(ids == place_ref[1], probs, 0.0), 1, keepdims=True)
    place = place_ref[0]
    own = scaled_ref[SINK - 1, place] / row_ref[SINK - 1, place]
    ids = lax.broadcasted_iota(jnp.int32, own.shape, 0)
    gate_ref[...] = EXPERTS * jnp.sum(jnp.where(ids == route_ref[...], own, 0.0), 0, keepdims=True)


def sinkhorn_back_kernel(place_ref, logit_ref, scaled_ref, row_ref, column_ref, grad_ref, out_ref, held):
    grad = grad_ref[...]
    for sweep in reversed(range(SINK)):
        scaled, row = scaled_ref[sweep], row_ref[sweep]
        inner = jnp.sum(grad * (scaled / row), 1, keepdims=True)
        grad = (grad - inner) / row
        along = over_tokens(grad * scaled)
        grad = (grad - along[None]) / column_ref[sweep][:, 0:1][None]
    held[...] = grad
    place = place_ref[0]
    out_ref[...] = held[place] * jnp.exp(logit_ref[place])


def in_vmem(count):
    return [pl.BlockSpec(memory_space=pltpu.SMEM)] + [pl.BlockSpec(memory_space=pltpu.VMEM)] * count


def sinkhorn(place, logits, routes):
    devices, experts, tokens = logits.shape
    f32 = lambda *shape: jax.ShapeDtypeStruct(shape, jnp.float32)
    return pl.pallas_call(
        sinkhorn_kernel,
        in_specs=in_vmem(2),
        out_specs=in_vmem(5)[1:],
        out_shape=[
            f32(1, tokens),
            f32(SINK, devices, experts, tokens),
            f32(SINK, devices, 1, tokens),
            f32(SINK, experts, LANES),
            f32(devices, 1, tokens),
        ],
        compiler_params=pltpu.CompilerParams(vmem_limit_bytes=VMEM_LIMIT),
        name="sinkhorn",
    )(place, logits, routes)


def sinkhorn_back(place, logits, scaled, rows, columns, grad):
    devices, experts, tokens = logits.shape
    return pl.pallas_call(
        sinkhorn_back_kernel,
        in_specs=in_vmem(5),
        out_specs=in_vmem(1)[1],
        out_shape=jax.ShapeDtypeStruct((experts, tokens), jnp.float32),
        scratch_shapes=[pltpu.VMEM(logits.shape, jnp.float32)],
        compiler_params=pltpu.CompilerParams(vmem_limit_bytes=VMEM_LIMIT),
        name="sinkhorn_back",
    )(place, logits, scaled, rows, columns, grad)


def expert_kernel(
    share, rows_ref, grad_ref, gate_ref, up_ref, down_ref, out_ref, back_ref, up_kept, up_sent, down_kept,
    down_sent, rows_t, grad_t, out_sum, back_sum, whole, half, held, sent, came, send_sem, recv_sem,
):
    step, last = pl.program_id(0), pl.num_programs(0) - 1
    features = up_ref.shape[2]
    me = lax.axis_index("seq")
    side, next_side = lax.rem(me, 2), lax.rem(lax.div(me, 2), 2)
    peer = {"seq": opposite(me, 1)}

    def copy(k):
        return pltpu.make_async_remote_copy(
            src_ref=sent.at[k], dst_ref=came.at[k], send_sem=send_sem.at[k], recv_sem=recv_sem.at[k],
            device_id=peer, device_id_type=MESH,
        )

    @pl.when(step == 0)
    def _():
        greet([peer])
        rows_t[...] = rows_ref[...].T
        grad_t[...] = (grad_ref[...].astype(jnp.float32) * gate_ref[...]).astype(jnp.bfloat16).T

    def halved_rows(total, which):
        whole[...] = total
        for k in range(half.shape[0] // features):
            low = whole[2 * k * features : (2 * k + 1) * features]
            high = whole[(2 * k + 1) * features : (2 * k + 2) * features]
            half[k * features : (k + 1) * features] = jnp.where(which == 0, low, high)
        return half[...].astype(jnp.bfloat16)

    def dot(a, b, over=((1,), (0,))):
        return lax.dot_general(a, b, (over, ((), ())), preferred_element_type=jnp.float32)

    def joined(ref):
        for q in range(ref.shape[0]):
            for j in range(ref.shape[1]):
                first = (j * ref.shape[0] + q) * features
                whole[first : first + features] = ref[q, j].astype(jnp.float32)
        return whole[...].astype(jnp.bfloat16)

    def send(k, total):
        held[k] = halved_rows(total, side)
        sent[k] = halved_rows(total, 1 - side)
        copy(k).start()

    @pl.when(step < last)
    def _():
        across = ((1,), (1,))
        up, down = joined(up_ref), joined(down_ref)
        pre = dot(rows_ref[...], up)
        square = pre * pre
        bend = jnp.tanh(GELU_SCALE * (pre + GELU_CUBE * pre * square))
        rise = 0.5 * (1.0 + bend)
        act = (pre * rise).astype(jnp.bfloat16)
        slope = rise + 0.5 * pre * (1.0 - bend * bend) * (GELU_SCALE + 3.0 * GELU_SCALE * GELU_CUBE * square)
        grad_pre = dot(grad_ref[...], down) * slope
        out_part, back_part = dot(act, down, across), dot(grad_pre.astype(jnp.bfloat16), up, across)

        @pl.when(step == 0)
        def _():
            out_sum[...] = out_part
            back_sum[...] = back_part

        @pl.when(step > 0)
        def _():
            out_sum[...] += out_part
            back_sum[...] += back_part

        send(2 * step, dot(grad_t[...], act))
        send(2 * step + 1, dot(rows_t[...], (grad_pre * gate_ref[...]).astype(jnp.bfloat16)))

    @pl.when(step > 0)
    def _():
        for odd, kept_ref, sent_ref in ((0, down_kept, down_sent), (1, up_kept, up_sent)):
            k = 2 * (step - 1) + odd
            copy(k).wait()
            total = held[k].astype(jnp.float32) + came[k].astype(jnp.float32)
            half[...] = total
            for g in range(half.shape[0] // (2 * features)):
                low = half[2 * g * features : (2 * g + 1) * features]
                high = half[(2 * g + 1) * features : (2 * g + 2) * features]
                kept_ref[g] = jnp.where(next_side == 0, low, high).astype(kept_ref.dtype)
                sent_ref[g] = jnp.where(next_side == 0, high, low).astype(sent_ref.dtype)

    @pl.when(step == last)
    def _():
        out_ref[...] = out_sum[...].astype(out_ref.dtype)
        back_ref[...] = back_sum[...].astype(back_ref.dtype)


def expert_passes(rows, grad, gate, up, down):
    count, width = rows.shape
    share, own, features, hidden = up.shape
    tile = 512
    tiles = hidden // tile
    blocks = width // (4 * features)
    fixed = lambda *shape: pl.BlockSpec(shape, lambda k: (0,) * len(shape))
    weight_spec = pl.BlockSpec(
        (share, own, features, tile), lambda k: (0, 0, 0, jnp.minimum(k, tiles - 1))
    )
    part_spec = pl.BlockSpec((blocks, features, tile), lambda k: (0, 0, jnp.maximum(k - 1, 0)))
    part_shape = jax.ShapeDtypeStruct((blocks, features, hidden), jnp.bfloat16)
    row_shape = jax.ShapeDtypeStruct((count, width), jnp.bfloat16)
    return pl.pallas_call(
        partial(expert_kernel, share),
        grid=(tiles + 1,),
        in_specs=[
            fixed(count, width), fixed(count, width), fixed(count, 1), weight_spec, weight_spec,
        ],
        out_specs=[fixed(count, width), fixed(count, width)] + [part_spec] * 4,
        out_shape=[row_shape, row_shape] + [part_shape] * 4,
        scratch_shapes=[
            pltpu.VMEM((width, count), jnp.bfloat16),
            pltpu.VMEM((width, count), jnp.bfloat16),
            pltpu.VMEM((count, width), jnp.float32),
            pltpu.VMEM((count, width), jnp.float32),
            pltpu.VMEM((width, tile), jnp.float32),
            pltpu.VMEM((width // 2, tile), jnp.float32),
            pltpu.VMEM((2 * tiles, width // 2, tile), jnp.bfloat16),
            pltpu.VMEM((2 * tiles, width // 2, tile), jnp.bfloat16),
            pltpu.VMEM((2 * tiles, width // 2, tile), jnp.bfloat16),
            pltpu.SemaphoreType.DMA((2 * tiles,)),
            pltpu.SemaphoreType.DMA((2 * tiles,)),
        ],
        compiler_params=pltpu.CompilerParams(
            dimension_semantics=("arbitrary",), vmem_limit_bytes=VMEM_LIMIT, collective_id=9,
            has_side_effects=True,
        ),
        cost_estimate=pl.CostEstimate(
            flops=12 * count * width * hidden, bytes_accessed=8 * width * hidden, transcendentals=count * hidden
        ),
        name="expert_passes",
    )(rows, grad, gate, up, down)


def on_device(
    block_in,
    routes,
    doc_lengths,
    norm_gain,
    in_weight,
    conv_weight,
    conv_bias,
    xproj_weight,
    dt_weight,
    dt_bias,
    a_log,
    skip_gain,
    out_weight,
    moe_gain,
    router_weight,
    up_weight,
    down_weight,
    out_grad,
):
    tok_dev, model_width = block_in.shape
    chan_count = lax.axis_size("chan")
    chan_place, seq_place = lax.axis_index("chan"), lax.axis_index("seq")
    own, share = expert_groups()
    held_expert = chan_place * own + seq_place // share
    dev_ref = jnp.stack([seq_place * chan_count + chan_place, held_expert]).astype(jnp.int32)
    steps = tok_dev // CHUNKS
    tok_seq = tok_dev * chan_count
    channels = in_weight.shape[2]
    padded_channels = -(-channels // LANES) * LANES
    f32, bf16 = jnp.float32, jnp.bfloat16

    route_col = routes[:, 0]
    expert_ids = lax.broadcasted_iota(jnp.int32, (1, EXPERTS), 1)
    chosen = (route_col[:, None] == expert_ids).astype(bf16)
    row_ids = lax.broadcasted_iota(jnp.int32, (tok_dev, tok_dev), 0)
    col_ids = lax.broadcasted_iota(jnp.int32, (tok_dev, tok_dev), 1)
    counts = jnp.dot((col_ids <= row_ids).astype(bf16), chosen, preferred_element_type=f32)
    rank = (jnp.sum(counts * chosen.astype(f32), 1) - 1.0).astype(jnp.int32)
    capacity = tok_dev * 5 // (4 * EXPERTS) + 1
    capacity = -(-capacity // 16) * 16
    slot = to_steps(route_col * capacity + rank)
    route_steps = to_steps(route_col)
    slot_ids = lax.broadcasted_iota(jnp.int32, (1, EXPERTS * capacity), 1)
    placer = (slot[:, None] == slot_ids).astype(bf16)

    def pack(values):
        rows = jnp.einsum("ts,td->sd", placer, values, preferred_element_type=f32).astype(bf16)
        return rows.reshape(EXPERTS, capacity, model_width)

    def unpack(values):
        return jnp.einsum(
            "ts,sd->td",
            placer,
            values.reshape(EXPERTS * capacity, model_width),
            preferred_element_type=f32,
        )

    block_steps = to_steps(block_in)
    grad_steps = to_steps(out_grad)
    residual = block_steps.astype(f32)
    normed, norm_back = jax.vjp(norm_apply, residual, norm_gain)
    gathered = chan_rows(normed.astype(bf16))

    inner_b = jnp.dot(gathered, in_weight[0], preferred_element_type=f32).astype(bf16)
    gate_z = jnp.dot(gathered, in_weight[1], preferred_element_type=f32)

    shape4 = (chan_count, steps, CHUNKS)
    ids = [lax.broadcasted_iota(jnp.int32, shape4, axis) for axis in range(3)]
    position = seq_place * tok_seq + ids[0] * tok_dev + ids[2] * steps + ids[1]
    starts = jnp.cumsum(doc_lengths) - doc_lengths
    doc_first = jnp.max(
        jnp.where(starts <= position[..., None], starts, 0), axis=-1
    )
    reach = CONV - 1
    inner = inner_b.astype(f32).reshape(shape4 + (channels,))
    tails = jnp.swapaxes(inner[:, steps - reach :], 0, 1).reshape(reach, chan_count * CHUNKS, channels)
    previous = passed_along(tails[:, -1], "seq", 1)
    heads = jnp.concatenate([previous[:, None], tails[:, :-1]], 1)
    heads = jnp.swapaxes(heads.reshape(reach, chan_count, CHUNKS, channels), 0, 1)
    padded = jnp.concatenate([heads, inner], 1)
    masks = [
        (position - (reach - offset) >= doc_first).astype(f32)[..., None] for offset in range(CONV)
    ]
    conv_pre = conv_bias
    for offset in range(CONV):
        conv_pre = conv_pre + conv_weight[offset] * padded[:, offset : offset + steps] * masks[offset]
    conv_pre = conv_pre.reshape(tok_seq, channels)
    mixed_b = jax.nn.silu(conv_pre).astype(bf16)
    mixed = mixed_b.astype(f32)
    proj_all = proj_total(jnp.dot(mixed_b, xproj_weight, preferred_element_type=f32))
    low_rank = proj_all[:, :DT_RANK]
    b_in = proj_all[:, DT_RANK : DT_RANK + STATE]
    c_out = proj_all[:, DT_RANK + STATE :]
    step_pre = jnp.dot(low_rank, dt_weight, precision=HIGH) + dt_bias
    step_size = jax.nn.softplus(step_pre)

    def widened(values, axis=-1):
        more = padded_channels - channels
        if not more:
            return values
        pads = [(0, 0)] * values.ndim
        pads[axis] = (0, more)
        return jnp.pad(values, pads)

    scan = Scan(tok_seq, padded_channels, chan_count)
    decay_rates = jnp.exp(a_log)
    rates = widened((-LOG2E * decay_rates).T)
    breaks = jnp.any(position[..., None] == starts, axis=-1).astype(f32) * BREAK
    breaks = jnp.broadcast_to(breaks.reshape(tok_seq, 1), (tok_seq, LANES))
    step_w, mixed_w = widened(step_size), widened(mixed)
    token_slots = jnp.einsum(
        "ts,t->s", placer.astype(f32), 1.0 + lax.broadcasted_iota(f32, (tok_dev,), 0), precision=HIGH
    )
    token_slots = jnp.pad(token_slots.reshape(EXPERTS, 1, capacity), ((0, 0), (0, 7), (0, LANES - capacity)))
    part, sums, total, grad_arrived, token_arrived = scan.ends(
        step_w, mixed_w, breaks, b_in, rates, (pack(grad_steps), token_slots)
    )
    grad_arrived = grad_arrived.reshape(-1, model_width)
    device_entry = carried(total, rates, False)
    full_up = whole_expert(up_weight, None, device_entry)
    scan_out, gated_b, entry = scan.outputs(
        step_w, mixed_w, breaks, b_in, c_out, rates, part, sums, device_entry,
        widened(skip_gain[None]), widened(gate_z),
    )
    scan_out, gated_b = scan_out[:, :channels], gated_b[:, :channels]
    full_down = whole_expert(down_weight, device_entry, gated_b)

    mixer_rows = chan_sums(
        lambda rows: jnp.dot(rows, out_weight, preferred_element_type=f32), gated_b
    )
    hidden_one = residual + mixer_rows
    moe_in, moe_back = jax.vjp(norm_apply, hidden_one, moe_gain)
    logits = jnp.einsum("td,de->et", moe_in, router_weight, precision=HIGH)
    arrived, every_logit = rows_and_gather(pack(moe_in.astype(bf16)), logits)
    gate_row, scaled, row_totals, columns, every_gate = sinkhorn(
        dev_ref, every_logit, route_steps.reshape(1, tok_dev)
    )
    gate = gate_row.reshape(tok_dev)

    arrived = arrived.reshape(-1, model_width)
    senders = lax.dynamic_index_in_dim(
        every_gate.reshape(own, share, chan_count, tok_dev), seq_place % share, 1, False
    )
    senders = jnp.swapaxes(senders, 0, 1).reshape(EXPERTS, 1, tok_dev)
    token_ids = 1.0 + lax.broadcasted_iota(f32, (1, 1, tok_dev), 2)
    gate_arrived = jnp.sum(
        jnp.where(token_arrived[:, 0, :capacity, None] == token_ids, senders, 0.0), -1
    ).reshape(-1, 1)
    features, hidden = up_weight.shape[1:]
    expert_out, grad_rows_in, up_kept, up_sent, down_kept, down_sent = expert_passes(
        arrived, grad_arrived, gate_arrived, full_up, full_down
    )
    blocks = (EXPERTS, capacity, model_width)
    expert_back, grad_back = expert_rows(2, expert_out.reshape(blocks), grad_rows_in.reshape(blocks))
    expert_grads = [
        added(kept, swapped(sent, "seq", 2)).reshape(own, share // 4, features, hidden)
        for kept, sent in ((up_kept, up_sent), (down_kept, down_sent))
    ]
    for stage in range(2, share.bit_length() - 1):
        expert_grads = [halved(part, stage) for part in expert_grads]
    expert_tok = unpack(expert_back)
    plain_grad_part = unpack(grad_back)
    up_part, down_part = expert_grads

    block_out = from_steps((hidden_one + gate[:, None] * expert_tok).astype(bf16))
    grad_two = grad_steps.astype(f32)
    grad_gate = jnp.sum(expert_tok * grad_two, 1)
    grad_probs = jnp.where(
        route_steps[None] == lax.broadcasted_iota(jnp.int32, (EXPERTS, 1), 0),
        EXPERTS * grad_gate[None],
        0.0,
    )
    every_grad, up_part = gathered_everywhere(10, grad_probs, up_part)
    up_grad = to_owners(up_part.reshape(own, *up_part.shape[2:]))
    grad_logits = sinkhorn_back(dev_ref, every_logit, scaled, row_totals, columns, every_grad)
    router_grad = jnp.einsum("td,et->ed", moe_in, grad_logits, precision=HIGH)
    grad_moe_in = gate[:, None] * plain_grad_part + jnp.einsum(
        "et,de->td", grad_logits, router_weight, precision=HIGH
    )
    grad_hidden, moe_gain_grad = moe_back(grad_moe_in)
    grad_hidden = grad_hidden + grad_two

    grad_mix = chan_rows(grad_hidden.astype(bf16))
    grad_gated = jnp.einsum("td,ed->te", grad_mix, out_weight, preferred_element_type=f32)
    out_weight_grad = jnp.einsum("te,td->ed", gated_b, grad_mix, preferred_element_type=f32)
    grad_scan = grad_gated * jax.nn.silu(gate_z)
    grad_gate_z = (grad_gated * scan_out * silu_grad(gate_z)).astype(bf16)
    skip_grad = jnp.sum(grad_scan * mixed, 0)
    gate_weight_grad = jnp.einsum("td,te->de", gathered, grad_gate_z, preferred_element_type=f32)
    gains = jnp.concatenate([moe_gain_grad[None], router_grad], 0)
    gains = lax.psum(gains, "chan") if chan_count != 2 else gains + swapped(gains, "chan", 1)
    grad_scan_w = widened(grad_scan)
    back_part, back_sums, back_total = scan.ends(step_w, grad_scan_w, breaks, c_out, rates)
    back_entry = carried(back_total, rates, True, up_grad, down_part)
    step_grad, mixed_grad, b_grad, c_grad, rate_grad, early = scan.grads(
        step_w, mixed_w, breaks, grad_scan_w, b_in, c_out, rates, entry, back_part, back_sums,
        back_entry, (out_weight_grad.astype(bf16).reshape(-1, channels), gate_weight_grad.astype(bf16)),
    )
    early = early.reshape(-1, channels)
    down_grad = to_owners(after(down_part.reshape(own, *down_part.shape[2:]), step_grad))
    step_grad, mixed_grad = step_grad[:, :channels], mixed_grad[:, :channels]
    mixed_grad = mixed_grad + skip_gain * grad_scan
    a_log_rows = -decay_rates.T * rate_grad[:, :channels]
    step_pre_grad = step_grad * jax.nn.sigmoid(step_pre)
    dt_bias_grad = jnp.sum(step_pre_grad, 0)
    dt_weight_grad = jnp.einsum("tr,te->re", low_rank, step_pre_grad, precision=HIGH)
    rank_grad = jnp.einsum("te,re->tr", step_pre_grad, dt_weight, precision=HIGH)
    proj_grad_b = proj_total(jnp.concatenate([rank_grad, b_grad, c_grad], 1)).astype(bf16)
    mixed_grad = mixed_grad + jnp.einsum(
        "tp,ep->te", proj_grad_b, xproj_weight, preferred_element_type=f32
    )
    xproj_rows = jnp.einsum("te,tp->pe", mixed_b, proj_grad_b, preferred_element_type=f32)
    conv_grad = (mixed_grad * silu_grad(conv_pre)).reshape(shape4 + (channels,))
    conv_bias_grad = jnp.sum(conv_grad, (0, 1, 2))
    conv_weight_grad = jnp.stack(
        [
            jnp.sum(conv_grad * masks[offset] * padded[:, offset : offset + steps], (0, 1, 2))
            for offset in range(CONV)
        ]
    )
    padded_grad = 0.0
    for offset in range(CONV):
        padded_grad = padded_grad + jnp.pad(
            conv_weight[offset] * conv_grad * masks[offset],
            ((0, 0), (offset, reach - offset), (0, 0), (0, 0)),
        )
    head_grad = jnp.swapaxes(padded_grad[:, :reach], 0, 1).reshape(
        reach, chan_count * CHUNKS, channels
    )
    from_next = passed_along(head_grad[:, 0], "seq", -1)
    tail_grad = jnp.concatenate([head_grad[:, 1:], from_next[:, None]], 1)
    tail_grad = jnp.swapaxes(tail_grad.reshape(reach, chan_count, CHUNKS, channels), 0, 1)
    inner_grad = padded_grad[:, reach:] + jnp.pad(
        tail_grad, ((0, 0), (steps - reach, 0), (0, 0), (0, 0))
    )
    inner_grad_b = inner_grad.reshape(tok_seq, channels).astype(bf16)
    inner_weight_grad = jnp.einsum("td,te->de", gathered, inner_grad_b, preferred_element_type=f32)
    both_grad = jnp.concatenate([inner_grad_b, grad_gate_z], 1)
    normed_grad = chan_sums(
        lambda rows: jnp.dot(rows[:, :channels], in_weight[0].T, preferred_element_type=f32)
        + jnp.dot(rows[:, channels:], in_weight[1].T, preferred_element_type=f32),
        both_grad,
    )
    residual_grad, norm_gain_grad = norm_back(normed_grad)
    in_grad = from_steps(residual_grad + grad_hidden)

    norm_rows = norm_gain_grad[None]
    norm_rows = lax.psum(norm_rows, "chan") if chan_count != 2 else norm_rows + swapped(norm_rows, "chan", 1)
    pieces = (
        xproj_rows, dt_weight_grad, a_log_rows, conv_weight_grad, conv_bias_grad[None], dt_bias_grad[None],
        skip_grad[None], norm_rows.reshape(-1, channels), gains.reshape(-1, channels),
    )
    bounds = [sum(part.shape[0] for part in pieces[: k + 1]) for k in range(len(pieces) - 1)]
    inner_weight_grad, small = summed([after(inner_weight_grad.astype(bf16), down_grad), jnp.concatenate(pieces, 0)])
    out_weight_grad = early[:model_width].reshape(channels, model_width).astype(f32)
    gate_weight_grad = early[model_width : 2 * model_width]
    (
        xproj_rows, dt_weight_grad, a_log_rows, conv_weight_grad, conv_bias_grad, dt_bias_grad, skip_grad,
        norm_rows, gains,
    ) = jnp.split(small, bounds, 0)
    norm_gain_grad, gains = norm_rows.reshape(-1), gains.reshape(-1, model_width)
    xproj_grad, a_log_grad = xproj_rows.T, a_log_rows.T
    conv_bias_grad, dt_bias_grad, skip_grad = conv_bias_grad[0], dt_bias_grad[0], skip_grad[0]
    moe_gain_grad, router_grad = gains[0], gains[1:].T
    in_weight_grad = jnp.stack([inner_weight_grad.astype(bf16), gate_weight_grad]).astype(f32)
    return (
        block_out,
        in_grad,
        norm_gain_grad,
        in_weight_grad,
        conv_weight_grad,
        conv_bias_grad,
        xproj_grad,
        dt_weight_grad,
        dt_bias_grad,
        a_log_grad,
        skip_grad,
        out_weight_grad,
        moe_gain_grad,
        router_grad,
        up_grad.astype(f32),
        down_grad.astype(f32),
    )


def solution(mesh):
    in_specs = (
        P(("seq", "chan"), None),
        P(("seq", "chan"), None),
        P(),
        P(),
        P(None, None, "chan"),
        P(None, "chan"),
        P("chan"),
        P("chan", None),
        P(None, "chan"),
        P("chan"),
        P("chan", None),
        P("chan"),
        P("chan", None),
        P(),
        P(),
        P("chan", "seq", None),
        P("chan", "seq", None),
        P(("seq", "chan"), None),
    )
    out_specs = (
        P(("seq", "chan"), None),
        P(("seq", "chan"), None),
        P(),
        P(None, None, "chan"),
        P(None, "chan"),
        P("chan"),
        P("chan", None),
        P(None, "chan"),
        P("chan"),
        P("chan", None),
        P("chan"),
        P("chan", None),
        P(),
        P(),
        P("chan", "seq", None),
        P("chan", "seq", None),
    )
    return jax.shard_map(
        on_device, mesh=mesh, in_specs=in_specs, out_specs=out_specs, check_vma=False
    )
```
